128 devices in a mesh: batch: 4 (over y), centers: 32 (over x, z, core).
Axes of the slice: x: 4, y: 4, z: 4, core: 2. Of those that a mesh axis runs over, the one named last changes fastest.
Arguments:
- centers: bfloat16 [262144, 512], P('centers'), may hold values from -2 to 2, as said below
- coeffs: float32 [262144, 128], P('centers'), may hold values from -0.046875 to 0.046875
- targets: bfloat16 [262144, 128], P('centers'), may hold values from -6 to 6
- batch_index: int32 [4096], P('batch'), may hold values from 0 to 262143
- subset_index: int32 [65536], P('centers'), may hold values from 0 to 262143, as said below
- eigvec: float32 [160, 65536], P(None, 'centers'), may hold values from -0.0234375 to 0.0234375
- eigen_scale: float32 [160], replicated, may hold values from 0.1 to 1
Outputs:
- updated: float32 [262144, 128], P('centers')
- residual: float32 [4096, 128], P('batch')
The draws below stay inside these ranges and needn't reach their ends.
Inputs may be any that keep to these rules, and one draw needn't show every extreme that they name: `centers`: centers are embedding vectors of varied lengths. `subset_index`: the 2048 entries of block j (entries j * 2048 to (j + 1) * 2048 - 1) are distinct and lie in [j * 8192, (j + 1) * 8192).
All inputs are finite; a program needn't handle non-finite values.
Results may differ from the reference program's by a relative error of at most 0.0031.
Values may be sent and summed in bfloat16 or wider, within the bound.
No kernel may reach another device: no remote copies, remote signals or barrier semaphores. Data moves between devices by JAX's collectives and lax.ppermute only.
A program may use at most 128 MiB of HBM per device.

```python
import math
import jax
import jax.numpy as jnp
import numpy as np
from jax import lax

D = 512
C = 128
Q = 160
CEN_DEV = 8192
S_DEV = 2048
M = 262144
B = 4096
S = 65536
N_CENTERS = 32


def draw_centers(key, part):
    key = jax.random.fold_in(key, 3)
    first_key, second_key = jax.random.split(key)
    values = jnp.clip(jax.random.normal(first_key, (M, D), jnp.float32), -4.0, 4.0)
    scales = jnp.exp(jax.random.uniform(second_key, (M, 1), jnp.float32, math.log(0.3), math.log(3.0)))
    return (values * scales / math.sqrt(D)).astype(jnp.bfloat16)


def draw_subset_index(key, part):
    key = jax.random.fold_in(key, 7)
    stride = CEN_DEV // S_DEV
    jitter = jax.random.randint(key, (N_CENTERS, S_DEV), 0, stride).astype(jnp.int32)
    jitter = jitter.at[:, 0].set(0).at[:, S_DEV - 1].set(stride - 1)
    block_base = jnp.arange(N_CENTERS, dtype=jnp.int32)[:, None] * CEN_DEV
    slot_base = jnp.arange(S_DEV, dtype=jnp.int32)[None, :] * stride
    return (block_base + slot_base + jitter).reshape(-1).astype(jnp.int32)


def touch_ends(values, key, smallest, top_value):
    longest = values.shape.index(max(values.shape))
    spots = []
    for shift in (0, 1):
        where = [jax.random.randint(jax.random.fold_in(key, axis), (), 0, length) for axis, length in enumerate(values.shape)]
        where[longest] = (where[longest] + shift) % values.shape[longest]
        spots.append(tuple(where))
    return values.at[spots[0]].set(smallest).at[spots[1]].set(top_value)


def block_levels(rng, extent, cuts, least, high):
    factor_of, own = 1.0, jax.random.fold_in(rng, 6)
    for dim, shards_of in cuts:
        steps = jnp.exp(jax.random.uniform(jax.random.fold_in(own, dim), (shards_of,), jnp.float32, least / len(cuts), high / len(cuts)))
        factor_of = factor_of * jnp.repeat(steps, extent[dim] // shards_of).reshape([-1 if axis == dim else 1 for axis in range(len(extent))])
    return factor_of


def skewed_wide(key, extent, amount, slope):
    loads = [min(1 << octave, amount + 1 - (1 << octave)) * (1 << 20) // math.isqrt((1 << octave) ** slope) + 1 for octave in range((amount + 1).bit_length()) if 1 << octave <= amount]
    scale = 1 + sum(loads) // (1 << 30)
    table = np.cumsum(np.array([max(1, weight // scale) for weight in loads]))
    ticket = jax.random.randint(jax.random.fold_in(key, 1), extent, 0, int(table[len(loads) - 1]))
    start = jnp.left_shift(1, jnp.searchsorted(jnp.asarray(table, jnp.int32), ticket, side="right").astype(jnp.int32))
    standing = start - 1 + jax.random.randint(jax.random.fold_in(key, 4), extent, 0, 1 << 30) % jnp.minimum(start, amount + 1 - start)
    return jax.random.permutation(jax.random.fold_in(key, 2), amount)[standing].astype(jnp.int32)


def bell_draw(own_key, extent, deviation, bound, cuts=(), kind=jnp.bfloat16):
    drawn = deviation * jax.random.normal(own_key, extent, jnp.float32)
    if cuts:
        drawn = drawn * block_levels(own_key, extent, cuts, -0.22, 0.18)
    return jnp.clip(drawn, -bound, bound).astype(kind)


def setup_inputs(seed: int = 0) -> dict:
    splits = jax.random.split(jax.random.key(seed), 8)
    centers = draw_centers(jax.random.fold_in(splits[7], 71), 0)
    coeffs = bell_draw(splits[1], (M, C), (M // 16) ** -0.5, 0.046875, ((0, 32),), jnp.float32)
    targets = bell_draw(splits[2], (M, C), 1.0, 6.0, ((0, 32),))
    batch_index = touch_ends(skewed_wide(splits[3], (B,), M, 2), jax.random.fold_in(splits[3], 3), 0, M - 1).astype(jnp.int32)
    subset_index = draw_subset_index(jax.random.fold_in(splits[7], 71), 0)
    eigvec = bell_draw(splits[5], (Q, S), S ** -0.5, 0.0234375, ((1, 32),), jnp.float32)
    eigen_scale = jnp.clip(jnp.exp(jax.random.uniform(splits[6], (Q,), jnp.float32, math.log(0.1), math.log(1.0))), 0.1, 1.0)
    return dict(centers=centers, coeffs=coeffs, targets=targets, batch_index=batch_index, subset_index=subset_index, eigvec=eigvec, eigen_scale=eigen_scale)


spread = 1.0
step_size = 0.5

def laplace_kernel(first_rows, second_rows):
    first_norms = lax.optimization_barrier(jnp.sum(jnp.square(first_rows.astype(jnp.float32)), axis=1))
    second_norms = lax.optimization_barrier(jnp.sum(jnp.square(second_rows.astype(jnp.float32)), axis=1))
    products = lax.dot_general(first_rows, second_rows, (((1,), (1,)), ((), ())), preferred_element_type=jnp.float32)
    distance = first_norms[:, None] + second_norms[None, :] - 2.0 * products
    return jnp.exp(-jnp.sqrt(jnp.maximum(distance, 0.0) + 0.001) / spread).astype(jnp.bfloat16)

def reference(centers, coeffs, targets, batch_index, subset_index, eigvec, eigen_scale):
    batch_rows = centers[batch_index]
    batch_targets = targets[batch_index].astype(jnp.float32)
    center_blocks = centers.reshape(N_CENTERS, CEN_DEV, D)
    coeff_blocks = coeffs.reshape(N_CENTERS, CEN_DEV, C)

    def add_block(running, block_pair):
        kernel_rows = laplace_kernel(batch_rows, block_pair[0])
        term = jnp.dot(kernel_rows, block_pair[1].astype(jnp.bfloat16), preferred_element_type=jnp.float32)
        return (running + term, jnp.zeros((), jnp.float32))
    scanned = lax.scan(add_block, jnp.zeros((B, C), jnp.float32), (center_blocks, coeff_blocks))
    prediction = scanned[0]
    residual = prediction - batch_targets
    stepped = coeffs.at[batch_index].add(-step_size * residual)
    subset_rows = centers[subset_index].reshape(N_CENTERS, S_DEV, D)
    residual_half = residual.astype(jnp.bfloat16)

    def subset_block(running, block_rows):
        kernel_rows = laplace_kernel(block_rows, batch_rows)
        return (running, jnp.dot(kernel_rows, residual_half, preferred_element_type=jnp.float32))
    sums = lax.scan(subset_block, jnp.zeros((), jnp.float32), subset_rows)
    subset_sum = sums[1].reshape(S, C)
    projected = jnp.dot(eigvec, subset_sum, precision=lax.Precision.HIGHEST)
    weighted = eigen_scale[:, None] * projected
    correction = lax.dot_general(eigvec, weighted, (((0,), (0,)), ((), ())), precision=lax.Precision.HIGHEST)
    updated = stepped.at[subset_index].add(step_size * correction)
    return (updated, residual)
```

```python
import functools

import jax
import jax.numpy as jnp
from jax import lax
from jax.experimental import pallas as pl
from jax.experimental.pallas import tpu as pltpu
from jax.sharding import PartitionSpec as P

spread = 1.0
step_size = 0.5
NT = (((1,), (1,)), ((), ()))
TN = (((0,), (0,)), ((), ()))
bf16 = jnp.bfloat16
f32 = jnp.float32
i32 = jnp.int32
VMEM_LIMIT = 56 * 2**20
LOG2_E = 1.4426950408889634
SLOTS = 32


def split_two(values):
    high = values.astype(bf16)
    return high, (values - high.astype(f32)).astype(bf16)


def split_rounded(values):
    high = lax.reduce_precision(values, 8, 7)
    return high.astype(bf16), (values - high).astype(bf16)


def next_hits(index, offset, count):
    rows = index.shape[0]
    total = rows * 128
    lane = lax.broadcasted_iota(i32, (rows, 128), 1)
    sub = lax.broadcasted_iota(i32, (rows, 128), 0)
    local = index - offset
    found = jnp.where((local >= 0) & (local < count), sub * 128 + lane, total)
    shift = 1
    while shift < 128:
        moved = pltpu.roll(found, 128 - shift, 1)
        found = jnp.minimum(found, jnp.where(lane < 128 - shift, moved, total))
        shift *= 2
    later = jnp.broadcast_to(found[:, 0:1], (rows, 128))
    later = jnp.where(sub < rows - 1, pltpu.roll(later, rows - 1, 0), total)
    shift = 1
    while shift < rows:
        moved = pltpu.roll(later, rows - shift, 0)
        later = jnp.minimum(later, jnp.where(sub < rows - shift, moved, total))
        shift *= 2
    return jnp.minimum(found, later)


def following(nxt, pos, total):
    after = jnp.minimum(pos + 1, total - 1)
    return jnp.where(pos + 1 < total, nxt[after // 128, after % 128], total)


def pick_kernel(
    place, index_s, index_v, centers, targets, mine, other, labels,
    nxt_v, nxt, tiles, label_tiles, wide, label_wide, rows, sems, nxt_sem,
):
    total = rows.shape[0]
    half = total // 2
    offset, core = place[0], place[1]
    nxt_v[...] = next_hits(index_v[...], offset, centers.shape[0])
    copy = pltpu.make_async_copy(nxt_v, nxt, nxt_sem)
    copy.start()
    rows[...] = jnp.zeros_like(rows)
    labels[...] = jnp.zeros_like(labels)
    copy.wait()

    def copies(pos, slot):
        local = index_s[pos] - offset
        base = pl.multiple_of((local // 16) * 16, 16)
        return (
            pltpu.make_async_copy(centers.at[pl.ds(base, 16), :], tiles.at[slot], sems.at[0, slot]),
            pltpu.make_async_copy(targets.at[pl.ds(base, 16), :], label_tiles.at[slot], sems.at[1, slot]),
        )

    def issue(state):
        slot, pos = state
        for one in copies(pos, slot):
            one.start()
        return slot + 1, following(nxt, pos, total)

    def drain(slot, pos):
        for one in copies(pos, slot):
            one.wait()
        line = (index_s[pos] - offset) % 16
        wide[...] = tiles[slot].astype(f32)
        label_wide[...] = label_tiles[slot].astype(f32)
        spot = jnp.where(core == 0, pos, pos ^ half)
        rows[pl.ds(spot, 1), :] = wide[pl.ds(line, 1), :]
        labels[pl.ds(spot, 1), :] = label_wide[pl.ds(line, 1), :]
        return following(nxt, pos, total)

    def batch(pos):
        used, _ = lax.while_loop(
            lambda s: (s[0] < SLOTS) & (s[1] < total), issue, (jnp.int32(0), pos)
        )
        return lax.fori_loop(0, used, drain, pos)

    lax.while_loop(lambda pos: pos < total, batch, nxt[0, 0])
    mine[...] = rows[0:half, :].astype(bf16)
    other[...] = rows[half:total, :].astype(bf16)


def pick(place, index, centers, targets):
    total, width, labels = index.shape[0], centers.shape[1], targets.shape[1]
    vmem = pl.BlockSpec(memory_space=pltpu.VMEM)
    smem = pl.BlockSpec(memory_space=pltpu.SMEM)
    hbm = pl.BlockSpec(memory_space=pl.ANY)
    return pl.pallas_call(
        pick_kernel,
        name="pick",
        in_specs=[smem, smem, vmem, hbm, hbm],
        out_specs=[vmem, vmem, vmem],
        out_shape=[
            jax.ShapeDtypeStruct((total // 2, width), bf16),
            jax.ShapeDtypeStruct((total // 2, width), bf16),
            jax.ShapeDtypeStruct((total, labels), f32),
        ],
        scratch_shapes=[
            pltpu.VMEM((total // 128, 128), i32),
            pltpu.SMEM((total // 128, 128), i32),
            pltpu.VMEM((SLOTS, 16, width), bf16),
            pltpu.VMEM((SLOTS, 16, labels), bf16),
            pltpu.VMEM((16, width), f32),
            pltpu.VMEM((16, labels), f32),
            pltpu.VMEM((total, width), f32),
            pltpu.SemaphoreType.DMA((2, SLOTS)),
            pltpu.SemaphoreType.DMA,
        ],
        compiler_params=pltpu.CompilerParams(vmem_limit_bytes=VMEM_LIMIT),
        cost_estimate=pl.CostEstimate(flops=0, bytes_accessed=4 * 2**20, transcendentals=0),
    )(place, index, index.reshape(total // 128, 128), centers, targets)


def prepare_kernel(subset, eigvec, coeffs, vt, low, turned, spreaded):
    vectors, count = eigvec.shape
    channels = coeffs.shape[1]
    spreaded[...] = jnp.zeros_like(spreaded)
    block = 512
    for start in range(0, count, block):
        turned[start : start + block, 0:vectors] = eigvec[:, start : start + block].T

    def put(group, _):
        for step in range(8):
            k = group * 8 + step
            spreaded[pl.ds(subset[k], 1), 0:vectors] = turned[pl.ds(k, 1), 0:vectors]
        return 0

    lax.fori_loop(0, count // 8, put, 0)
    for start in range(0, spreaded.shape[0], block):
        span = slice(start, start + block)
        high, rest = split_two(spreaded[span, 0:vectors].T)
        vt[0:channels, span] = coeffs[span, :].T.astype(bf16)
        vt[channels:, span] = high
        low[:, span] = rest


def prepare(subset, eigvec, coeffs):
    vectors, count = eigvec.shape
    centers, channels = coeffs.shape
    vmem = pl.BlockSpec(memory_space=pltpu.VMEM)
    smem = pl.BlockSpec(memory_space=pltpu.SMEM)
    lanes = -(-vectors // 128) * 128
    return pl.pallas_call(
        prepare_kernel,
        name="prepare",
        in_specs=[smem, vmem, vmem],
        out_specs=[vmem, vmem],
        out_shape=[
            jax.ShapeDtypeStruct((channels + vectors, centers), bf16),
            jax.ShapeDtypeStruct((vectors, centers), bf16),
        ],
        scratch_shapes=[pltpu.VMEM((count, lanes), f32), pltpu.VMEM((centers, lanes), f32)],
        compiler_params=pltpu.CompilerParams(vmem_limit_bytes=VMEM_LIMIT),
        cost_estimate=pl.CostEstimate(flops=0, bytes_accessed=30 * 2**20, transcendentals=0),
    )(subset, eigvec, coeffs)


def main_kernel(
    centers, vt, rows_mine, rows_other, labels, mine, other, turned, norms, total, *, part
):
    step = pl.program_id(0)
    half = rows_mine.shape[0]
    channels = labels.shape[1]
    vectors = vt.shape[0] - channels

    @pl.when(step == 0)
    def _():
        ones = jnp.ones((8, rows_mine.shape[1]), bf16)
        for start, rows in ((0, rows_mine), (half, rows_other)):
            span = slice(start, start + half)
            values = rows[...]
            high, low = split_two(jnp.square(values.astype(f32)))
            norms[:, span] = (
                lax.dot_general(ones, high, NT, preferred_element_type=f32)
                + lax.dot_general(ones, low, NT, preferred_element_type=f32)
                + 0.001
            )
            turned[:, span] = (values * jnp.asarray(-2.0, bf16)).T
        total[...] = jnp.zeros_like(total)

    spots = list(range(0, centers.shape[0], part))

    def products(start):
        block = centers[start : start + part, :]
        own = jnp.sum(jnp.square(block.astype(f32)), axis=1, keepdims=True)
        return own, jnp.dot(block, turned[...], preferred_element_type=f32)

    ahead = products(spots[0])
    for number, start in enumerate(spots):
        own, prods = ahead
        if number + 1 < len(spots):
            ahead = products(spots[number + 1])
        distance = jnp.maximum(prods + (own + norms[0:1, :]), 0.001)
        kernel = jnp.exp2(distance * lax.rsqrt(distance) * (-LOG2_E / spread)).astype(bf16)
        total[...] += jnp.dot(vt[:, start : start + part], kernel, preferred_element_type=f32)

    @pl.when(step == pl.num_programs(0) - 1)
    def _():
        for start, out in ((0, mine), (half, other)):
            span = slice(start, start + half)
            partial = total[0:channels, span].T - labels[span, :]
            high, low = split_two(partial)
            out[:, 0:channels] = high
            out[:, channels : 2 * channels] = low
            out[:, 2 * channels :] = jnp.zeros((half, out.shape[1] - 2 * channels), bf16)
            out[:, 2 * channels : 2 * channels + vectors] = total[channels:, span].T.astype(bf16)


def main(centers, vt, rows_mine, rows_other, labels):
    count, width = centers.shape
    half, channels = rows_mine.shape[0], labels.shape[1]
    block, part = 1024, 512
    whole = lambda shape: pl.BlockSpec(shape, lambda i: (0, 0))
    return pl.pallas_call(
        functools.partial(main_kernel, part=part),
        name="kernel_sums",
        grid=(count // block,),
        in_specs=[
            pl.BlockSpec((block, width), lambda i: (i, 0)),
            pl.BlockSpec((vt.shape[0], block), lambda i: (0, i)),
            whole((half, width)),
            whole((half, width)),
            whole((2 * half, channels)),
        ],
        out_specs=[whole((half, 512)), whole((half, 512))],
        out_shape=[jax.ShapeDtypeStruct((half, 512), bf16)] * 2,
        scratch_shapes=[
            pltpu.VMEM((width, 2 * half), bf16),
            pltpu.VMEM((8, 2 * half), f32),
            pltpu.VMEM((vt.shape[0], 2 * half), f32),
        ],
        compiler_params=pltpu.CompilerParams(vmem_limit_bytes=VMEM_LIMIT),
        cost_estimate=pl.CostEstimate(
            flops=2 * count * 2 * half * (width + vt.shape[0]),
            bytes_accessed=20 * 2**20,
            transcendentals=2 * count * 2 * half,
        ),
    )(centers, vt, rows_mine, rows_other, labels)


def finish_kernel(
    place, index_s, index_v, scale, vt, low, coeffs, mine, other, low_mine, low_other,
    updated, residual, nxt_v, nxt, all_rows, weights, nxt_sem,
):
    step = pl.program_id(0)
    members, channels = mine.shape[0], mine.shape[2]
    half = low_mine.shape[0]
    vectors = scale.shape[0]
    offset, core, row = place[0], place[1], place[2]
    total = 2 * half * members
    block = coeffs.shape[0]

    @pl.when(step == 0)
    def _():
        nxt_v[...] = next_hits(index_v[...], offset, updated.shape[0])
        copy = pltpu.make_async_copy(nxt_v, nxt, nxt_sem)
        copy.start()
        projected = jnp.zeros((vectors, channels), f32)
        for side, part in enumerate((mine, other)):
            for member in range(members):
                all_rows[side, member] = part[member, 0:half, :].astype(f32)
                projected += part[member, half : half + vectors, :].astype(f32)
                projected += part[member, half + vectors :, :].astype(f32)
        high, rest = split_two(projected * scale[...] * step_size)
        weights[0] = high
        weights[1] = rest
        first = pl.multiple_of(core * half, half)
        second = pl.multiple_of(half - core * half, half)
        residual[pl.ds(first, half), :] = all_rows[0, row] + low_mine[...].astype(f32)
        residual[pl.ds(second, half), :] = all_rows[1, row] + low_other[...].astype(f32)
        copy.wait()

    high = vt[channels:, :]
    correction = lax.dot_general(weights[0], high, TN, preferred_element_type=f32)
    correction += lax.dot_general(weights[1], high, TN, preferred_element_type=f32)
    correction += lax.dot_general(weights[0], low[...], TN, preferred_element_type=f32)
    span = pl.ds(pl.multiple_of(step * block, block), block)
    updated[span, :] = coeffs[...] + correction.T

    @pl.when(step == pl.num_programs(0) - 1)
    def _():
        def add(pos):
            local = index_s[pos] - offset
            member = (row - pos // (2 * half)) % members
            spot = pos % (2 * half)
            side = jnp.where(spot // half == core, 0, 1)
            value = all_rows[side, member, pl.ds(spot % half, 1), :]
            updated[pl.ds(local, 1), :] = updated[pl.ds(local, 1), :] - step_size * value
            return following(nxt, pos, total)

        lax.while_loop(lambda pos: pos < total, add, nxt[0, 0])


def finish(place, index, scale, vt, low, coeffs, mine, other, low_mine, low_other):
    count, channels = coeffs.shape
    vectors = scale.shape[0]
    half, members = low_mine.shape[0], mine.shape[0]
    total = index.shape[0]
    block = 1024
    smem = pl.BlockSpec(memory_space=pltpu.SMEM)
    whole = lambda shape: pl.BlockSpec(shape, lambda i: (0,) * len(shape))
    return pl.pallas_call(
        finish_kernel,
        name="finish",
        grid=(count // block,),
        in_specs=[
            smem,
            smem,
            whole((total // 128, 128)),
            whole((vectors, 1)),
            pl.BlockSpec((vt.shape[0], block), lambda i: (0, i)),
            pl.BlockSpec((vectors, block), lambda i: (0, i)),
            pl.BlockSpec((block, channels), lambda i: (i, 0)),
            whole(mine.shape),
            whole(other.shape),
            whole(low_mine.shape),
            whole(low_other.shape),
        ],
        out_specs=[whole((count, channels)), whole((2 * half, channels))],
        out_shape=[
            jax.ShapeDtypeStruct((count, channels), f32),
            jax.ShapeDtypeStruct((2 * half, channels), f32),
        ],
        scratch_shapes=[
            pltpu.VMEM((total // 128, 128), i32),
            pltpu.SMEM((total // 128, 128), i32),
            pltpu.VMEM((2, members, half, channels), f32),
            pltpu.VMEM((2, vectors, channels), bf16),
            pltpu.SemaphoreType.DMA,
        ],
        compiler_params=pltpu.CompilerParams(vmem_limit_bytes=VMEM_LIMIT),
        cost_estimate=pl.CostEstimate(flops=10**9, bytes_accessed=14 * 2**20, transcendentals=0),
    )(
        place, index, index.reshape(total // 128, 128), scale.reshape(vectors, 1), vt, low,
        coeffs, mine, other, low_mine, low_other,
    )


def body(centers, coeffs, targets, batch_index, subset_index, eigvec, eigen_scale, *, groups):
    count = centers.shape[0]
    channels = coeffs.shape[1]
    vectors = eigvec.shape[0]
    position = lax.axis_index("centers")
    row = lax.axis_index("batch")
    offset = position * count
    place = jnp.stack([offset, position % 2, row, row]).astype(i32)
    members = lax.axis_size("batch")
    chips = len(groups[0])
    width = centers.shape[1]
    half = batch_index.shape[0] // 2
    swap = [(i, i ^ 1) for i in range(2 * chips)]

    def across(values):
        return lax.all_to_all(
            values, "centers", 0, 0, tiled=True, axis_index_groups=groups
        )

    turns = [
        lax.ppermute(batch_index, "batch", [(i, (i + k) % members) for i in range(members)])
        for k in range(1, members)
    ]
    all_index = jnp.concatenate([batch_index] + turns)

    mine, other, labels = pick(place, batch_index, centers, targets)
    summed = mine + lax.ppermute(other, "centers", swap)
    shards = across(summed).reshape(chips, half // chips, width)
    shard = jnp.sum(shards.astype(f32), axis=0).astype(bf16)
    rows_mine = across(jnp.tile(shard, (chips, 1)))
    rows_other = lax.ppermute(rows_mine, "centers", swap)

    vt, low = prepare(subset_index - offset, eigvec, coeffs)
    sums_mine, sums_other = main(centers, vt, rows_mine, rows_other, labels)

    def widened(values):
        values = values.astype(f32)
        return values[..., 0:channels] + values[..., channels : 2 * channels], values[..., 2 * channels :]

    def packed(residual, rest):
        high, low = split_rounded(residual)
        return jnp.concatenate([high, low, rest.astype(bf16)], axis=-1)

    first = widened(sums_mine)
    second = widened(lax.ppermute(sums_other, "centers", swap))
    chip_sums = packed(first[0] + second[0], first[1] + second[1])
    parts = widened(across(chip_sums).reshape(chips, half // chips, -1))
    shard = packed(jnp.sum(parts[0], axis=0), jnp.sum(parts[1], axis=0))
    gathered = across(jnp.tile(shard, (chips, 1)))
    high = gathered[:, 0:channels]
    low_mine = gathered[:, channels : 2 * channels]
    low_other = lax.ppermute(low_mine, "centers", swap)
    projected = lax.dot_general(
        gathered[:, 2 * channels : 2 * channels + vectors], high, TN, preferred_element_type=f32
    )
    message = jnp.concatenate([high, *split_rounded(projected)], axis=0)
    from_batch = lax.all_to_all(
        jnp.tile(message[None], (members, 1, 1)), "batch", 0, 0, tiled=True
    )
    from_other = lax.ppermute(from_batch, "centers", swap)
    return finish(
        place, all_index, eigen_scale, vt, low, coeffs, from_batch, from_other, low_mine, low_other
    )


def solution(mesh):
    chips = mesh.shape["centers"] // 2
    groups = [[2 * chip + core for chip in range(chips)] for core in range(2)]
    return jax.shard_map(
        functools.partial(body, groups=groups),
        mesh=mesh,
        in_specs=(
            P("centers", None),
            P("centers", None),
            P("centers", None),
            P("batch"),
            P("centers"),
            P(None, "centers"),
            P(),
        ),
        out_specs=(P("centers", None), P("batch", None)),
        check_vma=False,
    )
```

```python
import functools

import jax
import jax.numpy as jnp
from jax import lax
from jax.experimental import pallas as pl
from jax.experimental.pallas import tpu as pltpu
from jax.sharding import PartitionSpec as P

spread = 1.0
step_size = 0.5
NT = (((1,), (1,)), ((), ()))
TN = (((0,), (0,)), ((), ()))
bf16 = jnp.bfloat16
f32 = jnp.float32
i32 = jnp.int32
VMEM_LIMIT = 56 * 2**20
LOG2_E = 1.4426950408889634
SLOTS = 128


def split_two(values):
    high = values.astype(bf16)
    return high, (values - high.astype(f32)).astype(bf16)


def split_rounded(values):
    high = lax.reduce_precision(values, 8, 7)
    return high.astype(bf16), (values - high).astype(bf16)


def next_hits(index, offset, count):
    rows = index.shape[0]
    total = rows * 128
    lane = lax.broadcasted_iota(i32, (rows, 128), 1)
    sub = lax.broadcasted_iota(i32, (rows, 128), 0)
    local = index - offset
    found = jnp.where((local >= 0) & (local < count), sub * 128 + lane, total)
    shift = 1
    while shift < 128:
        moved = pltpu.roll(found, 128 - shift, 1)
        found = jnp.minimum(found, jnp.where(lane < 128 - shift, moved, total))
        shift *= 2
    later = jnp.broadcast_to(found[:, 0:1], (rows, 128))
    later = jnp.where(sub < rows - 1, pltpu.roll(later, rows - 1, 0), total)
    shift = 1
    while shift < rows:
        moved = pltpu.roll(later, rows - shift, 0)
        later = jnp.minimum(later, jnp.where(sub < rows - shift, moved, total))
        shift *= 2
    return jnp.minimum(found, later)


def following(nxt, pos, total):
    after = jnp.minimum(pos + 1, total - 1)
    return jnp.where(pos + 1 < total, nxt[after >> 7, after & 127], total)


def pick_kernel(
    place, index_s, index_v, centers, targets, mine, other, labels,
    nxt_v, nxt, tiles, label_tiles, wide, label_wide, rows, sems, nxt_sem,
):
    total = rows.shape[0]
    half = total // 2
    offset, core = place[0], place[1]
    nxt_v[...] = next_hits(index_v[...], offset, centers.shape[0])
    copy = pltpu.make_async_copy(nxt_v, nxt, nxt_sem)
    copy.start()
    rows[...] = jnp.zeros_like(rows)
    labels[...] = jnp.zeros_like(labels)
    copy.wait()

    def copies(pos, slot):
        local = index_s[pos] - offset
        base = pl.multiple_of((local >> 4) << 4, 16)
        return (
            pltpu.make_async_copy(centers.at[pl.ds(base, 16), :], tiles.at[slot], sems.at[0, slot]),
            pltpu.make_async_copy(targets.at[pl.ds(base, 16), :], label_tiles.at[slot], sems.at[1, slot]),
        )

    def issue(state):
        slot, pos = state
        for one in copies(pos, slot):
            one.start()
        return slot + 1, following(nxt, pos, total)

    def drain(slot, pos):
        for one in copies(pos, slot):
            one.wait()
        line = (index_s[pos] - offset) & 15
        wide[...] = tiles[slot].astype(f32)
        label_wide[...] = label_tiles[slot].astype(f32)
        spot = jnp.where(core == 0, pos, pos ^ half)
        rows[pl.ds(spot, 1), :] = wide[pl.ds(line, 1), :]
        labels[pl.ds(spot, 1), :] = label_wide[pl.ds(line, 1), :]
        return following(nxt, pos, total)

    def batch(pos):
        used, _ = lax.while_loop(
            lambda s: (s[0] < SLOTS) & (s[1] < total), issue, (jnp.int32(0), pos)
        )
        return lax.fori_loop(0, used, drain, pos)

    lax.while_loop(lambda pos: pos < total, batch, nxt[0, 0])
    mine[...] = rows[0:half, :].astype(bf16)
    other[...] = rows[half:total, :].astype(bf16)


def pick(place, index, centers, targets):
    total, width, labels = index.shape[0], centers.shape[1], targets.shape[1]
    vmem = pl.BlockSpec(memory_space=pltpu.VMEM)
    smem = pl.BlockSpec(memory_space=pltpu.SMEM)
    hbm = pl.BlockSpec(memory_space=pl.ANY)
    return pl.pallas_call(
        pick_kernel,
        name="pick",
        in_specs=[smem, smem, vmem, hbm, hbm],
        out_specs=[vmem, vmem, vmem],
        out_shape=[
            jax.ShapeDtypeStruct((total // 2, width), bf16),
            jax.ShapeDtypeStruct((total // 2, width), bf16),
            jax.ShapeDtypeStruct((total, labels), f32),
        ],
        scratch_shapes=[
            pltpu.VMEM((total // 128, 128), i32),
            pltpu.SMEM((total // 128, 128), i32),
            pltpu.VMEM((SLOTS, 16, width), bf16),
            pltpu.VMEM((SLOTS, 16, labels), bf16),
            pltpu.VMEM((16, width), f32),
            pltpu.VMEM((16, labels), f32),
            pltpu.VMEM((total, width), f32),
            pltpu.SemaphoreType.DMA((2, SLOTS)),
            pltpu.SemaphoreType.DMA,
        ],
        compiler_params=pltpu.CompilerParams(vmem_limit_bytes=VMEM_LIMIT),
        cost_estimate=pl.CostEstimate(flops=0, bytes_accessed=4 * 2**20, transcendentals=0),
    )(place, index, index.reshape(total // 128, 128), centers, targets)


def prepare_kernel(place, subset, index_s, index_v, eigvec, high, low, hits, turned, spread_out, nxt_v, nxt, nxt_sem):
    step = pl.program_id(0)
    vectors, count = eigvec.shape
    block = high.shape[0]
    total = index_s.shape[0]

    @pl.when(step == 0)
    def _():
        offset, core, row, members, bits = place[0], place[1], place[2], place[3], place[4]
        nxt_v[...] = next_hits(index_v[...], offset, spread_out.shape[0])
        copy = pltpu.make_async_copy(nxt_v, nxt, nxt_sem)
        copy.start()
        spread_out[...] = jnp.zeros_like(spread_out)
        size = 512
        for start in range(0, count, size):
            turned[start : start + size, 0:vectors] = eigvec[:, start : start + size].T

        def put(group, _):
            for one in range(16):
                k = group * 16 + one
                spread_out[pl.ds(subset[k] - offset, 1), :] = turned[pl.ds(k, 1), :]
            return 0

        lax.fori_loop(0, count // 16, put, 0)
        copy.wait()

        def note(state):
            number, pos = state
            after = following(nxt, pos, total)
            member = (row + members - (pos >> (bits + 1))) & (members - 1)
            side = ((pos >> bits) & 1) ^ core
            source = (((side * members) + member) << bits) + (pos & ((1 << bits) - 1))
            hits[number] = (source << 16) + (index_s[pos] - offset)
            return number + 1, after

        number, _ = lax.while_loop(lambda s: s[1] < total, note, (jnp.int32(1), nxt[0, 0]))
        hits[0] = number - 1

    span = pl.ds(pl.multiple_of(step * block, block), block)
    top, rest = split_two(spread_out[span, 0:vectors])
    high[...] = top
    low[...] = rest


def prepare(place, subset, index, eigvec, centers):
    vectors, count = eigvec.shape
    total = index.shape[0]
    block = 1024
    smem = pl.BlockSpec(memory_space=pltpu.SMEM)
    whole = lambda shape: pl.BlockSpec(shape, lambda i: (0, 0))
    lanes = -(-vectors // 128) * 128
    return pl.pallas_call(
        prepare_kernel,
        name="prepare",
        grid=(centers // block,),
        in_specs=[smem, smem, smem, whole((total // 128, 128)), whole((vectors, count))],
        out_specs=[
            pl.BlockSpec((block, vectors), lambda i: (i, 0)),
            pl.BlockSpec((block, vectors), lambda i: (i, 0)),
            smem,
        ],
        out_shape=[
            jax.ShapeDtypeStruct((centers, vectors), bf16),
            jax.ShapeDtypeStruct((centers, vectors), bf16),
            jax.ShapeDtypeStruct((total + 8,), i32),
        ],
        scratch_shapes=[
            pltpu.VMEM((count, lanes), f32),
            pltpu.VMEM((centers, lanes), f32),
            pltpu.VMEM((total // 128, 128), i32),
            pltpu.SMEM((total // 128, 128), i32),
            pltpu.SemaphoreType.DMA,
        ],
        compiler_params=pltpu.CompilerParams(vmem_limit_bytes=VMEM_LIMIT),
        cost_estimate=pl.CostEstimate(flops=0, bytes_accessed=30 * 2**20, transcendentals=0),
    )(place, subset, index, index.reshape(total // 128, 128), eigvec)


def main_kernel(
    centers, coeffs, vectors_t, rows_mine, rows_other, labels, mine, other, turned, norms, total, *, part
):
    step = pl.program_id(0)
    half = rows_mine.shape[0]
    channels = labels.shape[1]
    vectors = vectors_t.shape[1]

    @pl.when(step == 0)
    def _():
        ones = jnp.ones((8, rows_mine.shape[1]), bf16)
        for start, rows in ((0, rows_mine), (half, rows_other)):
            span = slice(start, start + half)
            values = rows[...]
            high, low = split_two(jnp.square(values.astype(f32)))
            norms[:, span] = (
                lax.dot_general(ones, high, NT, preferred_element_type=f32)
                + lax.dot_general(ones, low, NT, preferred_element_type=f32)
                + 0.001
            )
            turned[:, span] = (values * jnp.asarray(-2.0, bf16)).T
        total[...] = jnp.zeros_like(total)

    spots = list(range(0, centers.shape[0], part))

    def products(start):
        block = centers[start : start + part, :]
        own = jnp.sum(jnp.square(block.astype(f32)), axis=1, keepdims=True)
        return own, jnp.dot(block, turned[...], preferred_element_type=f32)

    ahead = products(spots[0])
    for number, start in enumerate(spots):
        own, prods = ahead
        if number + 1 < len(spots):
            ahead = products(spots[number + 1])
        distance = jnp.maximum(prods + (own + norms[0:1, :]), 0.001)
        kernel = jnp.exp2(distance * lax.rsqrt(distance) * (-LOG2_E / spread)).astype(bf16)
        span = slice(start, start + part)
        total[0:channels, :] += lax.dot_general(
            coeffs[span, :].astype(bf16), kernel, TN, preferred_element_type=f32
        )
        total[channels:, :] += lax.dot_general(
            vectors_t[span, :], kernel, TN, preferred_element_type=f32
        )

    @pl.when(step == pl.num_programs(0) - 1)
    def _():
        for start, out in ((0, mine), (half, other)):
            span = slice(start, start + half)
            partial = total[0:channels, span].T - labels[span, :]
            high, low = split_two(partial)
            out[:, 0:channels] = high
            out[:, channels : 2 * channels] = low
            out[:, 2 * channels :] = jnp.zeros((half, out.shape[1] - 2 * channels), bf16)
            out[:, 2 * channels : 2 * channels + vectors] = total[channels:, span].T.astype(bf16)


def main(centers, coeffs, vectors_t, rows_mine, rows_other, labels):
    count, width = centers.shape
    half, channels = rows_mine.shape[0], labels.shape[1]
    columns = channels + vectors_t.shape[1]
    block, part = 1024, 512
    whole = lambda shape: pl.BlockSpec(shape, lambda i: (0, 0))
    return pl.pallas_call(
        functools.partial(main_kernel, part=part),
        name="kernel_sums",
        grid=(count // block,),
        in_specs=[
            pl.BlockSpec((block, width), lambda i: (i, 0)),
            pl.BlockSpec((block, channels), lambda i: (i, 0)),
            pl.BlockSpec((block, vectors_t.shape[1]), lambda i: (i, 0)),
            whole((half, width)),
            whole((half, width)),
            whole((2 * half, channels)),
        ],
        out_specs=[whole((half, 512)), whole((half, 512))],
        out_shape=[jax.ShapeDtypeStruct((half, 512), bf16)] * 2,
        scratch_shapes=[
            pltpu.VMEM((width, 2 * half), bf16),
            pltpu.VMEM((8, 2 * half), f32),
            pltpu.VMEM((columns, 2 * half), f32),
        ],
        compiler_params=pltpu.CompilerParams(vmem_limit_bytes=VMEM_LIMIT),
        cost_estimate=pl.CostEstimate(
            flops=2 * count * 2 * half * (width + columns),
            bytes_accessed=20 * 2**20,
            transcendentals=2 * count * 2 * half,
        ),
    )(centers, coeffs, vectors_t, rows_mine, rows_other, labels)


def finish_kernel(
    place, hits, scale, high, low, coeffs, mine, other, low_mine, low_other,
    updated, residual, all_rows, weights,
):
    step = pl.program_id(0)
    members, channels = mine.shape[0], mine.shape[2]
    half = low_mine.shape[0]
    vectors = scale.shape[0]
    core, row = place[1], place[2]
    block = coeffs.shape[0]

    @pl.when(step == 0)
    def _():
        projected = jnp.zeros((vectors, channels), f32)
        for side, part in enumerate((mine, other)):
            for member in range(members):
                start = (side * members + member) * half
                all_rows[start : start + half, :] = part[member, 0:half, :].astype(f32) * -step_size
                projected += part[member, half : half + vectors, :].astype(f32)
                projected += part[member, half + vectors :, :].astype(f32)
        top, rest = split_two(projected * scale[...] * step_size)
        weights[0] = top
        weights[1] = rest
        for side, part, rest in ((0, mine, low_mine), (1, other, low_other)):
            start = pl.multiple_of((core ^ side) * half, half)
            residual[pl.ds(start, half), :] = part[row, 0:half, :].astype(f32) + rest[...].astype(f32)

    correction = jnp.dot(high[...], weights[0], preferred_element_type=f32)
    correction += jnp.dot(high[...], weights[1], preferred_element_type=f32)
    correction += jnp.dot(low[...], weights[0], preferred_element_type=f32)
    span = pl.ds(pl.multiple_of(step * block, block), block)
    updated[span, :] = coeffs[...] + correction

    @pl.when(step == pl.num_programs(0) - 1)
    def _():
        def add(k):
            local = pl.ds(hits[k] & 65535, 1)
            updated[local, :] = updated[local, :] + all_rows[pl.ds(hits[k] >> 16, 1), :]

        def four(group, _):
            for one in range(4):
                add(group * 4 + one + 1)
            return 0

        def single(k, _):
            add(k)
            return 0

        fours = hits[0] >> 2
        lax.fori_loop(0, fours, four, 0)
        lax.fori_loop(fours * 4 + 1, hits[0] + 1, single, 0)


def finish(place, hits, scale, high, low, coeffs, mine, other, low_mine, low_other):
    count, channels = coeffs.shape
    vectors = scale.shape[0]
    half, members = low_mine.shape[0], mine.shape[0]
    block = 1024
    smem = pl.BlockSpec(memory_space=pltpu.SMEM)
    whole = lambda shape: pl.BlockSpec(shape, lambda i: (0,) * len(shape))
    return pl.pallas_call(
        finish_kernel,
        name="finish",
        grid=(count // block,),
        in_specs=[
            smem,
            smem,
            whole((vectors, 1)),
            pl.BlockSpec((block, vectors), lambda i: (i, 0)),
            pl.BlockSpec((block, vectors), lambda i: (i, 0)),
            pl.BlockSpec((block, channels), lambda i: (i, 0)),
            whole(mine.shape),
            whole(other.shape),
            whole(low_mine.shape),
            whole(low_other.shape),
        ],
        out_specs=[whole((count, channels)), whole((2 * half, channels))],
        out_shape=[
            jax.ShapeDtypeStruct((count, channels), f32),
            jax.ShapeDtypeStruct((2 * half, channels), f32),
        ],
        scratch_shapes=[
            pltpu.VMEM((2 * members * half, channels), f32),
            pltpu.VMEM((2, vectors, channels), bf16),
        ],
        compiler_params=pltpu.CompilerParams(vmem_limit_bytes=VMEM_LIMIT),
        cost_estimate=pl.CostEstimate(flops=10**9, bytes_accessed=14 * 2**20, transcendentals=0),
    )(place, hits, scale.reshape(vectors, 1), high, low, coeffs, mine, other, low_mine, low_other)


def body(centers, coeffs, targets, batch_index, subset_index, eigvec, eigen_scale, *, groups):
    count = centers.shape[0]
    channels = coeffs.shape[1]
    vectors = eigvec.shape[0]
    position = lax.axis_index("centers")
    row = lax.axis_index("batch")
    offset = position * count
    members = lax.axis_size("batch")
    half = batch_index.shape[0] // 2
    place = jnp.stack(
        [offset, position % 2, row, jnp.int32(members), jnp.int32(half.bit_length() - 1)]
    ).astype(i32)
    chips = len(groups[0])
    width = centers.shape[1]
    swap = [(i, i ^ 1) for i in range(2 * chips)]

    def across(values):
        return lax.all_to_all(
            values, "centers", 0, 0, tiled=True, axis_index_groups=groups
        )

    turns = [
        lax.ppermute(batch_index, "batch", [(i, (i + k) % members) for i in range(members)])
        for k in range(1, members)
    ]
    all_index = jnp.concatenate([batch_index] + turns)

    mine, other, labels = pick(place, batch_index, centers, targets)
    summed = mine + lax.ppermute(other, "centers", swap)
    shards = across(summed).reshape(chips, half // chips, width)
    shard = jnp.sum(shards.astype(f32), axis=0).astype(bf16)
    rows_mine = across(jnp.tile(shard, (chips, 1)))
    rows_other = lax.ppermute(rows_mine, "centers", swap)

    top, low, hits = prepare(place, subset_index, all_index, eigvec, count)
    sums_mine, sums_other = main(centers, coeffs, top, rows_mine, rows_other, labels)

    def widened(values):
        values = values.astype(f32)
        return values[..., 0:channels] + values[..., channels : 2 * channels], values[..., 2 * channels :]

    def packed(residual, rest):
        high, low = split_rounded(residual)
        return jnp.concatenate([high, low, rest.astype(bf16)], axis=-1)

    first = widened(sums_mine)
    second = widened(lax.ppermute(sums_other, "centers", swap))
    chip_sums = packed(first[0] + second[0], first[1] + second[1])
    parts = widened(across(chip_sums).reshape(chips, half // chips, -1))
    shard = packed(jnp.sum(parts[0], axis=0), jnp.sum(parts[1], axis=0))
    gathered = across(jnp.tile(shard, (chips, 1)))
    high = gathered[:, 0:channels]
    low_mine = gathered[:, channels : 2 * channels]
    low_other = lax.ppermute(low_mine, "centers", swap)
    projected = lax.dot_general(
        gathered[:, 2 * channels : 2 * channels + vectors], high, TN, preferred_element_type=f32
    )
    message = jnp.concatenate([high, *split_rounded(projected)], axis=0)
    from_batch = lax.all_to_all(
        jnp.tile(message[None], (members, 1, 1)), "batch", 0, 0, tiled=True
    )
    from_other = lax.ppermute(from_batch, "centers", swap)
    return finish(
        place, hits, eigen_scale, top, low, coeffs, from_batch, from_other, low_mine, low_other
    )


def solution(mesh):
    chips = mesh.shape["centers"] // 2
    groups = [[2 * chip + core for chip in range(chips)] for core in range(2)]
    return jax.shard_map(
        functools.partial(body, groups=groups),
        mesh=mesh,
        in_specs=(
            P("centers", None),
            P("centers", None),
            P("centers", None),
            P("batch"),
            P("centers"),
            P(None, "centers"),
            P(),
        ),
        out_specs=(P("centers", None), P("batch", None)),
        check_vma=False,
    )
```

```python
import functools

import jax
import jax.numpy as jnp
from jax import lax
from jax.experimental import pallas as pl
from jax.experimental.pallas import tpu as pltpu
from jax.sharding import PartitionSpec as P

spread = 1.0
step_size = 0.5
NT = (((1,), (1,)), ((), ()))
TN = (((0,), (0,)), ((), ()))
bf16 = jnp.bfloat16
f32 = jnp.float32
i32 = jnp.int32
VMEM_LIMIT = 56 * 2**20
LOG2_E = 1.4426950408889634
SLOTS = 16


def split_two(values):
    high = values.astype(bf16)
    return high, (values - high.astype(f32)).astype(bf16)


def split_rounded(values):
    high = lax.reduce_precision(values, 8, 7)
    return high.astype(bf16), (values - high).astype(bf16)


def next_hits(index, offset, count):
    rows = index.shape[0]
    total = rows * 128
    lane = lax.broadcasted_iota(i32, (rows, 128), 1)
    sub = lax.broadcasted_iota(i32, (rows, 128), 0)
    local = index - offset
    found = jnp.where((local >= 0) & (local < count), sub * 128 + lane, total)
    shift = 1
    while shift < 128:
        moved = pltpu.roll(found, 128 - shift, 1)
        found = jnp.minimum(found, jnp.where(lane < 128 - shift, moved, total))
        shift *= 2
    later = jnp.broadcast_to(found[:, 0:1], (rows, 128))
    later = jnp.where(sub < rows - 1, pltpu.roll(later, rows - 1, 0), total)
    shift = 1
    while shift < rows:
        moved = pltpu.roll(later, rows - shift, 0)
        later = jnp.minimum(later, jnp.where(sub < rows - shift, moved, total))
        shift *= 2
    return jnp.minimum(found, later)


def following(nxt, pos, total):
    after = jnp.minimum(pos + 1, total - 1)
    return jnp.where(pos + 1 < total, nxt[after >> 7, after & 127], total)


def pick_kernel(
    index_s, index_v, centers, targets, mine, other, labels,
    nxt_v, nxt, tiles, label_tiles, wide, label_wide, rows, sems, nxt_sem,
):
    total = rows.shape[0]
    half = total // 2
    position = lax.axis_index("centers")
    offset = position * centers.shape[0]
    turn = (position & 1) * half
    nxt_v[...] = next_hits(index_v[...], offset, centers.shape[0])
    copy = pltpu.make_async_copy(nxt_v, nxt, nxt_sem)
    copy.start()
    rows[...] = jnp.zeros_like(rows)
    labels[...] = jnp.zeros_like(labels)
    copy.wait()

    def copies(pos, slot):
        base = pl.multiple_of(((index_s[pos] - offset) >> 4) << 4, 16)
        return (
            pltpu.make_async_copy(centers.at[pl.ds(base, 16), :], tiles.at[slot], sems.at[0, slot]),
            pltpu.make_async_copy(targets.at[pl.ds(base, 16), :], label_tiles.at[slot], sems.at[1, slot]),
        )

    def issue(pos, slot):
        for one in copies(pos, slot):
            one.start()
        return following(nxt, pos, total)

    def drain(pos, slot):
        for one in copies(pos, slot):
            one.wait()
        line = pl.ds((index_s[pos] - offset) & 15, 1)
        spot = pl.ds(pos ^ turn, 1)
        wide[...] = tiles[slot].astype(f32)
        label_wide[...] = label_tiles[slot].astype(f32)
        rows[spot, :] = wide[line, :]
        labels[spot, :] = label_wide[line, :]
        return following(nxt, pos, total)

    first = nxt[0, 0]
    used, ahead = lax.while_loop(
        lambda s: (s[0] < SLOTS) & (s[1] < total),
        lambda s: (s[0] + 1, issue(s[1], s[0])),
        (jnp.int32(0), first),
    )

    def both(state):
        slot, behind, ahead = state
        behind = drain(behind, slot)
        ahead = issue(ahead, slot)
        return jnp.where(slot == SLOTS - 1, 0, slot + 1), behind, ahead

    slot, behind, _ = lax.while_loop(
        lambda s: s[2] < total, both, (jnp.int32(0), first, ahead)
    )

    def rest(state):
        slot, behind = state
        behind = drain(behind, slot)
        return jnp.where(slot == SLOTS - 1, 0, slot + 1), behind

    lax.while_loop(lambda s: s[1] < total, rest, (slot, behind))
    mine[...] = rows[0:half, :].astype(bf16)
    other[...] = rows[half:total, :].astype(bf16)


def pick(index, centers, targets):
    total, width, labels = index.shape[0], centers.shape[1], targets.shape[1]
    vmem = pl.BlockSpec(memory_space=pltpu.VMEM)
    smem = pl.BlockSpec(memory_space=pltpu.SMEM)
    hbm = pl.BlockSpec(memory_space=pl.ANY)
    return pl.pallas_call(
        pick_kernel,
        name="pick",
        in_specs=[smem, vmem, hbm, hbm],
        out_specs=[vmem, vmem, vmem],
        out_shape=[
            jax.ShapeDtypeStruct((total // 2, width), bf16),
            jax.ShapeDtypeStruct((total // 2, width), bf16),
            jax.ShapeDtypeStruct((total, labels), f32),
        ],
        scratch_shapes=[
            pltpu.VMEM((total // 128, 128), i32),
            pltpu.SMEM((total // 128, 128), i32),
            pltpu.VMEM((SLOTS, 16, width), bf16),
            pltpu.VMEM((SLOTS, 16, labels), bf16),
            pltpu.VMEM((16, width), f32),
            pltpu.VMEM((16, labels), f32),
            pltpu.VMEM((total, width), f32),
            pltpu.SemaphoreType.DMA((2, SLOTS)),
            pltpu.SemaphoreType.DMA,
        ],
        compiler_params=pltpu.CompilerParams(vmem_limit_bytes=VMEM_LIMIT),
        cost_estimate=pl.CostEstimate(flops=0, bytes_accessed=4 * 2**20, transcendentals=0),
    )(index, index.reshape(total // 128, 128), centers, targets)


def prepare_kernel(*refs, members, half):
    subset, *refs = refs
    index_s, refs = refs[:members], refs[members:]
    index_v, refs = refs[:members], refs[members:]
    eigvec, spread_rows, hits, wide, nxt_v, nxt, nxt_sem = refs
    step = pl.program_id(0)
    vectors, count = eigvec.shape
    block = spread_rows.shape[0]
    total = 2 * half * members
    each = 2 * half
    bits = half.bit_length() - 1

    @pl.when(step == 0)
    def _():
        position, row = lax.axis_index("centers"), lax.axis_index("batch")
        offset = position * wide.shape[0]
        core = position & 1
        lines = each // 128
        for member in range(members):
            nxt_v[member * lines : (member + 1) * lines, :] = index_v[member][...]
        nxt_v[...] = next_hits(nxt_v[...], offset, wide.shape[0])
        copy = pltpu.make_async_copy(nxt_v, nxt, nxt_sem)
        copy.start()
        wide[...] = jnp.zeros_like(wide)

        def put(group, _):
            start = pl.multiple_of(group * 128, 128)
            rows = eigvec[:, pl.ds(start, 128)].T
            for eight in range(0, 128, 8):
                spots = [subset[start + eight + one] - offset for one in range(8)]
                for one in range(8):
                    wide[pl.ds(spots[one], 1), 0:vectors] = rows[eight + one : eight + one + 1, :]
            return 0

        lax.fori_loop(0, count // 128, put, 0)
        copy.wait()

        def gather_member(member, state):
            limit = (member + 1) * each
            owner = (row + members - member) & (members - 1)

            def note(state):
                number, pos = state
                after = following(nxt, pos, total)
                spot = pos - member * each
                side = (spot >> bits) ^ core
                source = (((side * members) + owner) << bits) + (spot & (half - 1))
                hits[number] = (source << 16) + (index_s[member][spot] - offset)
                return number + 1, after

            return lax.while_loop(lambda s: s[1] < limit, note, state)

        state = (jnp.int32(1), nxt[0, 0])
        for member in range(members):
            state = gather_member(member, state)
        hits[0] = state[0] - 1

    span = pl.ds(pl.multiple_of(step * block, block), block)
    spread_rows[...] = wide[span, 0:vectors].astype(bf16)


def prepare(subset, indices, eigvec, centers):
    vectors, count = eigvec.shape
    members, each = len(indices), indices[0].shape[0]
    total = members * each
    block = 2048
    smem = pl.BlockSpec(memory_space=pltpu.SMEM)
    whole = lambda shape: pl.BlockSpec(shape, lambda i: (0, 0))
    lanes = -(-vectors // 128) * 128
    return pl.pallas_call(
        functools.partial(prepare_kernel, members=members, half=each // 2),
        name="prepare",
        grid=(centers // block,),
        in_specs=[smem] * (1 + members)
        + [whole((each // 128, 128))] * members
        + [whole((vectors, count))],
        out_specs=[pl.BlockSpec((block, vectors), lambda i: (i, 0)), smem],
        out_shape=[
            jax.ShapeDtypeStruct((centers, vectors), bf16),
            jax.ShapeDtypeStruct((total + 8,), i32),
        ],
        scratch_shapes=[
            pltpu.VMEM((centers, lanes), f32),
            pltpu.VMEM((total // 128, 128), i32),
            pltpu.SMEM((total // 128, 128), i32),
            pltpu.SemaphoreType.DMA,
        ],
        compiler_params=pltpu.CompilerParams(vmem_limit_bytes=VMEM_LIMIT),
        cost_estimate=pl.CostEstimate(flops=0, bytes_accessed=30 * 2**20, transcendentals=0),
    )(subset, *indices, *[one.reshape(each // 128, 128) for one in indices], eigvec)


def main_kernel(
    centers, coeffs, vectors_t, rows_mine, rows_other, labels, mine, other, turned, norms, total, *, part
):
    step = pl.program_id(0)
    half = rows_mine.shape[0]
    channels = labels.shape[1]
    vectors = vectors_t.shape[1]

    @pl.when(step == 0)
    def _():
        ones = jnp.ones((8, rows_mine.shape[1]), bf16)
        for start, rows in ((0, rows_mine), (half, rows_other)):
            span = slice(start, start + half)
            values = rows[...]
            high, low = split_two(jnp.square(values.astype(f32)))
            norms[:, span] = (
                lax.dot_general(ones, high, NT, preferred_element_type=f32)
                + lax.dot_general(ones, low, NT, preferred_element_type=f32)
                + 0.001
            )
            turned[:, span] = (values * jnp.asarray(-2.0, bf16)).T
        total[...] = jnp.zeros_like(total)

    spots = list(range(0, centers.shape[0], part))

    def products(start):
        block = centers[start : start + part, :]
        own = jnp.sum(jnp.square(block.astype(f32)), axis=1, keepdims=True)
        return own, jnp.dot(block, turned[...], preferred_element_type=f32)

    ahead = products(spots[0])
    for number, start in enumerate(spots):
        own, prods = ahead
        if number + 1 < len(spots):
            ahead = products(spots[number + 1])
        distance = jnp.maximum(prods + (own + norms[0:1, :]), 0.001)
        kernel = jnp.exp2(distance * lax.rsqrt(distance) * (-LOG2_E / spread)).astype(bf16)
        span = slice(start, start + part)
        total[0:channels, :] += lax.dot_general(
            coeffs[span, :].astype(bf16), kernel, TN, preferred_element_type=f32
        )
        total[channels:, :] += lax.dot_general(
            vectors_t[span, :], kernel, TN, preferred_element_type=f32
        )

    @pl.when(step == pl.num_programs(0) - 1)
    def _():
        for start, out in ((0, mine), (half, other)):
            span = slice(start, start + half)
            partial = total[0:channels, span].T - labels[span, :]
            high, low = split_two(partial)
            out[:, 0:channels] = high
            out[:, channels : 2 * channels] = low
            out[:, 2 * channels :] = jnp.zeros((half, out.shape[1] - 2 * channels), bf16)
            out[:, 2 * channels : 2 * channels + vectors] = total[channels:, span].T.astype(bf16)


def main(centers, coeffs, vectors_t, rows_mine, rows_other, labels):
    count, width = centers.shape
    half, channels = rows_mine.shape[0], labels.shape[1]
    columns = channels + vectors_t.shape[1]
    block, part = 1024, 512
    whole = lambda shape: pl.BlockSpec(shape, lambda i: (0, 0))
    return pl.pallas_call(
        functools.partial(main_kernel, part=part),
        name="kernel_sums",
        grid=(count // block,),
        in_specs=[
            pl.BlockSpec((block, width), lambda i: (i, 0)),
            pl.BlockSpec((block, channels), lambda i: (i, 0)),
            pl.BlockSpec((block, vectors_t.shape[1]), lambda i: (i, 0)),
            whole((half, width)),
            whole((half, width)),
            whole((2 * half, channels)),
        ],
        out_specs=[whole((half, 512)), whole((half, 512))],
        out_shape=[jax.ShapeDtypeStruct((half, 512), bf16)] * 2,
        scratch_shapes=[
            pltpu.VMEM((width, 2 * half), bf16),
            pltpu.VMEM((8, 2 * half), f32),
            pltpu.VMEM((columns, 2 * half), f32),
        ],
        compiler_params=pltpu.CompilerParams(vmem_limit_bytes=VMEM_LIMIT),
        cost_estimate=pl.CostEstimate(
            flops=2 * count * 2 * half * (width + columns),
            bytes_accessed=20 * 2**20,
            transcendentals=2 * count * 2 * half,
        ),
    )(centers, coeffs, vectors_t, rows_mine, rows_other, labels)


def finish_kernel(
    hits, scale, vectors_t, coeffs, mine, other, low_mine, low_other,
    updated, residual, all_rows, weights,
):
    step = pl.program_id(0)
    members, channels = mine.shape[0], mine.shape[2]
    half = low_mine.shape[0]
    vectors = scale.shape[0]
    block = coeffs.shape[0]

    @pl.when(step == 0)
    def _():
        core, row = lax.axis_index("centers") & 1, lax.axis_index("batch")
        projected = jnp.zeros((vectors, channels), f32)
        for side, part in enumerate((mine, other)):
            for member in range(members):
                start = (side * members + member) * half
                all_rows[start : start + half, :] = part[member, 0:half, :].astype(f32) * -step_size
                projected += part[member, half : half + vectors, :].astype(f32)
                projected += part[member, half + vectors :, :].astype(f32)
        top, rest = split_two(projected * scale[...] * step_size)
        weights[:, 0:channels] = top
        weights[:, channels:] = rest
        for side, part, rest in ((0, mine, low_mine), (1, other, low_other)):
            start = pl.multiple_of((core ^ side) * half, half)
            residual[pl.ds(start, half), :] = part[row, 0:half, :].astype(f32) + rest[...].astype(f32)

    correction = jnp.dot(vectors_t[...], weights[...], preferred_element_type=f32)
    span = pl.ds(pl.multiple_of(step * block, block), block)
    updated[span, :] = coeffs[...] + (correction[:, 0:channels] + correction[:, channels:])

    @pl.when(step == pl.num_programs(0) - 1)
    def _():
        def add(numbers):
            codes = [hits[k] for k in numbers]
            changes = [all_rows[pl.ds(code >> 16, 1), :] for code in codes]
            for code, change in zip(codes, changes):
                local = pl.ds(code & 65535, 1)
                updated[local, :] = updated[local, :] + change

        def eight(group, _):
            add([group * 8 + one for one in range(1, 9)])
            return 0

        def single(k, _):
            add([k])
            return 0

        eights = hits[0] >> 3
        lax.fori_loop(0, eights, eight, 0)
        lax.fori_loop(eights * 8 + 1, hits[0] + 1, single, 0)


def finish(hits, scale, vectors_t, coeffs, mine, other, low_mine, low_other):
    count, channels = coeffs.shape
    vectors = scale.shape[0]
    half, members = low_mine.shape[0], mine.shape[0]
    block = 2048
    smem = pl.BlockSpec(memory_space=pltpu.SMEM)
    whole = lambda shape: pl.BlockSpec(shape, lambda i: (0,) * len(shape))
    return pl.pallas_call(
        finish_kernel,
        name="finish",
        grid=(count // block,),
        in_specs=[
            smem,
            whole((vectors, 1)),
            pl.BlockSpec((block, vectors), lambda i: (i, 0)),
            pl.BlockSpec((block, channels), lambda i: (i, 0)),
            whole(mine.shape),
            whole(other.shape),
            whole(low_mine.shape),
            whole(low_other.shape),
        ],
        out_specs=[whole((count, channels)), whole((2 * half, channels))],
        out_shape=[
            jax.ShapeDtypeStruct((count, channels), f32),
            jax.ShapeDtypeStruct((2 * half, channels), f32),
        ],
        scratch_shapes=[
            pltpu.VMEM((2 * members * half, channels), f32),
            pltpu.VMEM((vectors, 2 * channels), bf16),
        ],
        compiler_params=pltpu.CompilerParams(vmem_limit_bytes=VMEM_LIMIT),
        cost_estimate=pl.CostEstimate(flops=10**9, bytes_accessed=14 * 2**20, transcendentals=0),
    )(hits, scale.reshape(vectors, 1), vectors_t, coeffs, mine, other, low_mine, low_other)


def body(centers, coeffs, targets, batch_index, subset_index, eigvec, eigen_scale, *, groups):
    count = centers.shape[0]
    channels = coeffs.shape[1]
    vectors = eigvec.shape[0]
    members = lax.axis_size("batch")
    half = batch_index.shape[0] // 2
    chips = len(groups[0])
    width = centers.shape[1]
    swap = [(i, i ^ 1) for i in range(2 * chips)]

    def across(values):
        return lax.all_to_all(
            values, "centers", 0, 0, tiled=True, axis_index_groups=groups
        )

    turns = [
        lax.ppermute(batch_index, "batch", [(i, (i + k) % members) for i in range(members)])
        for k in range(1, members)
    ]
    mine, other, labels = pick(batch_index, centers, targets)
    summed = mine + lax.ppermute(other, "centers", swap)
    summed, *turns = lax.optimization_barrier((summed, *turns))
    shards = across(summed).reshape(chips, half // chips, width)
    shard = jnp.sum(shards.astype(f32), axis=0).astype(bf16)
    rows_mine = across(jnp.tile(shard, (chips, 1)))
    rows_other = lax.ppermute(rows_mine, "centers", swap)

    vectors_t, hits = prepare(subset_index, [batch_index, *turns], eigvec, count)
    sums_mine, sums_other = main(centers, coeffs, vectors_t, rows_mine, rows_other, labels)

    def widened(values):
        values = values.astype(f32)
        return values[..., 0:channels] + values[..., channels : 2 * channels], values[..., 2 * channels :]

    def packed(residual, rest):
        high, low = split_rounded(residual)
        return jnp.concatenate([high, low, rest.astype(bf16)], axis=-1)

    first = widened(sums_mine)
    second = widened(lax.ppermute(sums_other, "centers", swap))
    chip_sums = packed(first[0] + second[0], first[1] + second[1])
    parts = widened(across(chip_sums).reshape(chips, half // chips, -1))
    shard = packed(jnp.sum(parts[0], axis=0), jnp.sum(parts[1], axis=0))
    gathered = across(jnp.tile(shard, (chips, 1)))
    high = gathered[:, 0:channels]
    low_mine = gathered[:, channels : 2 * channels]
    low_other = lax.ppermute(low_mine, "centers", swap)
    projected = lax.dot_general(
        gathered[:, 2 * channels : 2 * channels + vectors], high, TN, preferred_element_type=f32
    )
    message = jnp.concatenate([high, *split_rounded(projected)], axis=0)
    from_batch = lax.all_to_all(
        jnp.tile(message[None], (members, 1, 1)), "batch", 0, 0, tiled=True
    )
    from_other = lax.ppermute(from_batch, "centers", swap)
    return finish(
        hits, eigen_scale, vectors_t, coeffs, from_batch, from_other, low_mine, low_other
    )


def solution(mesh):
    chips = mesh.shape["centers"] // 2
    groups = [[2 * chip + core for chip in range(chips)] for core in range(2)]
    return jax.shard_map(
        functools.partial(body, groups=groups),
        mesh=mesh,
        in_specs=(
            P("centers", None),
            P("centers", None),
            P("centers", None),
            P("batch"),
            P("centers"),
            P(None, "centers"),
            P(),
        ),
        out_specs=(P("centers", None), P("batch", None)),
        check_vma=False,
    )
```

```python
import functools

import jax
import jax.numpy as jnp
from jax import lax
from jax.experimental import pallas as pl
from jax.experimental.pallas import tpu as pltpu
from jax.sharding import PartitionSpec as P

spread = 1.0
step_size = 0.5
NT = (((1,), (1,)), ((), ()))
TN = (((0,), (0,)), ((), ()))
bf16 = jnp.bfloat16
f32 = jnp.float32
i32 = jnp.int32
VMEM_LIMIT = 56 * 2**20
LOG2_E = 1.4426950408889634


def split_two(values):
    high = values.astype(bf16)
    return high, (values - high.astype(f32)).astype(bf16)


def split_rounded(values):
    high = lax.reduce_precision(values, 8, 7)
    return high.astype(bf16), (values - high).astype(bf16)


def next_hits(index, offset, count):
    rows = index.shape[0]
    total = rows * 128
    lane = lax.broadcasted_iota(i32, (rows, 128), 1)
    sub = lax.broadcasted_iota(i32, (rows, 128), 0)
    local = index - offset
    found = jnp.where((local >= 0) & (local < count), sub * 128 + lane, total)
    shift = 1
    while shift < 128:
        moved = pltpu.roll(found, 128 - shift, 1)
        found = jnp.minimum(found, jnp.where(lane < 128 - shift, moved, total))
        shift *= 2
    later = jnp.broadcast_to(found[:, 0:1], (rows, 128))
    later = jnp.where(sub < rows - 1, pltpu.roll(later, rows - 1, 0), total)
    shift = 1
    while shift < rows:
        moved = pltpu.roll(later, rows - shift, 0)
        later = jnp.minimum(later, jnp.where(sub < rows - shift, moved, total))
        shift *= 2
    return jnp.minimum(found, later)


def following(nxt, pos, total):
    after = jnp.minimum(pos + 1, total - 1)
    return jnp.where(pos + 1 < total, nxt[after >> 7, after & 127], total)


def pick_kernel(
    index_s, index_v, centers, mine, other, nxt_v, nxt, all_centers, wide, rows, sems
):
    total = rows.shape[0]
    half = total // 2
    position = lax.axis_index("centers")
    offset = position * centers.shape[0]
    turn = (position & 1) * half
    load = pltpu.make_async_copy(centers, all_centers, sems.at[0])
    load.start()
    nxt_v[...] = next_hits(index_v[...], offset, centers.shape[0])
    copy = pltpu.make_async_copy(nxt_v, nxt, sems.at[1])
    copy.start()
    rows[...] = jnp.zeros_like(rows)
    copy.wait()
    load.wait()

    def take(pos):
        after = following(nxt, pos, total)
        local = index_s[pos] - offset
        tile = pl.ds(pl.multiple_of((local >> 4) << 4, 16), 16)
        line = pl.ds(local & 15, 1)
        spot = pl.ds(pos ^ turn, 1)
        wide[...] = all_centers[tile, :].astype(f32)
        rows[spot, :] = wide[line, :]
        return after

    lax.while_loop(lambda pos: pos < total, take, nxt[0, 0])
    mine[...] = rows[0:half, :].astype(bf16)
    other[...] = rows[half:total, :].astype(bf16)


def pick(index, centers):
    total, width = index.shape[0], centers.shape[1]
    vmem = pl.BlockSpec(memory_space=pltpu.VMEM)
    smem = pl.BlockSpec(memory_space=pltpu.SMEM)
    hbm = pl.BlockSpec(memory_space=pl.ANY)
    return pl.pallas_call(
        pick_kernel,
        name="pick",
        in_specs=[smem, vmem, hbm],
        out_specs=[vmem, vmem],
        out_shape=[
            jax.ShapeDtypeStruct((total // 2, width), bf16),
            jax.ShapeDtypeStruct((total // 2, width), bf16),
        ],
        scratch_shapes=[
            pltpu.VMEM((total // 128, 128), i32),
            pltpu.SMEM((total // 128, 128), i32),
            pltpu.VMEM(centers.shape, bf16),
            pltpu.VMEM((16, width), f32),
            pltpu.VMEM((total, width), f32),
            pltpu.SemaphoreType.DMA((2,)),
        ],
        compiler_params=pltpu.CompilerParams(vmem_limit_bytes=VMEM_LIMIT),
        cost_estimate=pl.CostEstimate(flops=0, bytes_accessed=14 * 2**20, transcendentals=0),
    )(index, index.reshape(total // 128, 128), centers)


def prepare_kernel(
    subset, index_s, index_v, eigvec, targets, spread_rows, hits, labels,
    wide, all_targets, label_wide, nxt_v, nxt, sems,
):
    step = pl.program_id(0)
    vectors, count = eigvec.shape
    block = spread_rows.shape[0]
    total = index_s.shape[0]
    centers = wide.shape[0]

    @pl.when(step == 0)
    def _():
        position = lax.axis_index("centers")
        offset = position * centers
        turn = (position & 1) * (total // 2)
        load = pltpu.make_async_copy(targets, all_targets, sems.at[0])
        load.start()
        nxt_v[...] = next_hits(index_v[...], offset, centers)
        copy = pltpu.make_async_copy(nxt_v, nxt, sems.at[1])
        copy.start()
        labels[...] = jnp.zeros_like(labels)
        wide[...] = jnp.zeros_like(wide)

        def put(group, _):
            start = pl.multiple_of(group * 128, 128)
            rows = eigvec[:, pl.ds(start, 128)].T
            for eight in range(0, 128, 8):
                spots = [subset[start + eight + one] - offset for one in range(8)]
                for one in range(8):
                    wide[pl.ds(spots[one], 1), 0:vectors] = rows[eight + one : eight + one + 1, :]
            return 0

        lax.fori_loop(0, count // 128, put, 0)
        copy.wait()
        load.wait()

        def note(state):
            number, pos = state
            after = following(nxt, pos, total)
            local = index_s[pos] - offset
            hits[number] = pos * centers + local
            tile = pl.ds(pl.multiple_of((local >> 4) << 4, 16), 16)
            label_wide[...] = all_targets[tile, :].astype(f32)
            labels[pl.ds(pos ^ turn, 1), :] = label_wide[pl.ds(local & 15, 1), :]
            return number + 1, after

        number, _ = lax.while_loop(lambda s: s[1] < total, note, (jnp.int32(1), nxt[0, 0]))
        hits[0] = number - 1

    span = pl.ds(pl.multiple_of(step * block, block), block)
    spread_rows[...] = wide[span, 0:vectors].astype(bf16)


def prepare(subset, index, eigvec, targets):
    vectors, count = eigvec.shape
    centers, channels = targets.shape
    total = index.shape[0]
    block = 2048
    smem = pl.BlockSpec(memory_space=pltpu.SMEM)
    whole = lambda shape: pl.BlockSpec(shape, lambda i: (0, 0))
    lanes = -(-vectors // 128) * 128
    return pl.pallas_call(
        prepare_kernel,
        name="prepare",
        grid=(centers // block,),
        in_specs=[
            smem,
            smem,
            whole((total // 128, 128)),
            whole((vectors, count)),
            pl.BlockSpec(memory_space=pl.ANY),
        ],
        out_specs=[
            pl.BlockSpec((block, vectors), lambda i: (i, 0)),
            smem,
            whole((total, channels)),
        ],
        out_shape=[
            jax.ShapeDtypeStruct((centers, vectors), bf16),
            jax.ShapeDtypeStruct((total + 128,), i32),
            jax.ShapeDtypeStruct((total, channels), f32),
        ],
        scratch_shapes=[
            pltpu.VMEM((centers, lanes), f32),
            pltpu.VMEM(targets.shape, bf16),
            pltpu.VMEM((16, channels), f32),
            pltpu.VMEM((total // 128, 128), i32),
            pltpu.SMEM((total // 128, 128), i32),
            pltpu.SemaphoreType.DMA((2,)),
        ],
        compiler_params=pltpu.CompilerParams(vmem_limit_bytes=VMEM_LIMIT),
        cost_estimate=pl.CostEstimate(flops=0, bytes_accessed=30 * 2**20, transcendentals=0),
    )(subset, index, index.reshape(total // 128, 128), eigvec, targets)


def main_kernel(
    centers, coeffs, vectors_t, rows_mine, rows_other, labels, mine, other, turned, norms, total, *, part
):
    step = pl.program_id(0)
    half = rows_mine.shape[0]
    channels = labels.shape[1]
    vectors = vectors_t.shape[1]

    @pl.when(step == 0)
    def _():
        ones = jnp.ones((8, rows_mine.shape[1]), bf16)
        for start, rows in ((0, rows_mine), (half, rows_other)):
            span = slice(start, start + half)
            values = rows[...]
            high, low = split_two(jnp.square(values.astype(f32)))
            norms[:, span] = (
                lax.dot_general(ones, high, NT, preferred_element_type=f32)
                + lax.dot_general(ones, low, NT, preferred_element_type=f32)
                + 0.001
            )
            turned[:, span] = (values * jnp.asarray(-2.0, bf16)).T
        total[...] = jnp.zeros_like(total)

    spots = list(range(0, centers.shape[0], part))

    def products(start):
        block = centers[start : start + part, :]
        own = jnp.sum(jnp.square(block.astype(f32)), axis=1, keepdims=True)
        return own, jnp.dot(block, turned[...], preferred_element_type=f32)

    ahead = products(spots[0])
    for number, start in enumerate(spots):
        own, prods = ahead
        if number + 1 < len(spots):
            ahead = products(spots[number + 1])
        distance = jnp.maximum(prods + (own + norms[0:1, :]), 0.001)
        kernel = jnp.exp2(distance * lax.rsqrt(distance) * (-LOG2_E / spread)).astype(bf16)
        span = slice(start, start + part)
        columns = jnp.concatenate([coeffs[span, :].astype(bf16), vectors_t[span, :]], axis=1)
        total[...] += lax.dot_general(columns, kernel, TN, preferred_element_type=f32)

    @pl.when(step == pl.num_programs(0) - 1)
    def _():
        for start, out in ((0, mine), (half, other)):
            span = slice(start, start + half)
            partial = total[0:channels, span].T - labels[span, :]
            high, low = split_two(partial)
            out[:, 0:channels] = high
            out[:, channels : 2 * channels] = low
            out[:, 2 * channels :] = jnp.zeros((half, out.shape[1] - 2 * channels), bf16)
            out[:, 2 * channels : 2 * channels + vectors] = total[channels:, span].T.astype(bf16)


def main(centers, coeffs, vectors_t, rows_mine, rows_other, labels):
    count, width = centers.shape
    half, channels = rows_mine.shape[0], labels.shape[1]
    columns = channels + vectors_t.shape[1]
    block, part = 1024, 512
    whole = lambda shape: pl.BlockSpec(shape, lambda i: (0, 0))
    return pl.pallas_call(
        functools.partial(main_kernel, part=part),
        name="kernel_sums",
        grid=(count // block,),
        in_specs=[
            pl.BlockSpec((block, width), lambda i: (i, 0)),
            pl.BlockSpec((block, channels), lambda i: (i, 0)),
            pl.BlockSpec((block, vectors_t.shape[1]), lambda i: (i, 0)),
            whole((half, width)),
            whole((half, width)),
            whole((2 * half, channels)),
        ],
        out_specs=[whole((half, 512)), whole((half, 512))],
        out_shape=[jax.ShapeDtypeStruct((half, 512), bf16)] * 2,
        scratch_shapes=[
            pltpu.VMEM((width, 2 * half), bf16),
            pltpu.VMEM((8, 2 * half), f32),
            pltpu.VMEM((columns, 2 * half), f32),
        ],
        compiler_params=pltpu.CompilerParams(vmem_limit_bytes=VMEM_LIMIT),
        cost_estimate=pl.CostEstimate(
            flops=2 * count * 2 * half * (width + columns),
            bytes_accessed=20 * 2**20,
            transcendentals=2 * count * 2 * half,
        ),
    )(centers, coeffs, vectors_t, rows_mine, rows_other, labels)


def finish_kernel(
    scale, vectors_t, coeffs, mine, other, updated, residual, all_rows, weights, codes_v, codes, sem
):
    step = pl.program_id(0)
    members, channels = mine.shape[0], mine.shape[2]
    half = residual.shape[0] // 2
    vectors = scale.shape[1]
    block = coeffs.shape[0]
    count = updated.shape[0]
    listed = half + 2 * vectors
    lines = codes.shape[0] // members
    copy = pltpu.make_async_copy(codes_v, codes, sem)

    @pl.when(step == 0)
    def _():
        core, row = lax.axis_index("centers") & 1, lax.axis_index("batch")
        first = (
            lax.broadcasted_iota(i32, (lines, 128), 0) + lax.broadcasted_iota(i32, (lines, 128), 1) == 0
        )
        for member in range(members):
            digits = [
                mine[member, listed + k * lines : listed + (k + 1) * lines, :].astype(f32)
                for k in range(3)
            ]
            code = (digits[0] + 256.0 * digits[1] + 65536.0 * digits[2]).astype(i32)
            local = code & (count - 1)
            pos = code >> (count.bit_length() - 1)
            side = (pos >> (half.bit_length() - 1)) ^ core
            source = (side * members + member) * half + (pos & (half - 1))
            codes_v[member * lines : (member + 1) * lines, :] = jnp.where(
                first, code, (source << 16) + local
            )
        copy.start()
        projected = jnp.zeros((vectors, channels), f32)
        for side, part in enumerate((mine, other)):
            for member in range(members):
                start = (side * members + member) * half
                all_rows[start : start + half, :] = part[member, 0:half, :].astype(f32) * -step_size
                projected += part[member, half : half + vectors, :].astype(f32)
                projected += part[member, half + vectors : half + 2 * vectors, :].astype(f32)
        scales = jnp.broadcast_to(scale[...], (channels, vectors)).T
        top, rest = split_two(projected * scales * step_size)
        weights[:, 0:channels] = top
        weights[:, channels:] = rest
        for side, part in enumerate((mine, other)):
            start = pl.multiple_of((core ^ side) * half, half)
            residual[pl.ds(start, half), :] = part[row, 0:half, :].astype(f32)

    correction = jnp.dot(vectors_t[...], weights[...], preferred_element_type=f32)
    span = pl.ds(pl.multiple_of(step * block, block), block)
    updated[span, :] = coeffs[...] + (correction[:, 0:channels] + correction[:, channels:])

    @pl.when(step == pl.num_programs(0) - 1)
    def _():
        copy.wait()
        for member in range(members):
            base = member * lines

            def add(numbers):
                found = [codes[base + (k >> 7), k & 127] for k in numbers]
                changes = [all_rows[pl.ds(code >> 16, 1), :] for code in found]
                for code, change in zip(found, changes):
                    local = pl.ds(code & 65535, 1)
                    updated[local, :] = updated[local, :] + change

            def eight(group, _):
                add([group * 8 + one for one in range(1, 9)])
                return 0

            def single(k, _):
                add([k])
                return 0

            number = codes[base, 0]
            eights = number >> 3
            lax.fori_loop(0, eights, eight, 0)
            lax.fori_loop(eights * 8 + 1, number + 1, single, 0)


def finish(scale, vectors_t, coeffs, mine, other):
    count, channels = coeffs.shape
    vectors = scale.shape[0]
    members = mine.shape[0]
    half = other.shape[1] - 2 * vectors
    lines = (mine.shape[1] - other.shape[1]) // 3
    block = 2048
    whole = lambda shape: pl.BlockSpec(shape, lambda i: (0,) * len(shape))
    return pl.pallas_call(
        finish_kernel,
        name="finish",
        grid=(count // block,),
        in_specs=[
            whole((1, vectors)),
            pl.BlockSpec((block, vectors), lambda i: (i, 0)),
            pl.BlockSpec((block, channels), lambda i: (i, 0)),
            whole(mine.shape),
            whole(other.shape),
        ],
        out_specs=[whole((count, channels)), whole((2 * half, channels))],
        out_shape=[
            jax.ShapeDtypeStruct((count, channels), f32),
            jax.ShapeDtypeStruct((2 * half, channels), f32),
        ],
        scratch_shapes=[
            pltpu.VMEM((2 * members * half, channels), f32),
            pltpu.VMEM((vectors, 2 * channels), bf16),
            pltpu.VMEM((members * lines, 128), i32),
            pltpu.SMEM((members * lines, 128), i32),
            pltpu.SemaphoreType.DMA,
        ],
        compiler_params=pltpu.CompilerParams(vmem_limit_bytes=VMEM_LIMIT),
        cost_estimate=pl.CostEstimate(flops=10**9, bytes_accessed=14 * 2**20, transcendentals=0),
    )(scale.reshape(1, vectors), vectors_t, coeffs, mine, other)


def body(centers, coeffs, targets, batch_index, subset_index, eigvec, eigen_scale, *, groups):
    count = centers.shape[0]
    channels = coeffs.shape[1]
    vectors = eigvec.shape[0]
    members = lax.axis_size("batch")
    half = batch_index.shape[0] // 2
    chips = len(groups[0])
    width = centers.shape[1]
    swap = [(i, i ^ 1) for i in range(2 * chips)]

    def across(values):
        return lax.all_to_all(
            values, "centers", 0, 0, tiled=True, axis_index_groups=groups
        )

    mine, other = pick(batch_index, centers)
    summed = mine + lax.ppermute(other, "centers", swap)
    shards = across(summed).reshape(chips, half // chips, width)
    shard = jnp.sum(shards.astype(f32), axis=0).astype(bf16)
    rows_mine = across(jnp.tile(shard, (chips, 1)))
    rows_other = lax.ppermute(rows_mine, "centers", swap)

    vectors_t, hits, labels = prepare(subset_index, batch_index, eigvec, targets)
    sums_mine, sums_other = main(centers, coeffs, vectors_t, rows_mine, rows_other, labels)

    def widened(values):
        values = values.astype(f32)
        return values[..., 0:channels] + values[..., channels : 2 * channels], values[..., 2 * channels :]

    def packed(residual, rest):
        high, low = split_rounded(residual)
        return jnp.concatenate([high, low, rest.astype(bf16)], axis=-1)

    first = widened(sums_mine)
    second = widened(lax.ppermute(sums_other, "centers", swap))
    chip_sums = packed(first[0] + second[0], first[1] + second[1])
    parts = widened(across(chip_sums).reshape(chips, half // chips, -1))
    shard = jnp.concatenate(
        [jnp.sum(parts[0], axis=0).astype(bf16), jnp.sum(parts[1], axis=0).astype(bf16)], axis=1
    )
    gathered = across(jnp.tile(shard, (chips, 1)))
    high = gathered[:, 0:channels]
    projected = lax.dot_general(
        gathered[:, channels : channels + vectors], high, TN, preferred_element_type=f32
    )
    lines = jnp.zeros((16 * 128,), i32).at[0 : hits.shape[0]].set(hits).reshape(16, 128)
    digits = [((lines >> (8 * k)) & 255).astype(bf16) for k in range(3)]
    message = jnp.concatenate([high, *split_rounded(projected), *digits], axis=0)
    from_batch = lax.all_to_all(
        jnp.tile(message[None], (members, 1, 1)), "batch", 0, 0, tiled=True
    )
    from_other = lax.ppermute(from_batch[:, 0 : half + 2 * vectors], "centers", swap)
    return finish(eigen_scale, vectors_t, coeffs, from_batch, from_other)


def solution(mesh):
    chips = mesh.shape["centers"] // 2
    groups = [[2 * chip + core for chip in range(chips)] for core in range(2)]
    return jax.shard_map(
        functools.partial(body, groups=groups),
        mesh=mesh,
        in_specs=(
            P("centers", None),
            P("centers", None),
            P("centers", None),
            P("batch"),
            P("centers"),
            P(None, "centers"),
            P(),
        ),
        out_specs=(P("centers", None), P("batch", None)),
        check_vma=False,
    )
```

```python
import functools

import jax
import jax.numpy as jnp
from jax import lax
from jax.experimental import pallas as pl
from jax.experimental.pallas import tpu as pltpu
from jax.sharding import PartitionSpec as P

spread = 1.0
step_size = 0.5
NT = (((1,), (1,)), ((), ()))
TN = (((0,), (0,)), ((), ()))
bf16 = jnp.bfloat16
f32 = jnp.float32
i32 = jnp.int32
LINES = 16
LOG2_E = 1.4426950408889634


def split_two(values):
    high = values.astype(bf16)
    return high, (values - high.astype(f32)).astype(bf16)


def split_rounded(values):
    high = lax.reduce_precision(values, 8, 7)
    return high.astype(bf16), (values - high).astype(bf16)


def next_hits(index, offset, count):
    rows = index.shape[0]
    total = rows * 128
    lane = lax.broadcasted_iota(i32, (rows, 128), 1)
    sub = lax.broadcasted_iota(i32, (rows, 128), 0)
    local = index - offset
    found = jnp.where((local >= 0) & (local < count), sub * 128 + lane, total)
    shift = 1
    while shift < 128:
        moved = pltpu.roll(found, 128 - shift, 1)
        found = jnp.minimum(found, jnp.where(lane < 128 - shift, moved, total))
        shift *= 2
    later = jnp.broadcast_to(found[:, 0:1], (rows, 128))
    later = jnp.where(sub < rows - 1, pltpu.roll(later, rows - 1, 0), total)
    shift = 1
    while shift < rows:
        moved = pltpu.roll(later, rows - shift, 0)
        later = jnp.minimum(later, jnp.where(sub < rows - shift, moved, total))
        shift *= 2
    return jnp.minimum(found, later)


def following(nxt, pos, total):
    after = jnp.minimum(pos + 1, total - 1)
    return jnp.where(pos + 1 < total, nxt[after >> 7, after & 127], total)


def pick_kernel(
    index_s, index_v, centers, mine, other, nxt_v, nxt, all_centers, wide, rows, sems
):
    total = rows.shape[0]
    half = total // 2
    position = lax.axis_index("centers")
    offset = position * centers.shape[0]
    turn = (position & 1) * half
    load = pltpu.make_async_copy(centers, all_centers, sems.at[0])
    load.start()
    nxt_v[...] = next_hits(index_v[...], offset, centers.shape[0])
    copy = pltpu.make_async_copy(nxt_v, nxt, sems.at[1])
    copy.start()
    rows[...] = jnp.zeros_like(rows)
    copy.wait()
    load.wait()

    def take(pos):
        after = following(nxt, pos, total)
        local = index_s[pos] - offset
        tile = pl.ds(pl.multiple_of((local >> 4) << 4, 16), 16)
        line = pl.ds(local & 15, 1)
        spot = pl.ds(pos ^ turn, 1)
        wide[...] = all_centers[tile, :].astype(f32)
        rows[spot, :] = wide[line, :]
        return after

    lax.while_loop(lambda pos: pos < total, take, nxt[0, 0])
    mine[...] = rows[0:half, :].astype(bf16)
    other[...] = rows[half:total, :].astype(bf16)


def pick(index, centers):
    total, width = index.shape[0], centers.shape[1]
    vmem = pl.BlockSpec(memory_space=pltpu.VMEM)
    smem = pl.BlockSpec(memory_space=pltpu.SMEM)
    hbm = pl.BlockSpec(memory_space=pl.ANY)
    return pl.pallas_call(
        pick_kernel,
        name="pick",
        in_specs=[smem, vmem, hbm],
        out_specs=[vmem, vmem],
        out_shape=[
            jax.ShapeDtypeStruct((total // 2, width), bf16),
            jax.ShapeDtypeStruct((total // 2, width), bf16),
        ],
        scratch_shapes=[
            pltpu.VMEM((total // 128, 128), i32),
            pltpu.SMEM((total // 128, 128), i32),
            pltpu.VMEM(centers.shape, bf16),
            pltpu.VMEM((16, width), f32),
            pltpu.VMEM((total, width), f32),
            pltpu.SemaphoreType.DMA((2,)),
        ],
        compiler_params=pltpu.CompilerParams(vmem_limit_bytes=56 * 2**20),
        cost_estimate=pl.CostEstimate(flops=0, bytes_accessed=14 * 2**20, transcendentals=0),
    )(index, index.reshape(total // 128, 128), centers)


def prepare_kernel(
    subset, index_s, index_v, eigvec, targets, spread_rows, hits, labels,
    wide, all_targets, label_wide, nxt_v, nxt, sems,
):
    step = pl.program_id(0)
    vectors, count = eigvec.shape
    block = spread_rows.shape[0]
    total = index_s.shape[0]
    centers = wide.shape[0]

    @pl.when(step == 0)
    def _():
        position = lax.axis_index("centers")
        offset = position * centers
        turn = (position & 1) * (total // 2)
        load = pltpu.make_async_copy(targets, all_targets, sems.at[0])
        load.start()
        nxt_v[...] = next_hits(index_v[...], offset, centers)
        copy = pltpu.make_async_copy(nxt_v, nxt, sems.at[1])
        copy.start()
        labels[...] = jnp.zeros_like(labels)
        wide[...] = jnp.zeros_like(wide)

        def put(group, _):
            start = pl.multiple_of(group * 128, 128)
            rows = eigvec[:, pl.ds(start, 128)].T
            for eight in range(0, 128, 8):
                spots = [subset[start + eight + one] - offset for one in range(8)]
                for one in range(8):
                    wide[pl.ds(spots[one], 1), 0:vectors] = rows[eight + one : eight + one + 1, :]
            return 0

        lax.fori_loop(0, count // 128, put, 0)
        copy.wait()
        load.wait()

        def note(state):
            number, pos = state
            after = following(nxt, pos, total)
            local = index_s[pos] - offset
            hits[number] = pos * centers + local
            tile = pl.ds(pl.multiple_of((local >> 4) << 4, 16), 16)
            label_wide[...] = all_targets[tile, :].astype(f32)
            labels[pl.ds(pos ^ turn, 1), :] = label_wide[pl.ds(local & 15, 1), :]
            return number + 1, after

        number, _ = lax.while_loop(lambda s: s[1] < total, note, (jnp.int32(1), nxt[0, 0]))
        hits[0] = number - 1

    span = pl.ds(pl.multiple_of(step * block, block), block)
    spread_rows[...] = wide[span, 0:vectors].astype(bf16)


def prepare(subset, index, eigvec, targets):
    vectors, count = eigvec.shape
    centers, channels = targets.shape
    total = index.shape[0]
    block = 2048
    smem = pl.BlockSpec(memory_space=pltpu.SMEM)
    whole = lambda shape: pl.BlockSpec(shape, lambda i: (0, 0))
    lanes = -(-vectors // 128) * 128
    return pl.pallas_call(
        prepare_kernel,
        name="prepare",
        grid=(centers // block,),
        in_specs=[
            smem,
            smem,
            whole((total // 128, 128)),
            whole((vectors, count)),
            pl.BlockSpec(memory_space=pl.ANY),
        ],
        out_specs=[
            pl.BlockSpec((block, vectors), lambda i: (i, 0)),
            smem,
            whole((total, channels)),
        ],
        out_shape=[
            jax.ShapeDtypeStruct((centers, vectors), bf16),
            jax.ShapeDtypeStruct((total + 128,), i32),
            jax.ShapeDtypeStruct((total, channels), f32),
        ],
        scratch_shapes=[
            pltpu.VMEM((centers, lanes), f32),
            pltpu.VMEM(targets.shape, bf16),
            pltpu.VMEM((16, channels), f32),
            pltpu.VMEM((total // 128, 128), i32),
            pltpu.SMEM((total // 128, 128), i32),
            pltpu.SemaphoreType.DMA((2,)),
        ],
        compiler_params=pltpu.CompilerParams(vmem_limit_bytes=20 * 2**20),
        cost_estimate=pl.CostEstimate(flops=0, bytes_accessed=30 * 2**20, transcendentals=0),
    )(subset, index, index.reshape(total // 128, 128), eigvec, targets)


def main_kernel(
    centers, coeffs, vectors_t, rows_mine, rows_other, labels, mine, other, turned, norms, total, *, part
):
    step = pl.program_id(0)
    half = rows_mine.shape[0]
    channels = labels.shape[1]
    vectors = vectors_t.shape[1]

    @pl.when(step == 0)
    def _():
        ones = jnp.ones((8, rows_mine.shape[1]), bf16)
        for start, rows in ((0, rows_mine), (half, rows_other)):
            span = slice(start, start + half)
            values = rows[...]
            high, low = split_two(jnp.square(values.astype(f32)))
            norms[:, span] = (
                lax.dot_general(ones, high, NT, preferred_element_type=f32)
                + lax.dot_general(ones, low, NT, preferred_element_type=f32)
                + 0.001
            )
            turned[:, span] = (values * jnp.asarray(-2.0, bf16)).T
        total[...] = jnp.zeros_like(total)

    spots = list(range(0, centers.shape[0], part))

    def products(start):
        block = centers[start : start + part, :]
        own = jnp.sum(jnp.square(block.astype(f32)), axis=1, keepdims=True)
        return own, jnp.dot(block, turned[...], preferred_element_type=f32)

    ahead = products(spots[0])
    for number, start in enumerate(spots):
        own, prods = ahead
        if number + 1 < len(spots):
            ahead = products(spots[number + 1])
        distance = jnp.maximum(prods + (own + norms[0:1, :]), 0.001)
        kernel = jnp.exp2(distance * lax.rsqrt(distance) * (-LOG2_E / spread)).astype(bf16)
        span = slice(start, start + part)
        columns = jnp.concatenate([coeffs[span, :].astype(bf16), vectors_t[span, :]], axis=1)
        total[...] += lax.dot_general(columns, kernel, TN, preferred_element_type=f32)

    @pl.when(step == pl.num_programs(0) - 1)
    def _():
        for start, out in ((0, mine), (half, other)):
            span = slice(start, start + half)
            partial = total[0:channels, span].T - labels[span, :]
            high, low = split_two(partial)
            out[:, 0:channels] = high
            out[:, channels : 2 * channels] = low
            out[:, 2 * channels :] = jnp.zeros((half, out.shape[1] - 2 * channels), bf16)
            out[:, 2 * channels : 2 * channels + vectors] = total[channels:, span].T.astype(bf16)


def main(centers, coeffs, vectors_t, rows_mine, rows_other, labels):
    count, width = centers.shape
    half, channels = rows_mine.shape[0], labels.shape[1]
    columns = channels + vectors_t.shape[1]
    block, part = 1024, 512
    whole = lambda shape: pl.BlockSpec(shape, lambda i: (0, 0))
    return pl.pallas_call(
        functools.partial(main_kernel, part=part),
        name="kernel_sums",
        grid=(count // block,),
        in_specs=[
            pl.BlockSpec((block, width), lambda i: (i, 0)),
            pl.BlockSpec((block, channels), lambda i: (i, 0)),
            pl.BlockSpec((block, vectors_t.shape[1]), lambda i: (i, 0)),
            whole((half, width)),
            whole((half, width)),
            whole((2 * half, channels)),
        ],
        out_specs=[whole((half, 512)), whole((half, 512))],
        out_shape=[jax.ShapeDtypeStruct((half, 512), bf16)] * 2,
        scratch_shapes=[
            pltpu.VMEM((width, 2 * half), bf16),
            pltpu.VMEM((8, 2 * half), f32),
            pltpu.VMEM((columns, 2 * half), f32),
        ],
        compiler_params=pltpu.CompilerParams(vmem_limit_bytes=28 * 2**20),
        cost_estimate=pl.CostEstimate(
            flops=2 * count * 2 * half * (width + columns),
            bytes_accessed=20 * 2**20,
            transcendentals=2 * count * 2 * half,
        ),
    )(centers, coeffs, vectors_t, rows_mine, rows_other, labels)


def finish_kernel(scale, vectors_t, coeffs, *refs, members):
    mine, other, refs = refs[:members], refs[members : 2 * members], refs[2 * members :]
    updated, residual, all_rows, weights, codes_v, codes, sem = refs
    step = pl.program_id(0)
    channels = coeffs.shape[1]
    half = residual.shape[0] // 2
    vectors = scale.shape[1]
    block = coeffs.shape[0]
    count = updated.shape[0]
    listed = half + 2 * vectors
    lines = codes.shape[0] // members
    copy = pltpu.make_async_copy(codes_v, codes, sem)

    @pl.when(step == 0)
    def _():
        core = lax.axis_index("centers") & 1
        first = (
            lax.broadcasted_iota(i32, (lines, 128), 0) + lax.broadcasted_iota(i32, (lines, 128), 1) == 0
        )
        for member in range(members):
            digits = [
                mine[member][listed + k * lines : listed + (k + 1) * lines, :].astype(f32)
                for k in range(3)
            ]
            code = (digits[0] + 256.0 * digits[1] + 65536.0 * digits[2]).astype(i32)
            local = code & (count - 1)
            pos = code >> (count.bit_length() - 1)
            side = (pos >> (half.bit_length() - 1)) ^ core
            source = (side * members + member) * half + (pos & (half - 1))
            codes_v[member * lines : (member + 1) * lines, :] = jnp.where(
                first, code, (source << 16) + local
            )
        copy.start()
        projected = jnp.zeros((vectors, channels), f32)
        for side, part in enumerate((mine, other)):
            for member in range(members):
                start = (side * members + member) * half
                all_rows[start : start + half, :] = part[member][0:half, :].astype(f32) * -step_size
                projected += part[member][half : half + vectors, :].astype(f32)
                projected += part[member][half + vectors : half + 2 * vectors, :].astype(f32)
        scales = jnp.broadcast_to(scale[...], (channels, vectors)).T
        top, rest = split_two(projected * scales * step_size)
        weights[:, 0:channels] = top
        weights[:, channels:] = rest
        for side, part in enumerate((mine, other)):
            start = pl.multiple_of((core ^ side) * half, half)
            residual[pl.ds(start, half), :] = part[0][0:half, :].astype(f32)

    correction = jnp.dot(vectors_t[...], weights[...], preferred_element_type=f32)
    span = pl.ds(pl.multiple_of(step * block, block), block)
    updated[span, :] = coeffs[...] + (correction[:, 0:channels] + correction[:, channels:])

    @pl.when(step == pl.num_programs(0) - 1)
    def _():
        copy.wait()
        for member in range(members):
            base = member * lines

            def add(numbers):
                found = [codes[base + (k >> 7), k & 127] for k in numbers]
                changes = [all_rows[pl.ds(code >> 16, 1), :] for code in found]
                for code, change in zip(found, changes):
                    local = pl.ds(code & 65535, 1)
                    updated[local, :] = updated[local, :] + change

            def eight(group, _):
                add([group * 8 + one for one in range(1, 9)])
                return 0

            def single(k, _):
                add([k])
                return 0

            number = codes[base, 0]
            eights = number >> 3
            lax.fori_loop(0, eights, eight, 0)
            lax.fori_loop(eights * 8 + 1, number + 1, single, 0)


def finish(scale, vectors_t, coeffs, mine, other):
    count, channels = coeffs.shape
    vectors = scale.shape[0]
    members = len(mine)
    lines = LINES
    half = mine[0].shape[0] - 2 * vectors - 3 * lines
    block = 2048
    whole = lambda shape: pl.BlockSpec(shape, lambda i: (0,) * len(shape))
    return pl.pallas_call(
        functools.partial(finish_kernel, members=members),
        name="finish",
        grid=(count // block,),
        in_specs=[
            whole((1, vectors)),
            pl.BlockSpec((block, vectors), lambda i: (i, 0)),
            pl.BlockSpec((block, channels), lambda i: (i, 0)),
        ]
        + [whole(one.shape) for one in (*mine, *other)],
        out_specs=[whole((count, channels)), whole((2 * half, channels))],
        out_shape=[
            jax.ShapeDtypeStruct((count, channels), f32),
            jax.ShapeDtypeStruct((2 * half, channels), f32),
        ],
        scratch_shapes=[
            pltpu.VMEM((2 * members * half, channels), f32),
            pltpu.VMEM((vectors, 2 * channels), bf16),
            pltpu.VMEM((members * lines, 128), i32),
            pltpu.SMEM((members * lines, 128), i32),
            pltpu.SemaphoreType.DMA,
        ],
        compiler_params=pltpu.CompilerParams(vmem_limit_bytes=24 * 2**20),
        cost_estimate=pl.CostEstimate(flops=10**9, bytes_accessed=14 * 2**20, transcendentals=0),
    )(scale.reshape(1, vectors), vectors_t, coeffs, *mine, *other)


def body(centers, coeffs, targets, batch_index, subset_index, eigvec, eigen_scale, *, groups):
    count = centers.shape[0]
    channels = coeffs.shape[1]
    vectors = eigvec.shape[0]
    members = lax.axis_size("batch")
    half = batch_index.shape[0] // 2
    chips = len(groups[0])
    width = centers.shape[1]
    swap = [(i, i ^ 1) for i in range(2 * chips)]

    def across(values):
        return lax.all_to_all(
            values, "centers", 0, 0, tiled=True, axis_index_groups=groups
        )

    mine, other = pick(batch_index, centers)
    summed = mine + lax.ppermute(other, "centers", swap)
    shards = across(summed).reshape(chips, half // chips, width)
    shard = jnp.sum(shards.astype(f32), axis=0).astype(bf16)
    rows_mine = across(jnp.tile(shard, (chips, 1)))
    rows_other = lax.ppermute(rows_mine, "centers", swap)

    vectors_t, hits, labels = prepare(subset_index, batch_index, eigvec, targets)
    sums_mine, sums_other = main(centers, coeffs, vectors_t, rows_mine, rows_other, labels)

    def widened(values):
        values = values.astype(f32)
        return values[..., 0:channels] + values[..., channels : 2 * channels], values[..., 2 * channels :]

    def packed(residual, rest):
        high, low = split_rounded(residual)
        return jnp.concatenate([high, low, rest.astype(bf16)], axis=-1)

    first = widened(sums_mine)
    second = widened(lax.ppermute(sums_other, "centers", swap))
    chip_sums = packed(first[0] + second[0], first[1] + second[1])
    parts = widened(across(chip_sums).reshape(chips, half // chips, -1))
    shard = jnp.concatenate(
        [jnp.sum(parts[0], axis=0).astype(bf16), jnp.sum(parts[1], axis=0).astype(bf16)], axis=1
    )
    gathered = across(jnp.tile(shard, (chips, 1)))
    high = gathered[:, 0:channels]
    projected = lax.dot_general(
        gathered[:, channels : channels + vectors], high, TN, preferred_element_type=f32
    )
    lines = jnp.zeros((LINES * 128,), i32).at[0 : hits.shape[0]].set(hits).reshape(LINES, 128)
    digits = [((lines >> (8 * k)) & 255).astype(bf16) for k in range(3)]
    message = jnp.concatenate([high, *split_rounded(projected), *digits], axis=0)
    from_batch = [message] + [
        lax.ppermute(message, "batch", [(i, (i + k) % members) for i in range(members)])
        for k in range(1, members)
    ]
    from_other = [lax.ppermute(one, "centers", swap) for one in from_batch]
    return finish(eigen_scale, vectors_t, coeffs, from_batch, from_other)


def solution(mesh):
    chips = mesh.shape["centers"] // 2
    groups = [[2 * chip + core for chip in range(chips)] for core in range(2)]
    return jax.shard_map(
        functools.partial(body, groups=groups),
        mesh=mesh,
        in_specs=(
            P("centers", None),
            P("centers", None),
            P("centers", None),
            P("batch"),
            P("centers"),
            P(None, "centers"),
            P(),
        ),
        out_specs=(P("centers", None), P("batch", None)),
        check_vma=False,
    )
```

```python
import functools

import jax
import jax.numpy as jnp
from jax import lax
from jax.experimental import pallas as pl
from jax.experimental.pallas import tpu as pltpu
from jax.sharding import PartitionSpec as P

spread = 1.0
step_size = 0.5
NT = (((1,), (1,)), ((), ()))
TN = (((0,), (0,)), ((), ()))
bf16 = jnp.bfloat16
f32 = jnp.float32
i32 = jnp.int32
LINES = 16
LOG2_E = 1.4426950408889634


def split_two(values):
    high = values.astype(bf16)
    return high, (values - high.astype(f32)).astype(bf16)


def split_rounded(values):
    high = lax.reduce_precision(values, 8, 7)
    return high.astype(bf16), (values - high).astype(bf16)


def total_of(parts):
    return functools.reduce(jnp.add, [parts[k] for k in range(parts.shape[0])])


def next_hits(index, offset, count):
    rows = index.shape[0]
    total = rows * 128
    lane = lax.broadcasted_iota(i32, (rows, 128), 1)
    sub = lax.broadcasted_iota(i32, (rows, 128), 0)
    local = index - offset
    found = jnp.where((local >= 0) & (local < count), sub * 128 + lane, total)
    shift = 1
    while shift < 128:
        moved = pltpu.roll(found, 128 - shift, 1)
        found = jnp.minimum(found, jnp.where(lane < 128 - shift, moved, total))
        shift *= 2
    later = jnp.broadcast_to(found[:, 0:1], (rows, 128))
    later = jnp.where(sub < rows - 1, pltpu.roll(later, rows - 1, 0), total)
    shift = 1
    while shift < rows:
        moved = pltpu.roll(later, rows - shift, 0)
        later = jnp.minimum(later, jnp.where(sub < rows - shift, moved, total))
        shift *= 2
    return jnp.minimum(found, later)


def following(nxt, pos, total):
    after = jnp.minimum(pos + 1, total - 1)
    return jnp.where(pos + 1 < total, nxt[after >> 7, after & 127], total)


def pick_kernel(
    index_s, index_v, centers, mine, other, nxt_v, nxt, all_centers, wide, rows, sems
):
    total = rows.shape[0]
    half = total // 2
    position = lax.axis_index("centers")
    offset = position * centers.shape[0]
    turn = (position & 1) * half
    load = pltpu.make_async_copy(centers, all_centers, sems.at[0])
    load.start()
    nxt_v[...] = next_hits(index_v[...], offset, centers.shape[0])
    copy = pltpu.make_async_copy(nxt_v, nxt, sems.at[1])
    copy.start()
    rows[...] = jnp.zeros_like(rows)
    copy.wait()
    load.wait()

    def take(pos):
        after = following(nxt, pos, total)
        local = index_s[pos] - offset
        tile = pl.ds(pl.multiple_of((local >> 4) << 4, 16), 16)
        line = pl.ds(local & 15, 1)
        spot = pl.ds(pos ^ turn, 1)
        wide[...] = all_centers[tile, :].astype(f32)
        rows[spot, :] = wide[line, :]
        return after

    lax.while_loop(lambda pos: pos < total, take, nxt[0, 0])
    mine[...] = rows[0:half, :].astype(bf16)
    other[...] = rows[half:total, :].astype(bf16)


def pick(index, centers):
    total, width = index.shape[0], centers.shape[1]
    vmem = pl.BlockSpec(memory_space=pltpu.VMEM)
    smem = pl.BlockSpec(memory_space=pltpu.SMEM)
    hbm = pl.BlockSpec(memory_space=pltpu.HBM)
    return pl.pallas_call(
        pick_kernel,
        name="pick",
        in_specs=[smem, vmem, hbm],
        out_specs=[vmem, vmem],
        out_shape=[
            jax.ShapeDtypeStruct((total // 2, width), bf16),
            jax.ShapeDtypeStruct((total // 2, width), bf16),
        ],
        scratch_shapes=[
            pltpu.VMEM((total // 128, 128), i32),
            pltpu.SMEM((total // 128, 128), i32),
            pltpu.VMEM(centers.shape, bf16),
            pltpu.VMEM((16, width), f32),
            pltpu.VMEM((total, width), f32),
            pltpu.SemaphoreType.DMA((2,)),
        ],
        compiler_params=pltpu.CompilerParams(vmem_limit_bytes=56 * 2**20),
        cost_estimate=pl.CostEstimate(flops=0, bytes_accessed=14 * 2**20, transcendentals=0),
    )(index, index.reshape(total // 128, 128), centers)


def prepare_kernel(
    subset, index_s, index_v, eigvec, targets, spread_rows, hits, labels,
    wide, all_targets, label_wide, nxt_v, nxt, sems,
):
    step = pl.program_id(0)
    vectors, count = eigvec.shape
    block = spread_rows.shape[0]
    total = index_s.shape[0]
    centers = wide.shape[0]

    @pl.when(step == 0)
    def _():
        position = lax.axis_index("centers")
        offset = position * centers
        turn = (position & 1) * (total // 2)
        load = pltpu.make_async_copy(targets, all_targets, sems.at[0])
        load.start()
        nxt_v[...] = next_hits(index_v[...], offset, centers)
        copy = pltpu.make_async_copy(nxt_v, nxt, sems.at[1])
        copy.start()
        labels[...] = jnp.zeros_like(labels)
        wide[...] = jnp.zeros_like(wide)

        def put(group, _):
            start = pl.multiple_of(group * 128, 128)
            rows = eigvec[:, pl.ds(start, 128)].T
            for eight in range(0, 128, 8):
                spots = [subset[start + eight + one] - offset for one in range(8)]
                for one in range(8):
                    wide[pl.ds(spots[one], 1), 0:vectors] = rows[eight + one : eight + one + 1, :]
            return 0

        lax.fori_loop(0, count // 128, put, 0)
        copy.wait()
        load.wait()

        def note(state):
            number, pos = state
            after = following(nxt, pos, total)
            local = index_s[pos] - offset
            hits[number] = pos * centers + local
            tile = pl.ds(pl.multiple_of((local >> 4) << 4, 16), 16)
            label_wide[...] = all_targets[tile, :].astype(f32)
            labels[pl.ds(pos ^ turn, 1), :] = label_wide[pl.ds(local & 15, 1), :]
            return number + 1, after

        number, _ = lax.while_loop(lambda s: s[1] < total, note, (jnp.int32(1), nxt[0, 0]))
        hits[0] = number - 1

    span = pl.ds(pl.multiple_of(step * block, block), block)
    spread_rows[...] = wide[span, 0:vectors].astype(bf16)


def prepare(subset, index, eigvec, targets):
    vectors, count = eigvec.shape
    centers, channels = targets.shape
    total = index.shape[0]
    block = 2048
    smem = pl.BlockSpec(memory_space=pltpu.SMEM)
    whole = lambda shape: pl.BlockSpec(shape, lambda i: (0, 0))
    lanes = -(-vectors // 128) * 128
    return pl.pallas_call(
        prepare_kernel,
        name="prepare",
        grid=(centers // block,),
        in_specs=[
            smem,
            smem,
            whole((total // 128, 128)),
            whole((vectors, count)),
            pl.BlockSpec(memory_space=pl.ANY),
        ],
        out_specs=[
            pl.BlockSpec((block, vectors), lambda i: (i, 0)),
            smem,
            whole((total, channels)),
        ],
        out_shape=[
            jax.ShapeDtypeStruct((centers, vectors), bf16),
            jax.ShapeDtypeStruct((total + 128,), i32),
            jax.ShapeDtypeStruct((total, channels), f32),
        ],
        scratch_shapes=[
            pltpu.VMEM((centers, lanes), f32),
            pltpu.VMEM(targets.shape, bf16),
            pltpu.VMEM((16, channels), f32),
            pltpu.VMEM((total // 128, 128), i32),
            pltpu.SMEM((total // 128, 128), i32),
            pltpu.SemaphoreType.DMA((2,)),
        ],
        compiler_params=pltpu.CompilerParams(vmem_limit_bytes=20 * 2**20),
        cost_estimate=pl.CostEstimate(flops=0, bytes_accessed=30 * 2**20, transcendentals=0),
    )(subset, index, index.reshape(total // 128, 128), eigvec, targets)


def main_kernel(
    all_centers, coeffs, vectors_t, rows_mine, rows_other, labels, mine, other,
    turned, norms, total, blocks, sems, *, part,
):
    step = pl.program_id(0)
    block = blocks.shape[1]
    slot = step & 1

    def load(step, slot):
        span = pl.ds(pl.multiple_of(step * block, block), block)
        return pltpu.make_async_copy(all_centers.at[span, :], blocks.at[slot], sems.at[slot])

    @pl.when(step == 0)
    def _():
        load(step, slot).start()

    @pl.when(step + 1 < pl.num_programs(0))
    def _():
        load(step + 1, 1 - slot).start()

    half = rows_mine.shape[0]
    channels = labels.shape[1]
    vectors = vectors_t.shape[1]

    @pl.when(step == 0)
    def _():
        ones = jnp.ones((8, rows_mine.shape[1]), bf16)
        for start, rows in ((0, rows_mine), (half, rows_other)):
            span = slice(start, start + half)
            values = rows[...]
            high, low = split_two(jnp.square(values.astype(f32)))
            norms[:, span] = (
                lax.dot_general(ones, high, NT, preferred_element_type=f32)
                + lax.dot_general(ones, low, NT, preferred_element_type=f32)
                + 0.001
            )
            turned[:, span] = (values * jnp.asarray(-2.0, bf16)).T
        total[...] = jnp.zeros_like(total)

    load(step, slot).wait()
    centers = blocks.at[slot]
    spots = list(range(0, block, part))

    def products(start):
        block = centers[start : start + part, :]
        own = jnp.sum(jnp.square(block.astype(f32)), axis=1, keepdims=True)
        return own, jnp.dot(block, turned[...], preferred_element_type=f32)

    ahead = products(spots[0])
    for number, start in enumerate(spots):
        own, prods = ahead
        if number + 1 < len(spots):
            ahead = products(spots[number + 1])
        distance = jnp.maximum(prods + (own + norms[0:1, :]), 0.001)
        kernel = jnp.exp2(distance * lax.rsqrt(distance) * (-LOG2_E / spread)).astype(bf16)
        span = slice(start, start + part)
        columns = jnp.concatenate([coeffs[span, :].astype(bf16), vectors_t[span, :]], axis=1)
        total[...] += lax.dot_general(columns, kernel, TN, preferred_element_type=f32)

    @pl.when(step == pl.num_programs(0) - 1)
    def _():
        for start, out in ((0, mine), (half, other)):
            span = slice(start, start + half)
            partial = total[0:channels, span].T - labels[span, :]
            high, low = split_two(partial)
            out[:, 0:channels] = high
            out[:, channels : 2 * channels] = low
            out[:, 2 * channels :] = jnp.zeros((half, out.shape[1] - 2 * channels), bf16)
            out[:, 2 * channels : 2 * channels + vectors] = total[channels:, span].T.astype(bf16)


def main(centers, coeffs, vectors_t, rows_mine, rows_other, labels):
    count, width = centers.shape
    half, channels = rows_mine.shape[0], labels.shape[1]
    columns = channels + vectors_t.shape[1]
    block, part = 1024, 512
    whole = lambda shape: pl.BlockSpec(shape, lambda i: (0, 0))
    return pl.pallas_call(
        functools.partial(main_kernel, part=part),
        name="kernel_sums",
        grid=(count // block,),
        in_specs=[
            pl.BlockSpec(memory_space=pltpu.HBM),
            pl.BlockSpec((block, channels), lambda i: (i, 0)),
            pl.BlockSpec((block, vectors_t.shape[1]), lambda i: (i, 0)),
            whole((half, width)),
            whole((half, width)),
            whole((2 * half, channels)),
        ],
        out_specs=[whole((half, 512)), whole((half, 512))],
        out_shape=[jax.ShapeDtypeStruct((half, 512), bf16)] * 2,
        scratch_shapes=[
            pltpu.VMEM((width, 2 * half), bf16),
            pltpu.VMEM((8, 2 * half), f32),
            pltpu.VMEM((columns, 2 * half), f32),
            pltpu.VMEM((2, block, width), bf16),
            pltpu.SemaphoreType.DMA((2,)),
        ],
        compiler_params=pltpu.CompilerParams(vmem_limit_bytes=28 * 2**20),
        cost_estimate=pl.CostEstimate(
            flops=2 * count * 2 * half * (width + columns),
            bytes_accessed=20 * 2**20,
            transcendentals=2 * count * 2 * half,
        ),
    )(centers, coeffs, vectors_t, rows_mine, rows_other, labels)


def finish_kernel(scale, vectors_t, coeffs, *refs, members):
    mine, other, refs = refs[:members], refs[members : 2 * members], refs[2 * members :]
    updated, residual, all_rows, weights, codes_v, codes, sem = refs
    step = pl.program_id(0)
    channels = coeffs.shape[1]
    half = residual.shape[0] // 2
    vectors = scale.shape[1]
    block = coeffs.shape[0]
    count = updated.shape[0]
    listed = half + 2 * vectors
    lines = codes.shape[0] // members
    copy = pltpu.make_async_copy(codes_v, codes, sem)

    @pl.when(step == 0)
    def _():
        core = lax.axis_index("centers") & 1
        first = (
            lax.broadcasted_iota(i32, (lines, 128), 0) + lax.broadcasted_iota(i32, (lines, 128), 1) == 0
        )
        for member in range(members):
            digits = [
                mine[member][listed + k * lines : listed + (k + 1) * lines, :].astype(f32)
                for k in range(3)
            ]
            code = (digits[0] + 256.0 * digits[1] + 65536.0 * digits[2]).astype(i32)
            local = code & (count - 1)
            pos = code >> (count.bit_length() - 1)
            side = (pos >> (half.bit_length() - 1)) ^ core
            source = (side * members + member) * half + (pos & (half - 1))
            codes_v[member * lines : (member + 1) * lines, :] = jnp.where(
                first, code, (source << 16) + local
            )
        copy.start()
        projected = jnp.zeros((vectors, channels), f32)
        for side, part in enumerate((mine, other)):
            for member in range(members):
                start = (side * members + member) * half
                all_rows[start : start + half, :] = part[member][0:half, :].astype(f32) * -step_size
                projected += part[member][half : half + vectors, :].astype(f32)
                projected += part[member][half + vectors : half + 2 * vectors, :].astype(f32)
        scales = jnp.broadcast_to(scale[...], (channels, vectors)).T
        top, rest = split_two(projected * scales * step_size)
        weights[:, 0:channels] = top
        weights[:, channels:] = rest
        for side, part in enumerate((mine, other)):
            start = pl.multiple_of((core ^ side) * half, half)
            residual[pl.ds(start, half), :] = part[0][0:half, :].astype(f32)

    correction = jnp.dot(vectors_t[...], weights[...], preferred_element_type=f32)
    span = pl.ds(pl.multiple_of(step * block, block), block)
    updated[span, :] = coeffs[...] + (correction[:, 0:channels] + correction[:, channels:])

    @pl.when(step == pl.num_programs(0) - 1)
    def _():
        copy.wait()
        for member in range(members):
            base = member * lines

            def add(numbers):
                found = [codes[base + (k >> 7), k & 127] for k in numbers]
                changes = [all_rows[pl.ds(code >> 16, 1), :] for code in found]
                for code, change in zip(found, changes):
                    local = pl.ds(code & 65535, 1)
                    updated[local, :] = updated[local, :] + change

            def eight(group, _):
                add([group * 8 + one for one in range(1, 9)])
                return 0

            def single(k, _):
                add([k])
                return 0

            number = codes[base, 0]
            eights = number >> 3
            lax.fori_loop(0, eights, eight, 0)
            lax.fori_loop(eights * 8 + 1, number + 1, single, 0)


def finish(scale, vectors_t, coeffs, mine, other):
    count, channels = coeffs.shape
    vectors = scale.shape[0]
    members = len(mine)
    lines = LINES
    half = mine[0].shape[0] - 2 * vectors - 3 * lines
    block = 2048
    whole = lambda shape: pl.BlockSpec(shape, lambda i: (0,) * len(shape))
    return pl.pallas_call(
        functools.partial(finish_kernel, members=members),
        name="finish",
        grid=(count // block,),
        in_specs=[
            whole((1, vectors)),
            pl.BlockSpec((block, vectors), lambda i: (i, 0)),
            pl.BlockSpec((block, channels), lambda i: (i, 0)),
        ]
        + [whole(one.shape) for one in (*mine, *other)],
        out_specs=[whole((count, channels)), whole((2 * half, channels))],
        out_shape=[
            jax.ShapeDtypeStruct((count, channels), f32),
            jax.ShapeDtypeStruct((2 * half, channels), f32),
        ],
        scratch_shapes=[
            pltpu.VMEM((2 * members * half, channels), f32),
            pltpu.VMEM((vectors, 2 * channels), bf16),
            pltpu.VMEM((members * lines, 128), i32),
            pltpu.SMEM((members * lines, 128), i32),
            pltpu.SemaphoreType.DMA,
        ],
        compiler_params=pltpu.CompilerParams(vmem_limit_bytes=24 * 2**20),
        cost_estimate=pl.CostEstimate(flops=10**9, bytes_accessed=14 * 2**20, transcendentals=0),
    )(scale.reshape(1, vectors), vectors_t, coeffs, *mine, *other)


def body(centers, coeffs, targets, batch_index, subset_index, eigvec, eigen_scale, *, groups):
    count = centers.shape[0]
    channels = coeffs.shape[1]
    vectors = eigvec.shape[0]
    members = lax.axis_size("batch")
    half = batch_index.shape[0] // 2
    chips = len(groups[0])
    width = centers.shape[1]
    swap = [(i, i ^ 1) for i in range(2 * chips)]

    def across(values):
        return lax.all_to_all(
            values, "centers", 0, 0, tiled=True, axis_index_groups=groups
        )

    mine, other = pick(batch_index, centers)
    mine, other, centers, coeffs, targets, eigvec = lax.optimization_barrier(
        (mine, other, centers, coeffs, targets, eigvec)
    )
    summed = mine + lax.ppermute(other, "centers", swap)
    shards = across(summed).reshape(chips, half // chips, width)
    shard = total_of(shards.astype(f32)).astype(bf16)
    rows_mine = across(jnp.tile(shard, (chips, 1)))
    rows_other = lax.ppermute(rows_mine, "centers", swap)

    vectors_t, hits, labels = prepare(subset_index, batch_index, eigvec, targets)
    sums_mine, sums_other = main(centers, coeffs, vectors_t, rows_mine, rows_other, labels)

    def widened(values):
        values = values.astype(f32)
        return values[..., 0:channels] + values[..., channels : 2 * channels], values[..., 2 * channels :]

    def packed(residual, rest):
        high, low = split_rounded(residual)
        return jnp.concatenate([high, low, rest.astype(bf16)], axis=-1)

    first = widened(sums_mine)
    second = widened(lax.ppermute(sums_other, "centers", swap))
    chip_sums = packed(first[0] + second[0], first[1] + second[1])
    parts = widened(across(chip_sums).reshape(chips, half // chips, -1))
    shard = jnp.concatenate(
        [total_of(parts[0]).astype(bf16), total_of(parts[1]).astype(bf16)], axis=1
    )
    gathered = across(jnp.tile(shard, (chips, 1)))
    high = gathered[:, 0:channels]
    projected = lax.dot_general(
        gathered[:, channels : channels + vectors], high, TN, preferred_element_type=f32
    )
    lines = jnp.zeros((LINES * 128,), i32).at[0 : hits.shape[0]].set(hits).reshape(LINES, 128)
    digits = [((lines >> (8 * k)) & 255).astype(bf16) for k in range(3)]
    message = jnp.concatenate([high, *split_rounded(projected), *digits], axis=0)
    from_batch = [message] + [
        lax.ppermute(message, "batch", [(i, (i + k) % members) for i in range(members)])
        for k in range(1, members)
    ]
    from_other = [lax.ppermute(one, "centers", swap) for one in from_batch]
    return finish(eigen_scale, vectors_t, coeffs, from_batch, from_other)


def solution(mesh):
    chips = mesh.shape["centers"] // 2
    groups = [[2 * chip + core for chip in range(chips)] for core in range(2)]
    return jax.shard_map(
        functools.partial(body, groups=groups),
        mesh=mesh,
        in_specs=(
            P("centers", None),
            P("centers", None),
            P("centers", None),
            P("batch"),
            P("centers"),
            P(None, "centers"),
            P(),
        ),
        out_specs=(P("centers", None), P("batch", None)),
        check_vma=False,
    )
```

```python
import functools

import jax
import jax.numpy as jnp
from jax import lax
from jax.experimental import pallas as pl
from jax.experimental.pallas import tpu as pltpu
from jax.sharding import PartitionSpec as P

spread = 1.0
step_size = 0.5
NT = (((1,), (1,)), ((), ()))
TN = (((0,), (0,)), ((), ()))
bf16 = jnp.bfloat16
f32 = jnp.float32
i32 = jnp.int32
LINES = 16
LOG2_E = 1.4426950408889634


def split_two(values):
    high = values.astype(bf16)
    return high, (values - high.astype(f32)).astype(bf16)


def split_rounded(values):
    high = lax.reduce_precision(values, 8, 7)
    return high.astype(bf16), (values - high).astype(bf16)


def total_of(parts):
    return functools.reduce(jnp.add, [parts[k] for k in range(parts.shape[0])])


def next_hits(index, offset, count):
    rows = index.shape[0]
    total = rows * 128
    lane = lax.broadcasted_iota(i32, (rows, 128), 1)
    sub = lax.broadcasted_iota(i32, (rows, 128), 0)
    local = index - offset
    found = jnp.where((local >= 0) & (local < count), sub * 128 + lane, total)
    shift = 1
    while shift < 128:
        moved = pltpu.roll(found, 128 - shift, 1)
        found = jnp.minimum(found, jnp.where(lane < 128 - shift, moved, total))
        shift *= 2
    later = jnp.broadcast_to(found[:, 0:1], (rows, 128))
    later = jnp.where(sub < rows - 1, pltpu.roll(later, rows - 1, 0), total)
    shift = 1
    while shift < rows:
        moved = pltpu.roll(later, rows - shift, 0)
        later = jnp.minimum(later, jnp.where(sub < rows - shift, moved, total))
        shift *= 2
    return jnp.minimum(found, later)


def following(nxt, pos, total):
    after = jnp.minimum(pos + 1, total - 1)
    return jnp.where(pos + 1 < total, nxt[after >> 7, after & 127], total)


def pick_kernel(
    subset, index_s, index_v, eigvec, centers, mine, other, nxt, high, low,
    nxt_v, vectors_v, all_centers, spread_out, high_v, low_v, wide, rows, sems,
):
    total = rows.shape[0]
    half = total // 2
    count = centers.shape[0]
    vectors = eigvec.shape[0]
    position = lax.axis_index("centers")
    offset = position * count
    turn = (position & 1) * half
    first = pltpu.make_async_copy(eigvec, vectors_v, sems.at[0])
    first.start()
    load = pltpu.make_async_copy(centers, all_centers, sems.at[1])
    load.start()
    nxt_v[...] = next_hits(index_v[...], offset, count)
    copy = pltpu.make_async_copy(nxt_v, nxt, sems.at[2])
    copy.start()
    spread_out[...] = jnp.zeros_like(spread_out)
    rows[...] = jnp.zeros_like(rows)
    first.wait()

    def put(group, _):
        start = pl.multiple_of(group * 128, 128)
        turned = vectors_v[:, pl.ds(start, 128)].T
        for eight in range(0, 128, 8):
            spots = [subset[start + eight + one] - offset for one in range(8)]
            for one in range(8):
                spread_out[pl.ds(spots[one], 1), 0:vectors] = turned[eight + one : eight + one + 1, :]
        return 0

    lax.fori_loop(0, eigvec.shape[1] // 128, put, 0)
    stores = []
    size = count // 4
    for part in range(4):
        span = pl.ds(part * size, size)
        high_v[span, :], low_v[span, :] = split_two(spread_out[span, 0:vectors])
        for k, (source, target) in enumerate(((high_v, high), (low_v, low))):
            store = pltpu.make_async_copy(
                source.at[span, :], target.at[span, :], sems.at[3 + 2 * part + k]
            )
            store.start()
            stores.append(store)
    copy.wait()
    load.wait()

    def take(pos):
        after = following(nxt, pos, total)
        local = index_s[pos] - offset
        tile = pl.ds(pl.multiple_of((local >> 4) << 4, 16), 16)
        wide[...] = all_centers[tile, :].astype(f32)
        rows[pl.ds(pos ^ turn, 1), :] = wide[pl.ds(local & 15, 1), :]
        return after

    lax.while_loop(lambda pos: pos < total, take, nxt[0, 0])
    mine[...] = rows[0:half, :].astype(bf16)
    other[...] = rows[half:total, :].astype(bf16)
    for store in stores:
        store.wait()


def pick(subset, index, eigvec, centers):
    total = index.shape[0]
    count, width = centers.shape
    vectors = eigvec.shape[0]
    lanes = -(-vectors // 128) * 128
    vmem = pl.BlockSpec(memory_space=pltpu.VMEM)
    smem = pl.BlockSpec(memory_space=pltpu.SMEM)
    hbm = pl.BlockSpec(memory_space=pltpu.HBM)
    anywhere = pl.BlockSpec(memory_space=pl.ANY)
    return pl.pallas_call(
        pick_kernel,
        name="pick",
        in_specs=[smem, smem, vmem, hbm, hbm],
        out_specs=[vmem, vmem, smem, anywhere, anywhere],
        out_shape=[
            jax.ShapeDtypeStruct((total // 2, width), bf16),
            jax.ShapeDtypeStruct((total // 2, width), bf16),
            jax.ShapeDtypeStruct((total // 128, 128), i32),
            jax.ShapeDtypeStruct((count, vectors), bf16),
            jax.ShapeDtypeStruct((count, vectors), bf16),
        ],
        scratch_shapes=[
            pltpu.VMEM((total // 128, 128), i32),
            pltpu.VMEM(eigvec.shape, f32),
            pltpu.VMEM(centers.shape, bf16),
            pltpu.VMEM((count, lanes), f32),
            pltpu.VMEM((count, vectors), bf16),
            pltpu.VMEM((count, vectors), bf16),
            pltpu.VMEM((16, width), f32),
            pltpu.VMEM((total, width), f32),
            pltpu.SemaphoreType.DMA((11,)),
        ],
        compiler_params=pltpu.CompilerParams(vmem_limit_bytes=56 * 2**20),
        cost_estimate=pl.CostEstimate(flops=0, bytes_accessed=24 * 2**20, transcendentals=0),
    )(subset, index, index.reshape(total // 128, 128), eigvec, centers)


def note_kernel(index_s, nxt, targets, hits, labels, all_targets, wide, sem):
    total = index_s.shape[0]
    count = targets.shape[0]
    position = lax.axis_index("centers")
    offset = position * count
    turn = (position & 1) * (total // 2)
    load = pltpu.make_async_copy(targets, all_targets, sem)
    load.start()
    labels[...] = jnp.zeros_like(labels)
    load.wait()

    def note(state):
        number, pos = state
        after = following(nxt, pos, total)
        local = index_s[pos] - offset
        hits[number] = pos * count + local
        tile = pl.ds(pl.multiple_of((local >> 4) << 4, 16), 16)
        wide[...] = all_targets[tile, :].astype(f32)
        labels[pl.ds(pos ^ turn, 1), :] = wide[pl.ds(local & 15, 1), :]
        return number + 1, after

    number, _ = lax.while_loop(lambda s: s[1] < total, note, (jnp.int32(1), nxt[0, 0]))
    hits[0] = number - 1


def note(index, nxt, targets):
    total, channels = index.shape[0], targets.shape[1]
    smem = pl.BlockSpec(memory_space=pltpu.SMEM)
    return pl.pallas_call(
        note_kernel,
        name="note",
        in_specs=[smem, smem, pl.BlockSpec(memory_space=pl.ANY)],
        out_specs=[smem, pl.BlockSpec(memory_space=pltpu.VMEM)],
        out_shape=[
            jax.ShapeDtypeStruct((total + 128,), i32),
            jax.ShapeDtypeStruct((total, channels), f32),
        ],
        scratch_shapes=[
            pltpu.VMEM(targets.shape, bf16),
            pltpu.VMEM((16, channels), f32),
            pltpu.SemaphoreType.DMA,
        ],
        compiler_params=pltpu.CompilerParams(vmem_limit_bytes=8 * 2**20),
        cost_estimate=pl.CostEstimate(flops=0, bytes_accessed=6 * 2**20, transcendentals=0),
    )(index, nxt, targets)


def main_kernel(
    all_centers, coeffs, vectors_t, rows_mine, rows_other, labels, mine, other,
    turned, norms, total, blocks, sems, *, part,
):
    step = pl.program_id(0)
    block = blocks.shape[1]
    slot = step & 1

    def load(step, slot):
        span = pl.ds(pl.multiple_of(step * block, block), block)
        return pltpu.make_async_copy(all_centers.at[span, :], blocks.at[slot], sems.at[slot])

    @pl.when(step == 0)
    def _():
        load(step, slot).start()

    @pl.when(step + 1 < pl.num_programs(0))
    def _():
        load(step + 1, 1 - slot).start()

    half = rows_mine.shape[0]
    channels = labels.shape[1]
    vectors = vectors_t.shape[1]

    @pl.when(step == 0)
    def _():
        ones = jnp.ones((8, rows_mine.shape[1]), bf16)
        for start, rows in ((0, rows_mine), (half, rows_other)):
            span = slice(start, start + half)
            values = rows[...]
            high, low = split_two(jnp.square(values.astype(f32)))
            norms[:, span] = (
                lax.dot_general(ones, high, NT, preferred_element_type=f32)
                + lax.dot_general(ones, low, NT, preferred_element_type=f32)
                + 0.001
            )
            turned[:, span] = (values * jnp.asarray(-2.0, bf16)).T
        total[...] = jnp.zeros_like(total)

    load(step, slot).wait()
    centers = blocks.at[slot]
    spots = list(range(0, block, part))

    def products(start):
        block = centers[start : start + part, :]
        own = jnp.sum(jnp.square(block.astype(f32)), axis=1, keepdims=True)
        return own, jnp.dot(block, turned[...], preferred_element_type=f32)

    ahead = products(spots[0])
    for number, start in enumerate(spots):
        own, prods = ahead
        if number + 1 < len(spots):
            ahead = products(spots[number + 1])
        distance = jnp.maximum(prods + (own + norms[0:1, :]), 0.001)
        kernel = jnp.exp2(distance * lax.rsqrt(distance) * (-LOG2_E / spread)).astype(bf16)
        span = slice(start, start + part)
        columns = jnp.concatenate([coeffs[span, :].astype(bf16), vectors_t[span, :]], axis=1)
        total[...] += lax.dot_general(columns, kernel, TN, preferred_element_type=f32)

    @pl.when(step == pl.num_programs(0) - 1)
    def _():
        for start, out in ((0, mine), (half, other)):
            span = slice(start, start + half)
            partial = total[0:channels, span].T - labels[span, :]
            high, low = split_two(partial)
            out[:, 0:channels] = high
            out[:, channels : 2 * channels] = low
            out[:, 2 * channels :] = jnp.zeros((half, out.shape[1] - 2 * channels), bf16)
            out[:, 2 * channels : 2 * channels + vectors] = total[channels:, span].T.astype(bf16)


def main(centers, coeffs, vectors_t, rows_mine, rows_other, labels):
    count, width = centers.shape
    half, channels = rows_mine.shape[0], labels.shape[1]
    columns = channels + vectors_t.shape[1]
    block, part = 1024, 512
    whole = lambda shape: pl.BlockSpec(shape, lambda i: (0, 0))
    return pl.pallas_call(
        functools.partial(main_kernel, part=part),
        name="kernel_sums",
        grid=(count // block,),
        in_specs=[
            pl.BlockSpec(memory_space=pltpu.HBM),
            pl.BlockSpec((block, channels), lambda i: (i, 0)),
            pl.BlockSpec((block, vectors_t.shape[1]), lambda i: (i, 0)),
            whole((half, width)),
            whole((half, width)),
            whole((2 * half, channels)),
        ],
        out_specs=[whole((half, 512)), whole((half, 512))],
        out_shape=[jax.ShapeDtypeStruct((half, 512), bf16)] * 2,
        scratch_shapes=[
            pltpu.VMEM((width, 2 * half), bf16),
            pltpu.VMEM((8, 2 * half), f32),
            pltpu.VMEM((columns, 2 * half), f32),
            pltpu.VMEM((2, block, width), bf16),
            pltpu.SemaphoreType.DMA((2,)),
        ],
        compiler_params=pltpu.CompilerParams(vmem_limit_bytes=46 * 2**20),
        cost_estimate=pl.CostEstimate(
            flops=2 * count * 2 * half * (width + columns),
            bytes_accessed=20 * 2**20,
            transcendentals=2 * count * 2 * half,
        ),
    )(centers, coeffs, vectors_t, rows_mine, rows_other, labels)


def finish_kernel(scale, high, low, coeffs, *refs, members):
    mine, other, refs = refs[:members], refs[members : 2 * members], refs[2 * members :]
    updated, residual, all_rows, weights, codes_v, codes, sem = refs
    step = pl.program_id(0)
    channels = coeffs.shape[1]
    half = residual.shape[0] // 2
    vectors = scale.shape[1]
    block = coeffs.shape[0]
    count = updated.shape[0]
    listed = half + vectors
    lines = codes.shape[0] // members
    copy = pltpu.make_async_copy(codes_v, codes, sem)

    @pl.when(step == 0)
    def _():
        core = lax.axis_index("centers") & 1
        first = (
            lax.broadcasted_iota(i32, (lines, 128), 0) + lax.broadcasted_iota(i32, (lines, 128), 1) == 0
        )
        for member in range(members):
            digits = [
                mine[member][listed + k * lines : listed + (k + 1) * lines, :].astype(f32)
                for k in range(3)
            ]
            code = (digits[0] + 256.0 * digits[1] + 65536.0 * digits[2]).astype(i32)
            local = code & (count - 1)
            pos = code >> (count.bit_length() - 1)
            side = (pos >> (half.bit_length() - 1)) ^ core
            source = (side * members + member) * half + (pos & (half - 1))
            codes_v[member * lines : (member + 1) * lines, :] = jnp.where(
                first, code, (source << 16) + local
            )
        copy.start()
        projected = jnp.zeros((vectors, channels), f32)
        for side, part in enumerate((mine, other)):
            for member in range(members):
                start = (side * members + member) * half
                all_rows[start : start + half, :] = part[member][0:half, :].astype(f32) * -step_size
                projected += part[member][half : half + vectors, :].astype(f32)
        scales = jnp.broadcast_to(scale[...], (channels, vectors)).T
        top, rest = split_two(projected * scales * step_size)
        weights[:, 0:channels] = top
        weights[:, channels:] = rest
        for side, part in enumerate((mine, other)):
            start = pl.multiple_of((core ^ side) * half, half)
            residual[pl.ds(start, half), :] = part[0][0:half, :].astype(f32)

    correction = jnp.dot(high[...], weights[...], preferred_element_type=f32)
    correction_low = jnp.dot(low[...], weights[:, 0:channels], preferred_element_type=f32)
    span = pl.ds(pl.multiple_of(step * block, block), block)
    updated[span, :] = coeffs[...] + (
        correction[:, 0:channels] + (correction[:, channels:] + correction_low)
    )

    @pl.when(step == pl.num_programs(0) - 1)
    def _():
        copy.wait()
        for member in range(members):
            base = member * lines

            def add(numbers):
                found = [codes[base + (k >> 7), k & 127] for k in numbers]
                changes = [all_rows[pl.ds(code >> 16, 1), :] for code in found]
                for code, change in zip(found, changes):
                    local = pl.ds(code & 65535, 1)
                    updated[local, :] = updated[local, :] + change

            def eight(group, _):
                add([group * 8 + one for one in range(1, 9)])
                return 0

            def single(k, _):
                add([k])
                return 0

            number = codes[base, 0]
            eights = number >> 3
            lax.fori_loop(0, eights, eight, 0)
            lax.fori_loop(eights * 8 + 1, number + 1, single, 0)


def finish(scale, high, low, coeffs, mine, other):
    count, channels = coeffs.shape
    vectors = scale.shape[0]
    members = len(mine)
    lines = LINES
    half = mine[0].shape[0] - vectors - 3 * lines
    block = 2048
    whole = lambda shape: pl.BlockSpec(shape, lambda i: (0,) * len(shape))
    return pl.pallas_call(
        functools.partial(finish_kernel, members=members),
        name="finish",
        grid=(count // block,),
        in_specs=[
            whole((1, vectors)),
            pl.BlockSpec((block, vectors), lambda i: (i, 0)),
            pl.BlockSpec((block, vectors), lambda i: (i, 0)),
            pl.BlockSpec((block, channels), lambda i: (i, 0)),
        ]
        + [whole(one.shape) for one in (*mine, *other)],
        out_specs=[whole((count, channels)), whole((2 * half, channels))],
        out_shape=[
            jax.ShapeDtypeStruct((count, channels), f32),
            jax.ShapeDtypeStruct((2 * half, channels), f32),
        ],
        scratch_shapes=[
            pltpu.VMEM((2 * members * half, channels), f32),
            pltpu.VMEM((vectors, 2 * channels), bf16),
            pltpu.VMEM((members * lines, 128), i32),
            pltpu.SMEM((members * lines, 128), i32),
            pltpu.SemaphoreType.DMA,
        ],
        compiler_params=pltpu.CompilerParams(vmem_limit_bytes=24 * 2**20),
        cost_estimate=pl.CostEstimate(flops=10**9, bytes_accessed=14 * 2**20, transcendentals=0),
    )(scale.reshape(1, vectors), high, low, coeffs, *mine, *other)


def body(centers, coeffs, targets, batch_index, subset_index, eigvec, eigen_scale, *, groups):
    count = centers.shape[0]
    channels = coeffs.shape[1]
    vectors = eigvec.shape[0]
    members = lax.axis_size("batch")
    half = batch_index.shape[0] // 2
    chips = len(groups[0])
    width = centers.shape[1]
    swap = [(i, i ^ 1) for i in range(2 * chips)]

    def across(values):
        return lax.all_to_all(
            values, "centers", 0, 0, tiled=True, axis_index_groups=groups
        )

    mine, other, nxt, vectors_t, vectors_low = pick(subset_index, batch_index, eigvec, centers)
    summed = mine + lax.ppermute(other, "centers", swap)
    shards = across(summed).reshape(chips, half // chips, width)
    shard = total_of(shards.astype(f32)).astype(bf16)
    rows_mine = across(jnp.tile(shard, (chips, 1)))
    rows_other = lax.ppermute(rows_mine, "centers", swap)

    hits, labels = note(batch_index, nxt, targets)
    sums_mine, sums_other = main(centers, coeffs, vectors_t, rows_mine, rows_other, labels)

    def widened(values):
        values = values.astype(f32)
        return values[..., 0:channels] + values[..., channels : 2 * channels], values[..., 2 * channels :]

    def packed(residual, rest):
        high, low = split_rounded(residual)
        return jnp.concatenate([high, low, rest.astype(bf16)], axis=-1)

    first = widened(sums_mine)
    second = widened(lax.ppermute(sums_other, "centers", swap))
    chip_sums = packed(first[0] + second[0], first[1] + second[1])
    parts = widened(across(chip_sums).reshape(chips, half // chips, -1))
    shard = jnp.concatenate(
        [total_of(parts[0]).astype(bf16), total_of(parts[1]).astype(bf16)], axis=1
    )
    gathered = across(jnp.tile(shard, (chips, 1)))
    high = gathered[:, 0:channels]
    projected = lax.dot_general(
        gathered[:, channels : channels + vectors], high, TN, preferred_element_type=f32
    )
    lines = jnp.zeros((LINES * 128,), i32).at[0 : hits.shape[0]].set(hits).reshape(LINES, 128)
    digits = [((lines >> (8 * k)) & 255).astype(bf16) for k in range(3)]
    message = jnp.concatenate([high, projected.astype(bf16), *digits], axis=0)
    from_batch = [message] + [
        lax.ppermute(message, "batch", [(i, (i + k) % members) for i in range(members)])
        for k in range(1, members)
    ]
    from_other = [lax.ppermute(one, "centers", swap) for one in from_batch]
    return finish(eigen_scale, vectors_t, vectors_low, coeffs, from_batch, from_other)


def solution(mesh):
    chips = mesh.shape["centers"] // 2
    groups = [[2 * chip + core for chip in range(chips)] for core in range(2)]
    return jax.shard_map(
        functools.partial(body, groups=groups),
        mesh=mesh,
        in_specs=(
            P("centers", None),
            P("centers", None),
            P("centers", None),
            P("batch"),
            P("centers"),
            P(None, "centers"),
            P(),
        ),
        out_specs=(P("centers", None), P("batch", None)),
        check_vma=False,
    )
```

```python
import functools

import jax
import jax.numpy as jnp
from jax import lax
from jax.experimental import pallas as pl
from jax.experimental.pallas import tpu as pltpu
from jax.sharding import PartitionSpec as P

spread = 1.0
step_size = 0.5
NT = (((1,), (1,)), ((), ()))
TN = (((0,), (0,)), ((), ()))
bf16 = jnp.bfloat16
f32 = jnp.float32
i32 = jnp.int32
LINES = 16
LOG2_E = 1.4426950408889634


def split_two(values):
    high = values.astype(bf16)
    return high, (values - high.astype(f32)).astype(bf16)


def split_rounded(values):
    high = lax.reduce_precision(values, 8, 7)
    return high.astype(bf16), (values - high).astype(bf16)


def total_of(parts):
    return functools.reduce(jnp.add, [parts[k] for k in range(parts.shape[0])])


def next_hits(index, offset, count):
    rows = index.shape[0]
    total = rows * 128
    lane = lax.broadcasted_iota(i32, (rows, 128), 1)
    sub = lax.broadcasted_iota(i32, (rows, 128), 0)
    local = index - offset
    found = jnp.where((local >= 0) & (local < count), sub * 128 + lane, total)
    shift = 1
    while shift < 128:
        moved = pltpu.roll(found, 128 - shift, 1)
        found = jnp.minimum(found, jnp.where(lane < 128 - shift, moved, total))
        shift *= 2
    later = jnp.broadcast_to(found[:, 0:1], (rows, 128))
    later = jnp.where(sub < rows - 1, pltpu.roll(later, rows - 1, 0), total)
    shift = 1
    while shift < rows:
        moved = pltpu.roll(later, rows - shift, 0)
        later = jnp.minimum(later, jnp.where(sub < rows - shift, moved, total))
        shift *= 2
    return jnp.minimum(found, later)


def following(nxt, pos, total):
    after = jnp.minimum(pos + 1, total - 1)
    return jnp.where(pos + 1 < total, nxt[after >> 7, after & 127], total)


def pick_kernel(
    index_s, index_v, centers, mine, other, nxt, nxt_v, all_centers, wide, rows, sems, *, sides
):
    total = rows.shape[0]
    half = total // 2
    shard = half // (sides[0] * sides[1])
    count = centers.shape[0]
    position = lax.axis_index("centers")
    offset = position * count
    core = position & 1
    first, second = (position >> 1) // sides[1], (position >> 1) & (sides[1] - 1)
    load = pltpu.make_async_copy(centers, all_centers, sems.at[0])
    load.start()
    nxt_v[...] = next_hits(index_v[...], offset, count)
    copy = pltpu.make_async_copy(nxt_v, nxt, sems.at[1])
    copy.start()
    rows[...] = jnp.zeros_like(rows)
    copy.wait()
    load.wait()

    shard_bits = shard.bit_length() - 1
    second_bits = sides[1].bit_length() - 1
    half_bits = half.bit_length() - 1

    def take(pos):
        after = following(nxt, pos, total)
        local = index_s[pos] - offset
        tile = pl.ds(pl.multiple_of((local >> 4) << 4, 16), 16)
        chip = (pos >> shard_bits) & (sides[0] * sides[1] - 1)
        along = ((chip >> second_bits) - first) & (sides[0] - 1)
        across = ((chip & (sides[1] - 1)) - second) & (sides[1] - 1)
        place = (((along << second_bits) | across) << shard_bits) | (pos & (shard - 1))
        spot = (((pos >> half_bits) ^ core) << half_bits) | place
        wide[...] = all_centers[tile, :].astype(f32)
        rows[pl.ds(spot, 1), :] = wide[pl.ds(local & 15, 1), :]
        return after

    lax.while_loop(lambda pos: pos < total, take, nxt[0, 0])
    mine[...] = rows[0:half, :].astype(bf16)
    other[...] = rows[half:total, :].astype(bf16)


def pick(index, centers, sides):
    total = index.shape[0]
    width = centers.shape[1]
    vmem = pl.BlockSpec(memory_space=pltpu.VMEM)
    smem = pl.BlockSpec(memory_space=pltpu.SMEM)
    hbm = pl.BlockSpec(memory_space=pltpu.HBM)
    return pl.pallas_call(
        functools.partial(pick_kernel, sides=sides),
        name="pick",
        in_specs=[smem, vmem, hbm],
        out_specs=[vmem, vmem, smem],
        out_shape=[
            jax.ShapeDtypeStruct((total // 2, width), bf16),
            jax.ShapeDtypeStruct((total // 2, width), bf16),
            jax.ShapeDtypeStruct((total // 128, 128), i32),
        ],
        scratch_shapes=[
            pltpu.VMEM((total // 128, 128), i32),
            pltpu.VMEM(centers.shape, bf16),
            pltpu.VMEM((16, width), f32),
            pltpu.VMEM((total, width), f32),
            pltpu.SemaphoreType.DMA((2,)),
        ],
        compiler_params=pltpu.CompilerParams(vmem_limit_bytes=56 * 2**20),
        cost_estimate=pl.CostEstimate(flops=0, bytes_accessed=14 * 2**20, transcendentals=0),
    )(index, index.reshape(total // 128, 128), centers)


def prepare_kernel(subset, eigvec, high, low, wide):
    step = pl.program_id(0)
    vectors, count = eigvec.shape
    block = high.shape[0]

    @pl.when(step == 0)
    def _():
        offset = lax.axis_index("centers") * wide.shape[0]
        wide[...] = jnp.zeros_like(wide)

        def put(group, _):
            start = pl.multiple_of(group * 128, 128)
            turned = eigvec[:, pl.ds(start, 128)].T
            for eight in range(0, 128, 8):
                spots = [subset[start + eight + one] - offset for one in range(8)]
                for one in range(8):
                    wide[pl.ds(spots[one], 1), 0:vectors] = turned[eight + one : eight + one + 1, :]
            return 0

        lax.fori_loop(0, count // 128, put, 0)

    span = pl.ds(pl.multiple_of(step * block, block), block)
    high[...], low[...] = split_two(wide[span, 0:vectors])


def prepare(subset, eigvec, centers):
    vectors, count = eigvec.shape
    block = 2048
    lanes = -(-vectors // 128) * 128
    part = pl.BlockSpec((block, vectors), lambda i: (i, 0))
    return pl.pallas_call(
        prepare_kernel,
        name="prepare",
        grid=(centers // block,),
        in_specs=[
            pl.BlockSpec(memory_space=pltpu.SMEM),
            pl.BlockSpec((vectors, count), lambda i: (0, 0)),
        ],
        out_specs=[part, part],
        out_shape=[jax.ShapeDtypeStruct((centers, vectors), bf16)] * 2,
        scratch_shapes=[pltpu.VMEM((centers, lanes), f32)],
        compiler_params=pltpu.CompilerParams(vmem_limit_bytes=20 * 2**20),
        cost_estimate=pl.CostEstimate(flops=0, bytes_accessed=24 * 2**20, transcendentals=0),
    )(subset, eigvec)


def note_kernel(index_s, nxt, targets, hits, labels, all_targets, wide, sem):
    total = index_s.shape[0]
    count = targets.shape[0]
    position = lax.axis_index("centers")
    offset = position * count
    turn = (position & 1) * (total // 2)
    load = pltpu.make_async_copy(targets, all_targets, sem)
    load.start()
    labels[...] = jnp.zeros_like(labels)
    load.wait()

    def note(state):
        number, pos = state
        after = following(nxt, pos, total)
        local = index_s[pos] - offset
        hits[number] = pos * count + local
        tile = pl.ds(pl.multiple_of((local >> 4) << 4, 16), 16)
        wide[...] = all_targets[tile, :].astype(f32)
        labels[pl.ds(pos ^ turn, 1), :] = wide[pl.ds(local & 15, 1), :]
        return number + 1, after

    number, _ = lax.while_loop(lambda s: s[1] < total, note, (jnp.int32(1), nxt[0, 0]))
    hits[0] = number - 1


def note(index, nxt, targets):
    total, channels = index.shape[0], targets.shape[1]
    smem = pl.BlockSpec(memory_space=pltpu.SMEM)
    return pl.pallas_call(
        note_kernel,
        name="note",
        in_specs=[smem, smem, pl.BlockSpec(memory_space=pl.ANY)],
        out_specs=[smem, pl.BlockSpec(memory_space=pltpu.VMEM)],
        out_shape=[
            jax.ShapeDtypeStruct((total + 128,), i32),
            jax.ShapeDtypeStruct((total, channels), f32),
        ],
        scratch_shapes=[
            pltpu.VMEM(targets.shape, bf16),
            pltpu.VMEM((16, channels), f32),
            pltpu.SemaphoreType.DMA,
        ],
        compiler_params=pltpu.CompilerParams(vmem_limit_bytes=8 * 2**20),
        cost_estimate=pl.CostEstimate(flops=0, bytes_accessed=6 * 2**20, transcendentals=0),
    )(index, nxt, targets)


def main_kernel(
    all_centers, coeffs, vectors_t, rows_mine, rows_other, labels, mine, other,
    turned, norms, total, blocks, sems, *, part,
):
    step = pl.program_id(0)
    block = blocks.shape[1]
    slot = step & 1

    def load(step, slot):
        span = pl.ds(pl.multiple_of(step * block, block), block)
        return pltpu.make_async_copy(all_centers.at[span, :], blocks.at[slot], sems.at[slot])

    @pl.when(step == 0)
    def _():
        load(step, slot).start()

    @pl.when(step + 1 < pl.num_programs(0))
    def _():
        load(step + 1, 1 - slot).start()

    half = rows_mine.shape[0]
    channels = labels.shape[1]
    vectors = vectors_t.shape[1]

    @pl.when(step == 0)
    def _():
        ones = jnp.ones((8, rows_mine.shape[1]), bf16)
        for start, rows in ((0, rows_mine), (half, rows_other)):
            span = slice(start, start + half)
            values = rows[...]
            high, low = split_two(jnp.square(values.astype(f32)))
            norms[:, span] = (
                lax.dot_general(ones, high, NT, preferred_element_type=f32)
                + lax.dot_general(ones, low, NT, preferred_element_type=f32)
                + 0.001
            )
            turned[:, span] = (values * jnp.asarray(-2.0, bf16)).T
        total[...] = jnp.zeros_like(total)

    load(step, slot).wait()
    centers = blocks.at[slot]
    spots = list(range(0, block, part))

    def products(start):
        block = centers[start : start + part, :]
        own = jnp.sum(jnp.square(block.astype(f32)), axis=1, keepdims=True)
        return own, jnp.dot(block, turned[...], preferred_element_type=f32)

    ahead = products(spots[0])
    for number, start in enumerate(spots):
        own, prods = ahead
        if number + 1 < len(spots):
            ahead = products(spots[number + 1])
        distance = jnp.maximum(prods + (own + norms[0:1, :]), 0.001)
        kernel = jnp.exp2(distance * lax.rsqrt(distance) * (-LOG2_E / spread)).astype(bf16)
        span = slice(start, start + part)
        columns = jnp.concatenate([coeffs[span, :].astype(bf16), vectors_t[span, :]], axis=1)
        total[...] += lax.dot_general(columns, kernel, TN, preferred_element_type=f32)

    @pl.when(step == pl.num_programs(0) - 1)
    def _():
        for start, out in ((0, mine), (half, other)):
            span = slice(start, start + half)
            partial = total[0:channels, span].T - labels[span, :]
            high, low = split_two(partial)
            out[:, 0:channels] = high
            out[:, channels : 2 * channels] = low
            out[:, 2 * channels :] = jnp.zeros((half, out.shape[1] - 2 * channels), bf16)
            out[:, 2 * channels : 2 * channels + vectors] = total[channels:, span].T.astype(bf16)


def main(centers, coeffs, vectors_t, rows_mine, rows_other, labels):
    count, width = centers.shape
    half, channels = rows_mine.shape[0], labels.shape[1]
    columns = channels + vectors_t.shape[1]
    block, part = 1024, 512
    whole = lambda shape: pl.BlockSpec(shape, lambda i: (0, 0))
    return pl.pallas_call(
        functools.partial(main_kernel, part=part),
        name="kernel_sums",
        grid=(count // block,),
        in_specs=[
            pl.BlockSpec(memory_space=pltpu.HBM),
            pl.BlockSpec((block, channels), lambda i: (i, 0)),
            pl.BlockSpec((block, vectors_t.shape[1]), lambda i: (i, 0)),
            whole((half, width)),
            whole((half, width)),
            whole((2 * half, channels)),
        ],
        out_specs=[whole((half, 512)), whole((half, 512))],
        out_shape=[jax.ShapeDtypeStruct((half, 512), bf16)] * 2,
        scratch_shapes=[
            pltpu.VMEM((width, 2 * half), bf16),
            pltpu.VMEM((8, 2 * half), f32),
            pltpu.VMEM((columns, 2 * half), f32),
            pltpu.VMEM((2, block, width), bf16),
            pltpu.SemaphoreType.DMA((2,)),
        ],
        compiler_params=pltpu.CompilerParams(vmem_limit_bytes=38 * 2**20),
        cost_estimate=pl.CostEstimate(
            flops=2 * count * 2 * half * (width + columns),
            bytes_accessed=20 * 2**20,
            transcendentals=2 * count * 2 * half,
        ),
    )(centers, coeffs, vectors_t, rows_mine, rows_other, labels)


def finish_kernel(scale, high, low, coeffs, *refs, members):
    mine, other, refs = refs[:members], refs[members : 2 * members], refs[2 * members :]
    updated, residual, all_rows, weights, codes_v, codes, sem = refs
    step = pl.program_id(0)
    channels = coeffs.shape[1]
    half = residual.shape[0] // 2
    vectors = scale.shape[1]
    block = coeffs.shape[0]
    count = updated.shape[0]
    listed = half + vectors
    lines = codes.shape[0] // members
    copy = pltpu.make_async_copy(codes_v, codes, sem)

    @pl.when(step == 0)
    def _():
        core = lax.axis_index("centers") & 1
        first = (
            lax.broadcasted_iota(i32, (lines, 128), 0) + lax.broadcasted_iota(i32, (lines, 128), 1) == 0
        )
        for member in range(members):
            digits = [
                mine[member][listed + k * lines : listed + (k + 1) * lines, :].astype(f32)
                for k in range(3)
            ]
            code = (digits[0] + 256.0 * digits[1] + 65536.0 * digits[2]).astype(i32)
            local = code & (count - 1)
            pos = code >> (count.bit_length() - 1)
            side = (pos >> (half.bit_length() - 1)) ^ core
            source = (side * members + member) * half + (pos & (half - 1))
            codes_v[member * lines : (member + 1) * lines, :] = jnp.where(
                first, code, (source << 16) + local
            )
        copy.start()
        projected = jnp.zeros((vectors, channels), f32)
        for side, part in enumerate((mine, other)):
            for member in range(members):
                start = (side * members + member) * half
                all_rows[start : start + half, :] = part[member][0:half, :].astype(f32) * -step_size
                projected += part[member][half : half + vectors, :].astype(f32)
        scales = jnp.broadcast_to(scale[...], (channels, vectors)).T
        top, rest = split_two(projected * scales * step_size)
        weights[:, 0:channels] = top
        weights[:, channels:] = rest
        for side, part in enumerate((mine, other)):
            start = pl.multiple_of((core ^ side) * half, half)
            residual[pl.ds(start, half), :] = part[0][0:half, :].astype(f32)

    correction = jnp.dot(high[...], weights[...], preferred_element_type=f32)
    correction_low = jnp.dot(low[...], weights[:, 0:channels], preferred_element_type=f32)
    span = pl.ds(pl.multiple_of(step * block, block), block)
    updated[span, :] = coeffs[...] + (
        correction[:, 0:channels] + (correction[:, channels:] + correction_low)
    )

    @pl.when(step == pl.num_programs(0) - 1)
    def _():
        copy.wait()
        for member in range(members):
            base = member * lines

            def add(numbers):
                found = [codes[base + (k >> 7), k & 127] for k in numbers]
                changes = [all_rows[pl.ds(code >> 16, 1), :] for code in found]
                for code, change in zip(found, changes):
                    local = pl.ds(code & 65535, 1)
                    updated[local, :] = updated[local, :] + change

            def eight(group, _):
                add([group * 8 + one for one in range(1, 9)])
                return 0

            def single(k, _):
                add([k])
                return 0

            number = codes[base, 0]
            eights = number >> 3
            lax.fori_loop(0, eights, eight, 0)
            lax.fori_loop(eights * 8 + 1, number + 1, single, 0)


def finish(scale, high, low, coeffs, mine, other):
    count, channels = coeffs.shape
    vectors = scale.shape[0]
    members = len(mine)
    lines = LINES
    half = mine[0].shape[0] - vectors - 3 * lines
    block = 2048
    whole = lambda shape: pl.BlockSpec(shape, lambda i: (0,) * len(shape))
    return pl.pallas_call(
        functools.partial(finish_kernel, members=members),
        name="finish",
        grid=(count // block,),
        in_specs=[
            whole((1, vectors)),
            pl.BlockSpec((block, vectors), lambda i: (i, 0)),
            pl.BlockSpec((block, vectors), lambda i: (i, 0)),
            pl.BlockSpec((block, channels), lambda i: (i, 0)),
        ]
        + [whole(one.shape) for one in (*mine, *other)],
        out_specs=[whole((count, channels)), whole((2 * half, channels))],
        out_shape=[
            jax.ShapeDtypeStruct((count, channels), f32),
            jax.ShapeDtypeStruct((2 * half, channels), f32),
        ],
        scratch_shapes=[
            pltpu.VMEM((2 * members * half, channels), f32),
            pltpu.VMEM((vectors, 2 * channels), bf16),
            pltpu.VMEM((members * lines, 128), i32),
            pltpu.SMEM((members * lines, 128), i32),
            pltpu.SemaphoreType.DMA,
        ],
        compiler_params=pltpu.CompilerParams(vmem_limit_bytes=24 * 2**20),
        cost_estimate=pl.CostEstimate(flops=10**9, bytes_accessed=14 * 2**20, transcendentals=0),
    )(scale.reshape(1, vectors), high, low, coeffs, *mine, *other)


def body(centers, coeffs, targets, batch_index, subset_index, eigvec, eigen_scale, *, groups):
    count = centers.shape[0]
    channels = coeffs.shape[1]
    vectors = eigvec.shape[0]
    members = lax.axis_size("batch")
    half = batch_index.shape[0] // 2
    chips = len(groups[0])
    sides = (chips // 4, 4)
    swap = [(i, i ^ 1) for i in range(2 * chips)]

    def across(values):
        return lax.all_to_all(
            values, "centers", 0, 0, tiled=True, axis_index_groups=groups
        )

    def turned(blocks, axis):
        total = blocks[0]
        for k in range(1, len(blocks)):
            pairs = []
            for chip in range(chips):
                place = [chip // sides[1], chip % sides[1]]
                place[axis] = (place[axis] + k) % sides[axis]
                target = place[0] * sides[1] + place[1]
                pairs += [(2 * chip + core, 2 * target + core) for core in range(2)]
            total = total + lax.ppermute(blocks[k], "centers", pairs)
        return total

    def cut(values, parts):
        size = values.shape[0] // parts
        return [values[k * size : (k + 1) * size] for k in range(parts)]

    mine, other, nxt = pick(batch_index, centers, sides)
    summed = mine + lax.ppermute(other, "centers", swap)
    summed, eigvec = lax.optimization_barrier((summed, eigvec))
    vectors_t, vectors_low = prepare(subset_index, eigvec, count)
    row_sums = turned(cut(summed, sides[0]), 0)
    row_sums, vectors_t, vectors_low = lax.optimization_barrier((row_sums, vectors_t, vectors_low))
    shard = turned(cut(row_sums, sides[1]), 1)
    rows_mine = across(jnp.tile(shard, (chips, 1)))
    rows_other = lax.ppermute(rows_mine, "centers", swap)

    hits, labels = note(batch_index, nxt, targets)
    sums_mine, sums_other = main(centers, coeffs, vectors_t, rows_mine, rows_other, labels)

    def widened(values):
        values = values.astype(f32)
        return values[..., 0:channels] + values[..., channels : 2 * channels], values[..., 2 * channels :]

    def packed(residual, rest):
        high, low = split_rounded(residual)
        return jnp.concatenate([high, low, rest.astype(bf16)], axis=-1)

    first = widened(sums_mine)
    second = widened(lax.ppermute(sums_other, "centers", swap))
    chip_sums = packed(first[0] + second[0], first[1] + second[1])
    parts = widened(across(chip_sums).reshape(chips, half // chips, -1))
    shard = jnp.concatenate(
        [total_of(parts[0]).astype(bf16), total_of(parts[1]).astype(bf16)], axis=1
    )
    gathered = across(jnp.tile(shard, (chips, 1)))
    high = gathered[:, 0:channels]
    projected = lax.dot_general(
        gathered[:, channels : channels + vectors], high, TN, preferred_element_type=f32
    )
    lines = jnp.zeros((LINES * 128,), i32).at[0 : hits.shape[0]].set(hits).reshape(LINES, 128)
    digits = [((lines >> (8 * k)) & 255).astype(bf16) for k in range(3)]
    message = jnp.concatenate([high, projected.astype(bf16), *digits], axis=0)
    from_batch = [message] + [
        lax.ppermute(message, "batch", [(i, (i + k) % members) for i in range(members)])
        for k in range(1, members)
    ]
    from_other = [lax.ppermute(one, "centers", swap) for one in from_batch]
    return finish(eigen_scale, vectors_t, vectors_low, coeffs, from_batch, from_other)


def solution(mesh):
    chips = mesh.shape["centers"] // 2
    groups = [[2 * chip + core for chip in range(chips)] for core in range(2)]
    return jax.shard_map(
        functools.partial(body, groups=groups),
        mesh=mesh,
        in_specs=(
            P("centers", None),
            P("centers", None),
            P("centers", None),
            P("batch"),
            P("centers"),
            P(None, "centers"),
            P(),
        ),
        out_specs=(P("centers", None), P("batch", None)),
        check_vma=False,
    )
```

```python
import functools

import jax
import jax.numpy as jnp
from jax import lax
from jax.experimental import pallas as pl
from jax.experimental.pallas import tpu as pltpu
from jax.sharding import PartitionSpec as P

spread = 1.0
step_size = 0.5
NT = (((1,), (1,)), ((), ()))
TN = (((0,), (0,)), ((), ()))
bf16 = jnp.bfloat16
f32 = jnp.float32
i32 = jnp.int32
LINES = 16
LOG2_E = 1.4426950408889634


def split_two(values):
    high = values.astype(bf16)
    return high, (values - high.astype(f32)).astype(bf16)


def split_rounded(values):
    high = lax.reduce_precision(values, 8, 7)
    return high.astype(bf16), (values - high).astype(bf16)


def total_of(parts):
    return functools.reduce(jnp.add, [parts[k] for k in range(parts.shape[0])])


def next_hits(index, offset, count):
    rows = index.shape[0]
    total = rows * 128
    lane = lax.broadcasted_iota(i32, (rows, 128), 1)
    sub = lax.broadcasted_iota(i32, (rows, 128), 0)
    local = index - offset
    found = jnp.where((local >= 0) & (local < count), sub * 128 + lane, total)
    shift = 1
    while shift < 128:
        moved = pltpu.roll(found, 128 - shift, 1)
        found = jnp.minimum(found, jnp.where(lane < 128 - shift, moved, total))
        shift *= 2
    later = jnp.broadcast_to(found[:, 0:1], (rows, 128))
    later = jnp.where(sub < rows - 1, pltpu.roll(later, rows - 1, 0), total)
    shift = 1
    while shift < rows:
        moved = pltpu.roll(later, rows - shift, 0)
        later = jnp.minimum(later, jnp.where(sub < rows - shift, moved, total))
        shift *= 2
    return jnp.minimum(found, later)


def following(nxt, pos, total):
    after = jnp.minimum(pos + 1, total - 1)
    return jnp.where(pos + 1 < total, nxt[after >> 7, after & 127], total)


def pick_kernel(
    index, centers, mine, other, nxt, index_s, index_v, nxt_v, all_centers, wide, rows, sems, *, sides
):
    total = rows.shape[0]
    half = total // 2
    shard = half // (sides[0] * sides[1])
    count = centers.shape[0]
    position = lax.axis_index("centers")
    offset = position * count
    core = position & 1
    first, second = (position >> 1) // sides[1], (position >> 1) & (sides[1] - 1)
    to_vector = pltpu.make_async_copy(index, index_v, sems.at[2])
    to_vector.start()
    to_scalar = pltpu.make_async_copy(index, index_s, sems.at[3])
    to_scalar.start()
    load = pltpu.make_async_copy(centers, all_centers, sems.at[0])
    load.start()
    rows[...] = jnp.zeros_like(rows)
    to_vector.wait()
    nxt_v[...] = next_hits(index_v[...], offset, count)
    copy = pltpu.make_async_copy(nxt_v, nxt, sems.at[1])
    copy.start()
    to_scalar.wait()
    copy.wait()
    load.wait()

    shard_bits = shard.bit_length() - 1
    second_bits = sides[1].bit_length() - 1
    half_bits = half.bit_length() - 1

    def take(pos):
        after = following(nxt, pos, total)
        local = index_s[pos >> 7, pos & 127] - offset
        tile = pl.ds(pl.multiple_of((local >> 4) << 4, 16), 16)
        chip = (pos >> shard_bits) & (sides[0] * sides[1] - 1)
        along = ((chip >> second_bits) - first) & (sides[0] - 1)
        across = ((chip & (sides[1] - 1)) - second) & (sides[1] - 1)
        place = (((along << second_bits) | across) << shard_bits) | (pos & (shard - 1))
        spot = (((pos >> half_bits) ^ core) << half_bits) | place
        wide[...] = all_centers[tile, :].astype(f32)
        rows[pl.ds(spot, 1), :] = wide[pl.ds(local & 15, 1), :]
        return after

    lax.while_loop(lambda pos: pos < total, take, nxt[0, 0])
    mine[...] = rows[0:half, :].astype(bf16)
    other[...] = rows[half:total, :].astype(bf16)


def pick(index, centers, sides):
    total = index.shape[0]
    width = centers.shape[1]
    vmem = pl.BlockSpec(memory_space=pltpu.VMEM)
    smem = pl.BlockSpec(memory_space=pltpu.SMEM)
    hbm = pl.BlockSpec(memory_space=pltpu.HBM)
    return pl.pallas_call(
        functools.partial(pick_kernel, sides=sides),
        name="pick",
        in_specs=[hbm, hbm],
        out_specs=[vmem, vmem, smem],
        out_shape=[
            jax.ShapeDtypeStruct((total // 2, width), bf16),
            jax.ShapeDtypeStruct((total // 2, width), bf16),
            jax.ShapeDtypeStruct((total // 128, 128), i32),
        ],
        scratch_shapes=[
            pltpu.SMEM((total // 128, 128), i32),
            pltpu.VMEM((total // 128, 128), i32),
            pltpu.VMEM((total // 128, 128), i32),
            pltpu.VMEM(centers.shape, bf16),
            pltpu.VMEM((16, width), f32),
            pltpu.VMEM((total, width), f32),
            pltpu.SemaphoreType.DMA((4,)),
        ],
        compiler_params=pltpu.CompilerParams(vmem_limit_bytes=50 * 2**20),
        cost_estimate=pl.CostEstimate(flops=0, bytes_accessed=14 * 2**20, transcendentals=0),
    )(index.reshape(total // 128, 128), centers)


def prepare_kernel(subset, eigvec, high, low, wide):
    step = pl.program_id(0)
    vectors, count = eigvec.shape
    block = high.shape[0]

    @pl.when(step == 0)
    def _():
        offset = lax.axis_index("centers") * wide.shape[0]
        wide[...] = jnp.zeros_like(wide)

        def put(group, _):
            start = pl.multiple_of(group * 128, 128)
            turned = eigvec[:, pl.ds(start, 128)].T
            for eight in range(0, 128, 8):
                spots = [subset[start + eight + one] - offset for one in range(8)]
                for one in range(8):
                    wide[pl.ds(spots[one], 1), 0:vectors] = turned[eight + one : eight + one + 1, :]
            return 0

        lax.fori_loop(0, count // 128, put, 0)

    span = pl.ds(pl.multiple_of(step * block, block), block)
    high[...], low[...] = split_two(wide[span, 0:vectors])


def prepare(subset, eigvec, centers):
    vectors, count = eigvec.shape
    block = 2048
    lanes = -(-vectors // 128) * 128
    part = pl.BlockSpec((block, vectors), lambda i: (i, 0))
    return pl.pallas_call(
        prepare_kernel,
        name="prepare",
        grid=(centers // block,),
        in_specs=[
            pl.BlockSpec(memory_space=pltpu.SMEM),
            pl.BlockSpec((vectors, count), lambda i: (0, 0)),
        ],
        out_specs=[part, part],
        out_shape=[jax.ShapeDtypeStruct((centers, vectors), bf16)] * 2,
        scratch_shapes=[pltpu.VMEM((centers, lanes), f32)],
        compiler_params=pltpu.CompilerParams(vmem_limit_bytes=20 * 2**20),
        cost_estimate=pl.CostEstimate(flops=0, bytes_accessed=24 * 2**20, transcendentals=0),
    )(subset, eigvec)


def note_kernel(index_s, nxt, targets, hits, labels, all_targets, wide, sem):
    total = index_s.shape[0]
    count = targets.shape[0]
    position = lax.axis_index("centers")
    offset = position * count
    turn = (position & 1) * (total // 2)
    load = pltpu.make_async_copy(targets, all_targets, sem)
    load.start()
    labels[...] = jnp.zeros_like(labels)
    load.wait()

    def note(state):
        number, pos = state
        after = following(nxt, pos, total)
        local = index_s[pos] - offset
        hits[number] = pos * count + local
        tile = pl.ds(pl.multiple_of((local >> 4) << 4, 16), 16)
        wide[...] = all_targets[tile, :].astype(f32)
        labels[pl.ds(pos ^ turn, 1), :] = wide[pl.ds(local & 15, 1), :]
        return number + 1, after

    number, _ = lax.while_loop(lambda s: s[1] < total, note, (jnp.int32(1), nxt[0, 0]))
    hits[0] = number - 1


def note(index, nxt, targets):
    total, channels = index.shape[0], targets.shape[1]
    smem = pl.BlockSpec(memory_space=pltpu.SMEM)
    return pl.pallas_call(
        note_kernel,
        name="note",
        in_specs=[smem, smem, pl.BlockSpec(memory_space=pl.ANY)],
        out_specs=[smem, pl.BlockSpec(memory_space=pltpu.VMEM)],
        out_shape=[
            jax.ShapeDtypeStruct((total + 128,), i32),
            jax.ShapeDtypeStruct((total, channels), f32),
        ],
        scratch_shapes=[
            pltpu.VMEM(targets.shape, bf16),
            pltpu.VMEM((16, channels), f32),
            pltpu.SemaphoreType.DMA,
        ],
        compiler_params=pltpu.CompilerParams(vmem_limit_bytes=8 * 2**20),
        cost_estimate=pl.CostEstimate(flops=0, bytes_accessed=6 * 2**20, transcendentals=0),
    )(index, nxt, targets)


def main_kernel(
    all_centers, coeffs, vectors_t, rows_mine, rows_other, labels, mine, other,
    turned, norms, total, blocks, sems, *, part,
):
    step = pl.program_id(0)
    block = blocks.shape[1]
    slot = step & 1

    def load(step, slot):
        span = pl.ds(pl.multiple_of(step * block, block), block)
        return pltpu.make_async_copy(all_centers.at[span, :], blocks.at[slot], sems.at[slot])

    @pl.when(step == 0)
    def _():
        load(step, slot).start()

    @pl.when(step + 1 < pl.num_programs(0))
    def _():
        load(step + 1, 1 - slot).start()

    half = rows_mine.shape[0]
    channels = labels.shape[1]
    vectors = vectors_t.shape[1]

    @pl.when(step == 0)
    def _():
        ones = jnp.ones((8, rows_mine.shape[1]), bf16)
        for start, rows in ((0, rows_mine), (half, rows_other)):
            span = slice(start, start + half)
            values = rows[...]
            high, low = split_two(jnp.square(values.astype(f32)))
            norms[:, span] = (
                lax.dot_general(ones, high, NT, preferred_element_type=f32)
                + lax.dot_general(ones, low, NT, preferred_element_type=f32)
                + 0.001
            )
            turned[:, span] = (values * jnp.asarray(-2.0, bf16)).T
        total[...] = jnp.zeros_like(total)

    load(step, slot).wait()
    centers = blocks.at[slot]
    spots = list(range(0, block, part))

    def products(start):
        block = centers[start : start + part, :]
        own = jnp.sum(jnp.square(block.astype(f32)), axis=1, keepdims=True)
        return own, jnp.dot(block, turned[...], preferred_element_type=f32)

    def add(start, kernel):
        span = slice(start, start + part)
        columns = jnp.concatenate([coeffs[span, :].astype(bf16), vectors_t[span, :]], axis=1)
        total[...] += lax.dot_general(columns, kernel, TN, preferred_element_type=f32)

    ahead = products(spots[0])
    for number, start in enumerate(spots):
        own, prods = ahead
        if number + 1 < len(spots):
            ahead = products(spots[number + 1])
        distance = jnp.maximum(prods + (own + norms[0:1, :]), 0.001)
        kernel = jnp.exp2(distance * lax.rsqrt(distance) * (-LOG2_E / spread)).astype(bf16)
        if number > 0:
            add(*late)
        late = (start, kernel)
    add(*late)

    @pl.when(step == pl.num_programs(0) - 1)
    def _():
        for start, out in ((0, mine), (half, other)):
            span = slice(start, start + half)
            partial = total[0:channels, span].T - labels[span, :]
            high, low = split_two(partial)
            out[:, 0:channels] = high
            out[:, channels : 2 * channels] = low
            out[:, 2 * channels :] = jnp.zeros((half, out.shape[1] - 2 * channels), bf16)
            out[:, 2 * channels : 2 * channels + vectors] = total[channels:, span].T.astype(bf16)


def main(centers, coeffs, vectors_t, rows_mine, rows_other, labels):
    count, width = centers.shape
    half, channels = rows_mine.shape[0], labels.shape[1]
    columns = channels + vectors_t.shape[1]
    block, part = 2048, 512
    whole = lambda shape: pl.BlockSpec(shape, lambda i: (0, 0))
    return pl.pallas_call(
        functools.partial(main_kernel, part=part),
        name="kernel_sums",
        grid=(count // block,),
        in_specs=[
            pl.BlockSpec(memory_space=pltpu.HBM),
            pl.BlockSpec((block, channels), lambda i: (i, 0)),
            pl.BlockSpec((block, vectors_t.shape[1]), lambda i: (i, 0)),
            whole((half, width)),
            whole((half, width)),
            whole((2 * half, channels)),
        ],
        out_specs=[whole((half, 512)), whole((half, 512))],
        out_shape=[jax.ShapeDtypeStruct((half, 512), bf16)] * 2,
        scratch_shapes=[
            pltpu.VMEM((width, 2 * half), bf16),
            pltpu.VMEM((8, 2 * half), f32),
            pltpu.VMEM((columns, 2 * half), f32),
            pltpu.VMEM((2, block, width), bf16),
            pltpu.SemaphoreType.DMA((2,)),
        ],
        compiler_params=pltpu.CompilerParams(vmem_limit_bytes=38 * 2**20),
        cost_estimate=pl.CostEstimate(
            flops=2 * count * 2 * half * (width + columns),
            bytes_accessed=20 * 2**20,
            transcendentals=2 * count * 2 * half,
        ),
    )(centers, coeffs, vectors_t, rows_mine, rows_other, labels)


def finish_kernel(scale, high, low, coeffs, *refs, members):
    mine, other, refs = refs[:members], refs[members : 2 * members], refs[2 * members :]
    updated, residual, all_rows, weights, codes_v, codes, sem = refs
    step = pl.program_id(0)
    channels = coeffs.shape[1]
    half = residual.shape[0] // 2
    vectors = scale.shape[1]
    block = coeffs.shape[0]
    count = updated.shape[0]
    listed = half + vectors
    lines = codes.shape[0] // members
    copy = pltpu.make_async_copy(codes_v, codes, sem)

    @pl.when(step == 0)
    def _():
        core = lax.axis_index("centers") & 1
        first = (
            lax.broadcasted_iota(i32, (lines, 128), 0) + lax.broadcasted_iota(i32, (lines, 128), 1) == 0
        )
        for member in range(members):
            digits = [
                mine[member][listed + k * lines : listed + (k + 1) * lines, :].astype(f32)
                for k in range(3)
            ]
            code = (digits[0] + 256.0 * digits[1] + 65536.0 * digits[2]).astype(i32)
            local = code & (count - 1)
            pos = code >> (count.bit_length() - 1)
            side = (pos >> (half.bit_length() - 1)) ^ core
            source = (side * members + member) * half + (pos & (half - 1))
            codes_v[member * lines : (member + 1) * lines, :] = jnp.where(
                first, code, (source << 16) + local
            )
        copy.start()
        projected = jnp.zeros((vectors, channels), f32)
        for side, part in enumerate((mine, other)):
            for member in range(members):
                start = (side * members + member) * half
                all_rows[start : start + half, :] = part[member][0:half, :].astype(f32) * -step_size
                projected += part[member][half : half + vectors, :].astype(f32)
        scales = jnp.broadcast_to(scale[...], (channels, vectors)).T
        top, rest = split_two(projected * scales * step_size)
        weights[:, 0:channels] = top
        weights[:, channels:] = rest
        for side, part in enumerate((mine, other)):
            start = pl.multiple_of((core ^ side) * half, half)
            residual[pl.ds(start, half), :] = part[0][0:half, :].astype(f32)

    correction = jnp.dot(high[...], weights[...], preferred_element_type=f32)
    correction_low = jnp.dot(low[...], weights[:, 0:channels], preferred_element_type=f32)
    span = pl.ds(pl.multiple_of(step * block, block), block)
    updated[span, :] = coeffs[...] + (
        correction[:, 0:channels] + (correction[:, channels:] + correction_low)
    )

    @pl.when(step == pl.num_programs(0) - 1)
    def _():
        copy.wait()
        for member in range(members):
            base = member * lines

            def add(numbers):
                found = [codes[base + (k >> 7), k & 127] for k in numbers]
                changes = [all_rows[pl.ds(code >> 16, 1), :] for code in found]
                for code, change in zip(found, changes):
                    local = pl.ds(code & 65535, 1)
                    updated[local, :] = updated[local, :] + change

            def eight(group, _):
                add([group * 8 + one for one in range(1, 9)])
                return 0

            def single(k, _):
                add([k])
                return 0

            number = codes[base, 0]
            eights = number >> 3
            lax.fori_loop(0, eights, eight, 0)
            lax.fori_loop(eights * 8 + 1, number + 1, single, 0)


def finish(scale, high, low, coeffs, mine, other):
    count, channels = coeffs.shape
    vectors = scale.shape[0]
    members = len(mine)
    lines = LINES
    half = mine[0].shape[0] - vectors - 3 * lines
    block = 2048
    whole = lambda shape: pl.BlockSpec(shape, lambda i: (0,) * len(shape))
    return pl.pallas_call(
        functools.partial(finish_kernel, members=members),
        name="finish",
        grid=(count // block,),
        in_specs=[
            whole((1, vectors)),
            pl.BlockSpec((block, vectors), lambda i: (i, 0)),
            pl.BlockSpec((block, vectors), lambda i: (i, 0)),
            pl.BlockSpec((block, channels), lambda i: (i, 0)),
        ]
        + [whole(one.shape) for one in (*mine, *other)],
        out_specs=[whole((count, channels)), whole((2 * half, channels))],
        out_shape=[
            jax.ShapeDtypeStruct((count, channels), f32),
            jax.ShapeDtypeStruct((2 * half, channels), f32),
        ],
        scratch_shapes=[
            pltpu.VMEM((2 * members * half, channels), f32),
            pltpu.VMEM((vectors, 2 * channels), bf16),
            pltpu.VMEM((members * lines, 128), i32),
            pltpu.SMEM((members * lines, 128), i32),
            pltpu.SemaphoreType.DMA,
        ],
        compiler_params=pltpu.CompilerParams(vmem_limit_bytes=24 * 2**20),
        cost_estimate=pl.CostEstimate(flops=10**9, bytes_accessed=14 * 2**20, transcendentals=0),
    )(scale.reshape(1, vectors), high, low, coeffs, *mine, *other)


def body(centers, coeffs, targets, batch_index, subset_index, eigvec, eigen_scale, *, groups):
    count = centers.shape[0]
    channels = coeffs.shape[1]
    vectors = eigvec.shape[0]
    members = lax.axis_size("batch")
    half = batch_index.shape[0] // 2
    chips = len(groups[0])
    sides = (chips // 4, 4)
    swap = [(i, i ^ 1) for i in range(2 * chips)]

    def across(values):
        return lax.all_to_all(
            values, "centers", 0, 0, tiled=True, axis_index_groups=groups
        )

    def turned(blocks, axis):
        total = blocks[0]
        for k in range(1, len(blocks)):
            pairs = []
            for chip in range(chips):
                place = [chip // sides[1], chip % sides[1]]
                place[axis] = (place[axis] + k) % sides[axis]
                target = place[0] * sides[1] + place[1]
                pairs += [(2 * chip + core, 2 * target + core) for core in range(2)]
            total = total + lax.ppermute(blocks[k], "centers", pairs)
        return total

    def cut(values, parts):
        size = values.shape[0] // parts
        return [values[k * size : (k + 1) * size] for k in range(parts)]

    mine, other, nxt = pick(batch_index, centers, sides)
    summed = mine + lax.ppermute(other, "centers", swap)
    summed, eigvec = lax.optimization_barrier((summed, eigvec))
    vectors_t, vectors_low = prepare(subset_index, eigvec, count)
    row_sums = turned(cut(summed, sides[0]), 0)
    row_sums, vectors_t, vectors_low = lax.optimization_barrier((row_sums, vectors_t, vectors_low))
    shard = turned(cut(row_sums, sides[1]), 1)
    rows_mine = across(jnp.tile(shard, (chips, 1)))
    rows_other = lax.ppermute(rows_mine, "centers", swap)

    hits, labels = note(batch_index, nxt, targets)
    sums_mine, sums_other = main(centers, coeffs, vectors_t, rows_mine, rows_other, labels)

    def widened(values):
        values = values.astype(f32)
        return values[..., 0:channels] + values[..., channels : 2 * channels], values[..., 2 * channels :]

    def packed(residual, rest):
        high, low = split_rounded(residual)
        return jnp.concatenate([high, low, rest.astype(bf16)], axis=-1)

    first = widened(sums_mine)
    second = widened(lax.ppermute(sums_other, "centers", swap))
    chip_sums = packed(first[0] + second[0], first[1] + second[1])
    parts = widened(across(chip_sums).reshape(chips, half // chips, -1))
    shard = jnp.concatenate(
        [total_of(parts[0]).astype(bf16), total_of(parts[1]).astype(bf16)], axis=1
    )
    gathered = across(jnp.tile(shard, (chips, 1)))
    high = gathered[:, 0:channels]
    projected = lax.dot_general(
        gathered[:, channels : channels + vectors], high, TN, preferred_element_type=f32
    )
    lines = jnp.zeros((LINES * 128,), i32).at[0 : hits.shape[0]].set(hits).reshape(LINES, 128)
    digits = [((lines >> (8 * k)) & 255).astype(bf16) for k in range(3)]
    message = jnp.concatenate([high, projected.astype(bf16), *digits], axis=0)
    from_batch = [message] + [
        lax.ppermute(message, "batch", [(i, (i + k) % members) for i in range(members)])
        for k in range(1, members)
    ]
    from_other = [lax.ppermute(one, "centers", swap) for one in from_batch]
    return finish(eigen_scale, vectors_t, vectors_low, coeffs, from_batch, from_other)


def solution(mesh):
    chips = mesh.shape["centers"] // 2
    groups = [[2 * chip + core for chip in range(chips)] for core in range(2)]
    return jax.shard_map(
        functools.partial(body, groups=groups),
        mesh=mesh,
        in_specs=(
            P("centers", None),
            P("centers", None),
            P("centers", None),
            P("batch"),
            P("centers"),
            P(None, "centers"),
            P(),
        ),
        out_specs=(P("centers", None), P("batch", None)),
        check_vma=False,
    )
```

```python
import functools

import jax
import jax.numpy as jnp
from jax import lax
from jax.experimental import pallas as pl
from jax.experimental.pallas import tpu as pltpu
from jax.sharding import PartitionSpec as P

spread = 1.0
step_size = 0.5
NT = (((1,), (1,)), ((), ()))
TN = (((0,), (0,)), ((), ()))
bf16 = jnp.bfloat16
f32 = jnp.float32
i32 = jnp.int32
LINES = 16
SIDE = 4
LOG2_E = 1.4426950408889634


def split_two(values):
    high = values.astype(bf16)
    return high, (values - high.astype(f32)).astype(bf16)


def split_rounded(values):
    high = lax.reduce_precision(values, 8, 7)
    return high.astype(bf16), (values - high).astype(bf16)


def total_of(parts):
    return functools.reduce(jnp.add, [parts[k] for k in range(parts.shape[0])])


def next_hits(index, offset, count):
    rows = index.shape[0]
    total = rows * 128
    lane = lax.broadcasted_iota(i32, (rows, 128), 1)
    sub = lax.broadcasted_iota(i32, (rows, 128), 0)
    local = index - offset
    found = jnp.where((local >= 0) & (local < count), sub * 128 + lane, total)
    shift = 1
    while shift < 128:
        moved = pltpu.roll(found, 128 - shift, 1)
        found = jnp.minimum(found, jnp.where(lane < 128 - shift, moved, total))
        shift *= 2
    later = jnp.broadcast_to(found[:, 0:1], (rows, 128))
    later = jnp.where(sub < rows - 1, pltpu.roll(later, rows - 1, 0), total)
    shift = 1
    while shift < rows:
        moved = pltpu.roll(later, rows - shift, 0)
        later = jnp.minimum(later, jnp.where(sub < rows - shift, moved, total))
        shift *= 2
    return jnp.minimum(found, later)


def following(nxt, pos, total):
    after = jnp.minimum(pos + 1, total - 1)
    return jnp.where(pos + 1 < total, nxt[after >> 7, after & 127], total)


def pick_kernel(
    index, centers, mine, other, nxt, index_s, index_v, nxt_v, all_centers, wide, rows, sems, *, sides
):
    total = rows.shape[0]
    half = total // 2
    shard = half // (sides[0] * sides[1])
    count = centers.shape[0]
    position = lax.axis_index("centers")
    offset = position * count
    core = position & 1
    first = (position >> 1) // sides[1]
    to_vector = pltpu.make_async_copy(index, index_v, sems.at[2])
    to_vector.start()
    to_scalar = pltpu.make_async_copy(index, index_s, sems.at[3])
    to_scalar.start()
    load = pltpu.make_async_copy(centers, all_centers, sems.at[0])
    load.start()
    rows[...] = jnp.zeros_like(rows)
    to_vector.wait()
    nxt_v[...] = next_hits(index_v[...], offset, count)
    copy = pltpu.make_async_copy(nxt_v, nxt, sems.at[1])
    copy.start()
    to_scalar.wait()
    copy.wait()
    load.wait()

    shard_bits = shard.bit_length() - 1
    second_bits = sides[1].bit_length() - 1
    half_bits = half.bit_length() - 1

    def take(pos):
        after = following(nxt, pos, total)
        local = index_s[pos >> 7, pos & 127] - offset
        tile = pl.ds(pl.multiple_of((local >> 4) << 4, 16), 16)
        chip = (pos >> shard_bits) & (sides[0] * sides[1] - 1)
        along = ((chip >> second_bits) - first) & (sides[0] - 1)
        across = chip & (sides[1] - 1)
        place = (((along << second_bits) | across) << shard_bits) | (pos & (shard - 1))
        spot = (((pos >> half_bits) ^ core) << half_bits) | place
        wide[...] = all_centers[tile, :].astype(f32)
        rows[pl.ds(spot, 1), :] = wide[pl.ds(local & 15, 1), :]
        return after

    lax.while_loop(lambda pos: pos < total, take, nxt[0, 0])
    mine[...] = rows[0:half, :].astype(bf16)
    other[...] = rows[half:total, :].astype(bf16)


def pick(index, centers, sides):
    total = index.shape[0]
    width = centers.shape[1]
    vmem = pl.BlockSpec(memory_space=pltpu.VMEM)
    smem = pl.BlockSpec(memory_space=pltpu.SMEM)
    hbm = pl.BlockSpec(memory_space=pltpu.HBM)
    return pl.pallas_call(
        functools.partial(pick_kernel, sides=sides),
        name="pick",
        in_specs=[hbm, hbm],
        out_specs=[vmem, vmem, smem],
        out_shape=[
            jax.ShapeDtypeStruct((total // 2, width), bf16),
            jax.ShapeDtypeStruct((total // 2, width), bf16),
            jax.ShapeDtypeStruct((total // 128, 128), i32),
        ],
        scratch_shapes=[
            pltpu.SMEM((total // 128, 128), i32),
            pltpu.VMEM((total // 128, 128), i32),
            pltpu.VMEM((total // 128, 128), i32),
            pltpu.VMEM(centers.shape, bf16),
            pltpu.VMEM((16, width), f32),
            pltpu.VMEM((total, width), f32),
            pltpu.SemaphoreType.DMA((4,)),
        ],
        compiler_params=pltpu.CompilerParams(vmem_limit_bytes=50 * 2**20),
        cost_estimate=pl.CostEstimate(flops=0, bytes_accessed=14 * 2**20, transcendentals=0),
    )(index.reshape(total // 128, 128), centers)


def prepare_kernel(subset, eigvec, high, low, wide):
    step = pl.program_id(0)
    vectors, count = eigvec.shape
    block = high.shape[0]

    @pl.when(step == 0)
    def _():
        offset = lax.axis_index("centers") * wide.shape[0]
        wide[...] = jnp.zeros_like(wide)

        def put(group, _):
            start = pl.multiple_of(group * 128, 128)
            turned = eigvec[:, pl.ds(start, 128)].T
            for eight in range(0, 128, 8):
                spots = [subset[start + eight + one] - offset for one in range(8)]
                for one in range(8):
                    wide[pl.ds(spots[one], 1), 0:vectors] = turned[eight + one : eight + one + 1, :]
            return 0

        lax.fori_loop(0, count // 128, put, 0)

    span = pl.ds(pl.multiple_of(step * block, block), block)
    high[...], low[...] = split_two(wide[span, 0:vectors])


def prepare(subset, eigvec, centers):
    vectors, count = eigvec.shape
    block = 2048
    lanes = -(-vectors // 128) * 128
    part = pl.BlockSpec((block, vectors), lambda i: (i, 0))
    return pl.pallas_call(
        prepare_kernel,
        name="prepare",
        grid=(centers // block,),
        in_specs=[
            pl.BlockSpec(memory_space=pltpu.SMEM),
            pl.BlockSpec((vectors, count), lambda i: (0, 0)),
        ],
        out_specs=[part, part],
        out_shape=[jax.ShapeDtypeStruct((centers, vectors), bf16)] * 2,
        scratch_shapes=[pltpu.VMEM((centers, lanes), f32)],
        compiler_params=pltpu.CompilerParams(vmem_limit_bytes=20 * 2**20),
        cost_estimate=pl.CostEstimate(flops=0, bytes_accessed=24 * 2**20, transcendentals=0),
    )(subset, eigvec)


def note_kernel(index_s, nxt, targets, hits, labels, all_targets, wide, sem):
    total = index_s.shape[0]
    count = targets.shape[0]
    position = lax.axis_index("centers")
    offset = position * count
    turn = (position & 1) * (total // 2)
    load = pltpu.make_async_copy(targets, all_targets, sem)
    load.start()
    labels[...] = jnp.zeros_like(labels)
    load.wait()

    def note(state):
        number, pos = state
        after = following(nxt, pos, total)
        local = index_s[pos] - offset
        hits[number] = pos * count + local
        tile = pl.ds(pl.multiple_of((local >> 4) << 4, 16), 16)
        wide[...] = all_targets[tile, :].astype(f32)
        labels[pl.ds(pos ^ turn, 1), :] = wide[pl.ds(local & 15, 1), :]
        return number + 1, after

    number, _ = lax.while_loop(lambda s: s[1] < total, note, (jnp.int32(1), nxt[0, 0]))
    hits[0] = number - 1


def note(index, nxt, targets):
    total, channels = index.shape[0], targets.shape[1]
    smem = pl.BlockSpec(memory_space=pltpu.SMEM)
    return pl.pallas_call(
        note_kernel,
        name="note",
        in_specs=[smem, smem, pl.BlockSpec(memory_space=pl.ANY)],
        out_specs=[smem, pl.BlockSpec(memory_space=pltpu.VMEM)],
        out_shape=[
            jax.ShapeDtypeStruct((total + 128,), i32),
            jax.ShapeDtypeStruct((total, channels), f32),
        ],
        scratch_shapes=[
            pltpu.VMEM(targets.shape, bf16),
            pltpu.VMEM((16, channels), f32),
            pltpu.SemaphoreType.DMA,
        ],
        compiler_params=pltpu.CompilerParams(vmem_limit_bytes=8 * 2**20),
        cost_estimate=pl.CostEstimate(flops=0, bytes_accessed=6 * 2**20, transcendentals=0),
    )(index, nxt, targets)


def main_kernel(
    all_centers, coeffs, vectors_t, labels, *refs, part, pieces
):
    rows_mine, rows_other, refs = refs[:pieces], refs[pieces : 2 * pieces], refs[2 * pieces :]
    mine, other, turned, norms, total, blocks, sems = refs
    step = pl.program_id(0)
    block = blocks.shape[1]
    slot = step & 1

    def load(step, slot):
        span = pl.ds(pl.multiple_of(step * block, block), block)
        return pltpu.make_async_copy(all_centers.at[span, :], blocks.at[slot], sems.at[slot])

    @pl.when(step == 0)
    def _():
        load(step, slot).start()

    @pl.when(step + 1 < pl.num_programs(0))
    def _():
        load(step + 1, 1 - slot).start()

    size = rows_mine[0].shape[0]
    half = size * pieces
    channels = labels.shape[1]
    vectors = vectors_t.shape[1]

    @pl.when(step == 0)
    def _():
        ones = jnp.ones((8, blocks.shape[2]), bf16)
        for number, rows in enumerate((*rows_mine, *rows_other)):
            span = slice(number * size, (number + 1) * size)
            values = rows[...]
            high, low = split_two(jnp.square(values.astype(f32)))
            norms[:, span] = (
                lax.dot_general(ones, high, NT, preferred_element_type=f32)
                + lax.dot_general(ones, low, NT, preferred_element_type=f32)
                + 0.001
            )
            turned[:, span] = (values * jnp.asarray(-2.0, bf16)).T
        total[...] = jnp.zeros_like(total)

    load(step, slot).wait()
    centers = blocks.at[slot]
    spots = list(range(0, block, part))

    def products(start):
        block = centers[start : start + part, :]
        own = jnp.sum(jnp.square(block.astype(f32)), axis=1, keepdims=True)
        return own, jnp.dot(block, turned[...], preferred_element_type=f32)

    def add(start, kernel):
        span = slice(start, start + part)
        columns = jnp.concatenate([coeffs[span, :].astype(bf16), vectors_t[span, :]], axis=1)
        total[...] += lax.dot_general(columns, kernel, TN, preferred_element_type=f32)

    ahead = products(spots[0])
    for number, start in enumerate(spots):
        own, prods = ahead
        if number + 1 < len(spots):
            ahead = products(spots[number + 1])
        distance = jnp.maximum(prods + (own + norms[0:1, :]), 0.001)
        kernel = jnp.exp2(distance * lax.rsqrt(distance) * (-LOG2_E / spread)).astype(bf16)
        if number > 0:
            add(*late)
        late = (start, kernel)
    add(*late)

    @pl.when(step == pl.num_programs(0) - 1)
    def _():
        chip = (lax.axis_index("centers") >> 1) // SIDE
        for start, out in ((0, mine), (half, other)):
            out[:, 2 * channels :] = jnp.zeros((half, out.shape[1] - 2 * channels), bf16)
            for k in range(pieces):
                span = slice(start + k * size, start + (k + 1) * size)
                place = pl.multiple_of(((chip - k) & (pieces - 1)) * size, size)
                to = pl.ds(place, size)
                partial = total[0:channels, span].T - labels[pl.ds(start + place, size), :]
                high, low = split_two(partial)
                out[to, 0:channels] = high
                out[to, channels : 2 * channels] = low
                out[to, 2 * channels : 2 * channels + vectors] = total[channels:, span].T.astype(bf16)


def main(centers, coeffs, vectors_t, rows_mine, rows_other, labels):
    count, width = centers.shape
    pieces, size, channels = len(rows_mine), rows_mine[0].shape[0], labels.shape[1]
    half = pieces * size
    columns = channels + vectors_t.shape[1]
    block, part = 2048, 512
    whole = lambda shape: pl.BlockSpec(shape, lambda i: (0, 0))
    return pl.pallas_call(
        functools.partial(main_kernel, part=part, pieces=pieces),
        name="kernel_sums",
        grid=(count // block,),
        in_specs=[
            pl.BlockSpec(memory_space=pltpu.HBM),
            pl.BlockSpec((block, channels), lambda i: (i, 0)),
            pl.BlockSpec((block, vectors_t.shape[1]), lambda i: (i, 0)),
            whole((2 * half, channels)),
        ]
        + [whole((size, width))] * (2 * pieces),
        out_specs=[whole((half, 512)), whole((half, 512))],
        out_shape=[jax.ShapeDtypeStruct((half, 512), bf16)] * 2,
        scratch_shapes=[
            pltpu.VMEM((width, 2 * half), bf16),
            pltpu.VMEM((8, 2 * half), f32),
            pltpu.VMEM((columns, 2 * half), f32),
            pltpu.VMEM((2, block, width), bf16),
            pltpu.SemaphoreType.DMA((2,)),
        ],
        compiler_params=pltpu.CompilerParams(vmem_limit_bytes=38 * 2**20),
        cost_estimate=pl.CostEstimate(
            flops=2 * count * 2 * half * (width + columns),
            bytes_accessed=20 * 2**20,
            transcendentals=2 * count * 2 * half,
        ),
    )(centers, coeffs, vectors_t, labels, *rows_mine, *rows_other)


def finish_kernel(scale, high, low, coeffs, *refs, members):
    mine, other, refs = refs[:members], refs[members : 2 * members], refs[2 * members :]
    updated, residual, all_rows, weights, codes_v, codes, sem = refs
    step = pl.program_id(0)
    channels = coeffs.shape[1]
    half = residual.shape[0] // 2
    vectors = scale.shape[1]
    block = coeffs.shape[0]
    count = updated.shape[0]
    listed = half + vectors
    lines = codes.shape[0] // members
    copy = pltpu.make_async_copy(codes_v, codes, sem)

    @pl.when(step == 0)
    def _():
        core = lax.axis_index("centers") & 1
        first = (
            lax.broadcasted_iota(i32, (lines, 128), 0) + lax.broadcasted_iota(i32, (lines, 128), 1) == 0
        )
        for member in range(members):
            digits = [
                mine[member][listed + k * lines : listed + (k + 1) * lines, :].astype(f32)
                for k in range(3)
            ]
            code = (digits[0] + 256.0 * digits[1] + 65536.0 * digits[2]).astype(i32)
            local = code & (count - 1)
            pos = code >> (count.bit_length() - 1)
            side = (pos >> (half.bit_length() - 1)) ^ core
            source = (side * members + member) * half + (pos & (half - 1))
            codes_v[member * lines : (member + 1) * lines, :] = jnp.where(
                first, code, (source << 16) + local
            )
        copy.start()
        projected = jnp.zeros((vectors, channels), f32)
        for side, part in enumerate((mine, other)):
            for member in range(members):
                start = (side * members + member) * half
                all_rows[start : start + half, :] = part[member][0:half, :].astype(f32) * -step_size
                projected += part[member][half : half + vectors, :].astype(f32)
        scales = jnp.broadcast_to(scale[...], (channels, vectors)).T
        top, rest = split_two(projected * scales * step_size)
        weights[:, 0:channels] = top
        weights[:, channels:] = rest
        for side, part in enumerate((mine, other)):
            start = pl.multiple_of((core ^ side) * half, half)
            residual[pl.ds(start, half), :] = part[0][0:half, :].astype(f32)

    correction = jnp.dot(high[...], weights[...], preferred_element_type=f32)
    correction_low = jnp.dot(low[...], weights[:, 0:channels], preferred_element_type=f32)
    span = pl.ds(pl.multiple_of(step * block, block), block)
    updated[span, :] = coeffs[...] + (
        correction[:, 0:channels] + (correction[:, channels:] + correction_low)
    )

    @pl.when(step == pl.num_programs(0) - 1)
    def _():
        copy.wait()
        for member in range(members):
            base = member * lines

            def add(numbers):
                found = [codes[base + (k >> 7), k & 127] for k in numbers]
                changes = [all_rows[pl.ds(code >> 16, 1), :] for code in found]
                for code, change in zip(found, changes):
                    local = pl.ds(code & 65535, 1)
                    updated[local, :] = updated[local, :] + change

            def eight(group, _):
                add([group * 8 + one for one in range(1, 9)])
                return 0

            def single(k, _):
                add([k])
                return 0

            number = codes[base, 0]
            eights = number >> 3
            lax.fori_loop(0, eights, eight, 0)
            lax.fori_loop(eights * 8 + 1, number + 1, single, 0)


def finish(scale, high, low, coeffs, mine, other):
    count, channels = coeffs.shape
    vectors = scale.shape[0]
    members = len(mine)
    lines = LINES
    half = mine[0].shape[0] - vectors - 3 * lines
    block = 2048
    whole = lambda shape: pl.BlockSpec(shape, lambda i: (0,) * len(shape))
    return pl.pallas_call(
        functools.partial(finish_kernel, members=members),
        name="finish",
        grid=(count // block,),
        in_specs=[
            whole((1, vectors)),
            pl.BlockSpec((block, vectors), lambda i: (i, 0)),
            pl.BlockSpec((block, vectors), lambda i: (i, 0)),
            pl.BlockSpec((block, channels), lambda i: (i, 0)),
        ]
        + [whole(one.shape) for one in (*mine, *other)],
        out_specs=[whole((count, channels)), whole((2 * half, channels))],
        out_shape=[
            jax.ShapeDtypeStruct((count, channels), f32),
            jax.ShapeDtypeStruct((2 * half, channels), f32),
        ],
        scratch_shapes=[
            pltpu.VMEM((2 * members * half, channels), f32),
            pltpu.VMEM((vectors, 2 * channels), bf16),
            pltpu.VMEM((members * lines, 128), i32),
            pltpu.SMEM((members * lines, 128), i32),
            pltpu.SemaphoreType.DMA,
        ],
        compiler_params=pltpu.CompilerParams(vmem_limit_bytes=24 * 2**20),
        cost_estimate=pl.CostEstimate(flops=10**9, bytes_accessed=14 * 2**20, transcendentals=0),
    )(scale.reshape(1, vectors), high, low, coeffs, *mine, *other)


def body(centers, coeffs, targets, batch_index, subset_index, eigvec, eigen_scale, *, groups):
    count = centers.shape[0]
    channels = coeffs.shape[1]
    vectors = eigvec.shape[0]
    members = lax.axis_size("batch")
    half = batch_index.shape[0] // 2
    chips = len(groups[0])
    sides = (chips // SIDE, SIDE)
    swap = [(i, i ^ 1) for i in range(2 * chips)]

    def across(values):
        return lax.all_to_all(
            values, "centers", 0, 0, tiled=True, axis_index_groups=groups
        )

    def ahead(values, axis, k):
        pairs = []
        for chip in range(chips):
            place = [chip // SIDE, chip % SIDE]
            place[axis] = (place[axis] + k) % sides[axis]
            target = place[0] * SIDE + place[1]
            pairs += [(2 * chip + core, 2 * target + core) for core in range(2)]
        return lax.ppermute(values, "centers", pairs)

    def cut(values, parts):
        size = values.shape[0] // parts
        return [values[k * size : (k + 1) * size] for k in range(parts)]

    mine, other, nxt = pick(batch_index, centers, sides)
    summed = mine + lax.ppermute(other, "centers", swap)
    summed, eigvec = lax.optimization_barrier((summed, eigvec))
    vectors_t, vectors_low = prepare(subset_index, eigvec, count)
    pieces = cut(summed, sides[0])
    row_sums = functools.reduce(
        jnp.add, [pieces[0]] + [ahead(pieces[k], 0, k) for k in range(1, sides[0])]
    )
    row_sums, vectors_t, vectors_low = lax.optimization_barrier((row_sums, vectors_t, vectors_low))
    own_rows = functools.reduce(
        jnp.add, [row_sums] + [ahead(row_sums, 1, k) for k in range(1, sides[1])]
    )
    rows_mine = [own_rows] + [ahead(own_rows, 0, k) for k in range(1, sides[0])]
    rows_other = [lax.ppermute(one, "centers", swap) for one in rows_mine]

    hits, labels = note(batch_index, nxt, targets)
    sums_mine, sums_other = main(centers, coeffs, vectors_t, rows_mine, rows_other, labels)

    def widened(values):
        values = values.astype(f32)
        return values[..., 0:channels] + values[..., channels : 2 * channels], values[..., 2 * channels :]

    def packed(residual, rest):
        high, low = split_rounded(residual)
        return jnp.concatenate([high, low, rest.astype(bf16)], axis=-1)

    first = widened(sums_mine)
    second = widened(lax.ppermute(sums_other, "centers", swap))
    chip_sums = packed(first[0] + second[0], first[1] + second[1])
    parts = widened(across(chip_sums).reshape(chips, half // chips, -1))
    shard = jnp.concatenate(
        [total_of(parts[0]).astype(bf16), total_of(parts[1]).astype(bf16)], axis=1
    )
    gathered = across(jnp.tile(shard, (chips, 1)))
    high = gathered[:, 0:channels]
    projected = lax.dot_general(
        gathered[:, channels : channels + vectors], high, TN, preferred_element_type=f32
    )
    lines = jnp.zeros((LINES * 128,), i32).at[0 : hits.shape[0]].set(hits).reshape(LINES, 128)
    digits = [((lines >> (8 * k)) & 255).astype(bf16) for k in range(3)]
    message = jnp.concatenate([high, projected.astype(bf16), *digits], axis=0)
    from_batch = [message] + [
        lax.ppermute(message, "batch", [(i, (i + k) % members) for i in range(members)])
        for k in range(1, members)
    ]
    from_other = [lax.ppermute(one, "centers", swap) for one in from_batch]
    return finish(eigen_scale, vectors_t, vectors_low, coeffs, from_batch, from_other)


def solution(mesh):
    chips = mesh.shape["centers"] // 2
    groups = [[2 * chip + core for chip in range(chips)] for core in range(2)]
    return jax.shard_map(
        functools.partial(body, groups=groups),
        mesh=mesh,
        in_specs=(
            P("centers", None),
            P("centers", None),
            P("centers", None),
            P("batch"),
            P("centers"),
            P(None, "centers"),
            P(),
        ),
        out_specs=(P("centers", None), P("batch", None)),
        check_vma=False,
    )
```

```python
import functools

import jax
import jax.numpy as jnp
from jax import lax
from jax.experimental import pallas as pl
from jax.experimental.pallas import tpu as pltpu
from jax.sharding import PartitionSpec as P

spread = 1.0
step_size = 0.5
NT = (((1,), (1,)), ((), ()))
TN = (((0,), (0,)), ((), ()))
bf16 = jnp.bfloat16
f32 = jnp.float32
i32 = jnp.int32
LINES = 16
LOG2_E = 1.4426950408889634


def split_two(values):
    high = values.astype(bf16)
    return high, (values - high.astype(f32)).astype(bf16)


def split_rounded(values):
    high = lax.reduce_precision(values, 8, 7)
    return high.astype(bf16), (values - high).astype(bf16)


def total_of(parts):
    return functools.reduce(jnp.add, [parts[k] for k in range(parts.shape[0])])


def next_hits(index, offset, count):
    rows = index.shape[0]
    total = rows * 128
    lane = lax.broadcasted_iota(i32, (rows, 128), 1)
    sub = lax.broadcasted_iota(i32, (rows, 128), 0)
    local = index - offset
    found = jnp.where((local >= 0) & (local < count), sub * 128 + lane, total)
    shift = 1
    while shift < 128:
        moved = pltpu.roll(found, 128 - shift, 1)
        found = jnp.minimum(found, jnp.where(lane < 128 - shift, moved, total))
        shift *= 2
    later = jnp.broadcast_to(found[:, 0:1], (rows, 128))
    later = jnp.where(sub < rows - 1, pltpu.roll(later, rows - 1, 0), total)
    shift = 1
    while shift < rows:
        moved = pltpu.roll(later, rows - shift, 0)
        later = jnp.minimum(later, jnp.where(sub < rows - shift, moved, total))
        shift *= 2
    return jnp.minimum(found, later)


def following(nxt, pos, total):
    after = jnp.minimum(pos + 1, total - 1)
    return jnp.where(pos + 1 < total, nxt[after >> 7, after & 127], total)


def pick_kernel(
    index, centers, mine, other, nxt, index_s, index_v, nxt_v, all_centers, wide, rows, sems, *, sides
):
    total = rows.shape[0]
    half = total // 2
    shard = half // (sides[0] * sides[1])
    count = centers.shape[0]
    position = lax.axis_index("centers")
    offset = position * count
    core = position & 1
    first, second = (position >> 1) // sides[1], (position >> 1) & (sides[1] - 1)
    to_vector = pltpu.make_async_copy(index, index_v, sems.at[2])
    to_vector.start()
    to_scalar = pltpu.make_async_copy(index, index_s, sems.at[3])
    to_scalar.start()
    load = pltpu.make_async_copy(centers, all_centers, sems.at[0])
    load.start()
    rows[...] = jnp.zeros_like(rows)
    to_vector.wait()
    nxt_v[...] = next_hits(index_v[...], offset, count)
    copy = pltpu.make_async_copy(nxt_v, nxt, sems.at[1])
    copy.start()
    to_scalar.wait()
    copy.wait()
    load.wait()

    shard_bits = shard.bit_length() - 1
    second_bits = sides[1].bit_length() - 1
    half_bits = half.bit_length() - 1

    def take(pos):
        after = following(nxt, pos, total)
        local = index_s[pos >> 7, pos & 127] - offset
        tile = pl.ds(pl.multiple_of((local >> 4) << 4, 16), 16)
        chip = (pos >> shard_bits) & (sides[0] * sides[1] - 1)
        along = ((chip >> second_bits) - first) & (sides[0] - 1)
        across = ((chip & (sides[1] - 1)) - second) & (sides[1] - 1)
        place = (((along << second_bits) | across) << shard_bits) | (pos & (shard - 1))
        spot = (((pos >> half_bits) ^ core) << half_bits) | place
        wide[...] = all_centers[tile, :].astype(f32)
        rows[pl.ds(spot, 1), :] = wide[pl.ds(local & 15, 1), :]
        return after

    lax.while_loop(lambda pos: pos < total, take, nxt[0, 0])
    mine[...] = rows[0:half, :].astype(bf16)
    other[...] = rows[half:total, :].astype(bf16)


def pick(index, centers, sides):
    total = index.shape[0]
    width = centers.shape[1]
    vmem = pl.BlockSpec(memory_space=pltpu.VMEM)
    smem = pl.BlockSpec(memory_space=pltpu.SMEM)
    hbm = pl.BlockSpec(memory_space=pltpu.HBM)
    return pl.pallas_call(
        functools.partial(pick_kernel, sides=sides),
        name="pick",
        in_specs=[hbm, hbm],
        out_specs=[vmem, vmem, smem],
        out_shape=[
            jax.ShapeDtypeStruct((total // 2, width), bf16),
            jax.ShapeDtypeStruct((total // 2, width), bf16),
            jax.ShapeDtypeStruct((total // 128, 128), i32),
        ],
        scratch_shapes=[
            pltpu.SMEM((total // 128, 128), i32),
            pltpu.VMEM((total // 128, 128), i32),
            pltpu.VMEM((total // 128, 128), i32),
            pltpu.VMEM(centers.shape, bf16),
            pltpu.VMEM((16, width), f32),
            pltpu.VMEM((total, width), f32),
            pltpu.SemaphoreType.DMA((4,)),
        ],
        compiler_params=pltpu.CompilerParams(vmem_limit_bytes=50 * 2**20),
        cost_estimate=pl.CostEstimate(flops=0, bytes_accessed=14 * 2**20, transcendentals=0),
    )(index.reshape(total // 128, 128), centers)


def prepare_kernel(subset, eigvec, high, low, wide):
    step = pl.program_id(0)
    vectors, count = eigvec.shape
    block = high.shape[0]

    @pl.when(step == 0)
    def _():
        offset = lax.axis_index("centers") * wide.shape[0]
        wide[...] = jnp.zeros_like(wide)

        def put(group, _):
            start = pl.multiple_of(group * 128, 128)
            turned = eigvec[:, pl.ds(start, 128)].T
            for eight in range(0, 128, 8):
                spots = [subset[start + eight + one] - offset for one in range(8)]
                for one in range(8):
                    wide[pl.ds(spots[one], 1), 0:vectors] = turned[eight + one : eight + one + 1, :]
            return 0

        lax.fori_loop(0, count // 128, put, 0)

    span = pl.ds(pl.multiple_of(step * block, block), block)
    high[...], low[...] = split_two(wide[span, 0:vectors])


def prepare(subset, eigvec, centers):
    vectors, count = eigvec.shape
    block = 2048
    lanes = -(-vectors // 128) * 128
    part = pl.BlockSpec((block, vectors), lambda i: (i, 0))
    return pl.pallas_call(
        prepare_kernel,
        name="prepare",
        grid=(centers // block,),
        in_specs=[
            pl.BlockSpec(memory_space=pltpu.SMEM),
            pl.BlockSpec((vectors, count), lambda i: (0, 0)),
        ],
        out_specs=[part, part],
        out_shape=[jax.ShapeDtypeStruct((centers, vectors), bf16)] * 2,
        scratch_shapes=[pltpu.VMEM((centers, lanes), f32)],
        compiler_params=pltpu.CompilerParams(vmem_limit_bytes=20 * 2**20),
        cost_estimate=pl.CostEstimate(flops=0, bytes_accessed=24 * 2**20, transcendentals=0),
    )(subset, eigvec)


def note_kernel(index_s, nxt, targets, hits, labels, all_targets, wide, sem):
    total = index_s.shape[0]
    count = targets.shape[0]
    position = lax.axis_index("centers")
    offset = position * count
    turn = (position & 1) * (total // 2)
    load = pltpu.make_async_copy(targets, all_targets, sem)
    load.start()
    labels[...] = jnp.zeros_like(labels)
    load.wait()

    def note(state):
        number, pos = state
        after = following(nxt, pos, total)
        local = index_s[pos] - offset
        hits[number] = pos * count + local
        tile = pl.ds(pl.multiple_of((local >> 4) << 4, 16), 16)
        wide[...] = all_targets[tile, :].astype(f32)
        labels[pl.ds(pos ^ turn, 1), :] = wide[pl.ds(local & 15, 1), :]
        return number + 1, after

    number, _ = lax.while_loop(lambda s: s[1] < total, note, (jnp.int32(1), nxt[0, 0]))
    hits[0] = number - 1


def note(index, nxt, targets):
    total, channels = index.shape[0], targets.shape[1]
    smem = pl.BlockSpec(memory_space=pltpu.SMEM)
    return pl.pallas_call(
        note_kernel,
        name="note",
        in_specs=[smem, smem, pl.BlockSpec(memory_space=pl.ANY)],
        out_specs=[smem, pl.BlockSpec(memory_space=pltpu.VMEM)],
        out_shape=[
            jax.ShapeDtypeStruct((total + 128,), i32),
            jax.ShapeDtypeStruct((total, channels), f32),
        ],
        scratch_shapes=[
            pltpu.VMEM(targets.shape, bf16),
            pltpu.VMEM((16, channels), f32),
            pltpu.SemaphoreType.DMA,
        ],
        compiler_params=pltpu.CompilerParams(vmem_limit_bytes=8 * 2**20),
        cost_estimate=pl.CostEstimate(flops=0, bytes_accessed=6 * 2**20, transcendentals=0),
    )(index, nxt, targets)


def main_kernel(
    all_centers, coeffs, vectors_t, rows_mine, rows_other, labels, mine, other,
    turned, norms, total, blocks, sems, *, part,
):
    step = pl.program_id(0)
    block = blocks.shape[1]
    slot = step & 1

    def load(step, slot):
        span = pl.ds(pl.multiple_of(step * block, block), block)
        return pltpu.make_async_copy(all_centers.at[span, :], blocks.at[slot], sems.at[slot])

    @pl.when(step == 0)
    def _():
        load(step, slot).start()

    @pl.when(step + 1 < pl.num_programs(0))
    def _():
        load(step + 1, 1 - slot).start()

    half = rows_mine.shape[0]
    channels = labels.shape[1]
    vectors = vectors_t.shape[1]

    @pl.when(step == 0)
    def _():
        ones = jnp.ones((8, rows_mine.shape[1]), bf16)
        for start, rows in ((0, rows_mine), (half, rows_other)):
            span = slice(start, start + half)
            values = rows[...]
            high, low = split_two(jnp.square(values.astype(f32)))
            norms[:, span] = (
                lax.dot_general(ones, high, NT, preferred_element_type=f32)
                + lax.dot_general(ones, low, NT, preferred_element_type=f32)
                + 0.001
            )
            turned[:, span] = (values * jnp.asarray(-2.0, bf16)).T
        total[...] = jnp.zeros_like(total)

    load(step, slot).wait()
    centers = blocks.at[slot]
    spots = list(range(0, block, part))

    def products(start):
        block = centers[start : start + part, :]
        own = jnp.sum(jnp.square(block.astype(f32)), axis=1, keepdims=True)
        return own, jnp.dot(block, turned[...], preferred_element_type=f32)

    def add(start, kernel):
        span = slice(start, start + part)
        columns = jnp.concatenate([coeffs[span, :].astype(bf16), vectors_t[span, :]], axis=1)
        total[...] += lax.dot_general(columns, kernel, TN, preferred_element_type=f32)

    ahead = products(spots[0])
    for number, start in enumerate(spots):
        own, prods = ahead
        if number + 1 < len(spots):
            ahead = products(spots[number + 1])
        distance = jnp.maximum(prods + (own + norms[0:1, :]), 0.001)
        kernel = jnp.exp2(distance * lax.rsqrt(distance) * (-LOG2_E / spread)).astype(bf16)
        if number > 0:
            add(*late)
        late = (start, kernel)
    add(*late)

    @pl.when(step == pl.num_programs(0) - 1)
    def _():
        for start, out in ((0, mine), (half, other)):
            span = slice(start, start + half)
            partial = total[0:channels, span].T - labels[span, :]
            high, low = split_two(partial)
            out[:, 0:channels] = high
            out[:, channels : 2 * channels] = low
            out[:, 2 * channels :] = jnp.zeros((half, out.shape[1] - 2 * channels), bf16)
            out[:, 2 * channels : 2 * channels + vectors] = total[channels:, span].T.astype(bf16)


def main(centers, coeffs, vectors_t, rows_mine, rows_other, labels):
    count, width = centers.shape
    half, channels = rows_mine.shape[0], labels.shape[1]
    columns = channels + vectors_t.shape[1]
    block, part = 2048, 512
    whole = lambda shape: pl.BlockSpec(shape, lambda i: (0, 0))
    return pl.pallas_call(
        functools.partial(main_kernel, part=part),
        name="kernel_sums",
        grid=(count // block,),
        in_specs=[
            pl.BlockSpec(memory_space=pltpu.HBM),
            pl.BlockSpec((block, channels), lambda i: (i, 0)),
            pl.BlockSpec((block, vectors_t.shape[1]), lambda i: (i, 0)),
            whole((half, width)),
            whole((half, width)),
            whole((2 * half, channels)),
        ],
        out_specs=[whole((half, 512)), whole((half, 512))],
        out_shape=[jax.ShapeDtypeStruct((half, 512), bf16)] * 2,
        scratch_shapes=[
            pltpu.VMEM((width, 2 * half), bf16),
            pltpu.VMEM((8, 2 * half), f32),
            pltpu.VMEM((columns, 2 * half), f32),
            pltpu.VMEM((2, block, width), bf16),
            pltpu.SemaphoreType.DMA((2,)),
        ],
        compiler_params=pltpu.CompilerParams(vmem_limit_bytes=38 * 2**20),
        cost_estimate=pl.CostEstimate(
            flops=2 * count * 2 * half * (width + columns),
            bytes_accessed=20 * 2**20,
            transcendentals=2 * count * 2 * half,
        ),
    )(centers, coeffs, vectors_t, rows_mine, rows_other, labels)


def finish_kernel(scale, high, low, coeffs, *refs, members):
    mine, other, refs = refs[:members], refs[members : 2 * members], refs[2 * members :]
    updated, residual, all_rows, weights, codes_v, codes, sem = refs
    step = pl.program_id(0)
    channels = coeffs.shape[1]
    half = residual.shape[0] // 2
    vectors = scale.shape[1]
    block = coeffs.shape[0]
    count = updated.shape[0]
    listed = half + vectors
    lines = codes.shape[0] // members
    copy = pltpu.make_async_copy(codes_v, codes, sem)

    @pl.when(step == 0)
    def _():
        core = lax.axis_index("centers") & 1
        first = (
            lax.broadcasted_iota(i32, (lines, 128), 0) + lax.broadcasted_iota(i32, (lines, 128), 1) == 0
        )
        for member in range(members):
            digits = [
                mine[member][listed + k * lines : listed + (k + 1) * lines, :].astype(f32)
                for k in range(3)
            ]
            code = (digits[0] + 256.0 * digits[1] + 65536.0 * digits[2]).astype(i32)
            local = code & (count - 1)
            pos = code >> (count.bit_length() - 1)
            side = (pos >> (half.bit_length() - 1)) ^ core
            source = (side * members + member) * half + (pos & (half - 1))
            codes_v[member * lines : (member + 1) * lines, :] = jnp.where(
                first, code, (source << 16) + local
            )
        copy.start()
        projected = jnp.zeros((vectors, channels), f32)
        for side, part in enumerate((mine, other)):
            for member in range(members):
                start = (side * members + member) * half
                all_rows[start : start + half, :] = part[member][0:half, :].astype(f32) * -step_size
                projected += part[member][half : half + vectors, :].astype(f32)
        scales = jnp.broadcast_to(scale[...], (channels, vectors)).T
        top, rest = split_two(projected * scales * step_size)
        weights[:, 0:channels] = top
        weights[:, channels:] = rest
        for side, part in enumerate((mine, other)):
            start = pl.multiple_of((core ^ side) * half, half)
            residual[pl.ds(start, half), :] = part[0][0:half, :].astype(f32)

    correction = jnp.dot(high[...], weights[...], preferred_element_type=f32)
    correction_low = jnp.dot(low[...], weights[:, 0:channels], preferred_element_type=f32)
    span = pl.ds(pl.multiple_of(step * block, block), block)
    updated[span, :] = coeffs[...] + (
        correction[:, 0:channels] + (correction[:, channels:] + correction_low)
    )

    @pl.when(step == pl.num_programs(0) - 1)
    def _():
        copy.wait()
        for member in range(members):
            base = member * lines

            def add(numbers):
                found = [codes[base + (k >> 7), k & 127] for k in numbers]
                changes = [all_rows[pl.ds(code >> 16, 1), :] for code in found]
                for code, change in zip(found, changes):
                    local = pl.ds(code & 65535, 1)
                    updated[local, :] = updated[local, :] + change

            def eight(group, _):
                add([group * 8 + one for one in range(1, 9)])
                return 0

            def single(k, _):
                add([k])
                return 0

            number = codes[base, 0]
            eights = number >> 3
            lax.fori_loop(0, eights, eight, 0)
            lax.fori_loop(eights * 8 + 1, number + 1, single, 0)


def finish(scale, high, low, coeffs, mine, other):
    count, channels = coeffs.shape
    vectors = scale.shape[0]
    members = len(mine)
    lines = LINES
    half = mine[0].shape[0] - vectors - 3 * lines
    block = 4096
    whole = lambda shape: pl.BlockSpec(shape, lambda i: (0,) * len(shape))
    return pl.pallas_call(
        functools.partial(finish_kernel, members=members),
        name="finish",
        grid=(count // block,),
        in_specs=[
            whole((1, vectors)),
            pl.BlockSpec((block, vectors), lambda i: (i, 0)),
            pl.BlockSpec((block, vectors), lambda i: (i, 0)),
            pl.BlockSpec((block, channels), lambda i: (i, 0)),
        ]
        + [whole(one.shape) for one in (*mine, *other)],
        out_specs=[whole((count, channels)), whole((2 * half, channels))],
        out_shape=[
            jax.ShapeDtypeStruct((count, channels), f32),
            jax.ShapeDtypeStruct((2 * half, channels), f32),
        ],
        scratch_shapes=[
            pltpu.VMEM((2 * members * half, channels), f32),
            pltpu.VMEM((vectors, 2 * channels), bf16),
            pltpu.VMEM((members * lines, 128), i32),
            pltpu.SMEM((members * lines, 128), i32),
            pltpu.SemaphoreType.DMA,
        ],
        compiler_params=pltpu.CompilerParams(vmem_limit_bytes=32 * 2**20),
        cost_estimate=pl.CostEstimate(flops=10**9, bytes_accessed=14 * 2**20, transcendentals=0),
    )(scale.reshape(1, vectors), high, low, coeffs, *mine, *other)


def body(centers, coeffs, targets, batch_index, subset_index, eigvec, eigen_scale, *, groups):
    count = centers.shape[0]
    channels = coeffs.shape[1]
    vectors = eigvec.shape[0]
    members = lax.axis_size("batch")
    half = batch_index.shape[0] // 2
    chips = len(groups[0])
    sides = (chips // 4, 4)
    swap = [(i, i ^ 1) for i in range(2 * chips)]

    def across(values):
        return lax.all_to_all(
            values, "centers", 0, 0, tiled=True, axis_index_groups=groups
        )

    def turned(blocks, axis):
        total = blocks[0]
        for k in range(1, len(blocks)):
            pairs = []
            for chip in range(chips):
                place = [chip // sides[1], chip % sides[1]]
                place[axis] = (place[axis] + k) % sides[axis]
                target = place[0] * sides[1] + place[1]
                pairs += [(2 * chip + core, 2 * target + core) for core in range(2)]
            total = total + lax.ppermute(blocks[k], "centers", pairs)
        return total

    def cut(values, parts):
        size = values.shape[0] // parts
        return [values[k * size : (k + 1) * size] for k in range(parts)]

    mine, other, nxt = pick(batch_index, centers, sides)
    summed = mine + lax.ppermute(other, "centers", swap)
    summed, eigvec = lax.optimization_barrier((summed, eigvec))
    vectors_t, vectors_low = prepare(subset_index, eigvec, count)
    row_sums = turned(cut(summed, sides[0]), 0)
    row_sums, vectors_t, vectors_low = lax.optimization_barrier((row_sums, vectors_t, vectors_low))
    shard = turned(cut(row_sums, sides[1]), 1)
    rows_mine = across(jnp.tile(shard, (chips, 1)))
    rows_other = lax.ppermute(rows_mine, "centers", swap)

    hits, labels = note(batch_index, nxt, targets)
    sums_mine, sums_other = main(centers, coeffs, vectors_t, rows_mine, rows_other, labels)

    def widened(values):
        values = values.astype(f32)
        return values[..., 0:channels] + values[..., channels : 2 * channels], values[..., 2 * channels :]

    def packed(residual, rest):
        high, low = split_rounded(residual)
        return jnp.concatenate([high, low, rest.astype(bf16)], axis=-1)

    first = widened(sums_mine)
    second = widened(lax.ppermute(sums_other, "centers", swap))
    chip_sums = packed(first[0] + second[0], first[1] + second[1])
    parts = widened(across(chip_sums).reshape(chips, half // chips, -1))
    shard = jnp.concatenate(
        [total_of(parts[0]).astype(bf16), total_of(parts[1]).astype(bf16)], axis=1
    )
    gathered = across(jnp.tile(shard, (chips, 1)))
    high = gathered[:, 0:channels]
    projected = lax.dot_general(
        gathered[:, channels : channels + vectors], high, TN, preferred_element_type=f32
    )
    lines = jnp.zeros((LINES * 128,), i32).at[0 : hits.shape[0]].set(hits).reshape(LINES, 128)
    digits = [((lines >> (8 * k)) & 255).astype(bf16) for k in range(3)]
    message = jnp.concatenate([high, projected.astype(bf16), *digits], axis=0)
    steps = sorted(range(1, members), key=lambda k: min(k, members - k))
    from_batch = [message] + [
        lax.ppermute(message, "batch", [(i, (i + k) % members) for i in range(members)])
        for k in steps
    ]
    from_other = [lax.ppermute(one, "centers", swap) for one in from_batch]
    return finish(eigen_scale, vectors_t, vectors_low, coeffs, from_batch, from_other)


def solution(mesh):
    chips = mesh.shape["centers"] // 2
    groups = [[2 * chip + core for chip in range(chips)] for core in range(2)]
    return jax.shard_map(
        functools.partial(body, groups=groups),
        mesh=mesh,
        in_specs=(
            P("centers", None),
            P("centers", None),
            P("centers", None),
            P("batch"),
            P("centers"),
            P(None, "centers"),
            P(),
        ),
        out_specs=(P("centers", None), P("batch", None)),
        check_vma=False,
    )
```

```python
import functools

import jax
import jax.numpy as jnp
from jax import lax
from jax.experimental import pallas as pl
from jax.experimental.pallas import tpu as pltpu
from jax.sharding import PartitionSpec as P

spread = 1.0
step_size = 0.5
NT = (((1,), (1,)), ((), ()))
TN = (((0,), (0,)), ((), ()))
bf16 = jnp.bfloat16
f32 = jnp.float32
i32 = jnp.int32
LINES = 16
LOG2_E = 1.4426950408889634


def split_two(values):
    high = values.astype(bf16)
    return high, (values - high.astype(f32)).astype(bf16)


def split_rounded(values):
    high = lax.reduce_precision(values, 8, 7)
    return high.astype(bf16), (values - high).astype(bf16)


def total_of(parts):
    return functools.reduce(jnp.add, [parts[k] for k in range(parts.shape[0])])


def next_hits(index, offset, count):
    rows = index.shape[0]
    total = rows * 128
    lane = lax.broadcasted_iota(i32, (rows, 128), 1)
    sub = lax.broadcasted_iota(i32, (rows, 128), 0)
    local = index - offset
    found = jnp.where((local >= 0) & (local < count), sub * 128 + lane, total)
    shift = 1
    while shift < 128:
        moved = pltpu.roll(found, 128 - shift, 1)
        found = jnp.minimum(found, jnp.where(lane < 128 - shift, moved, total))
        shift *= 2
    later = jnp.broadcast_to(found[:, 0:1], (rows, 128))
    later = jnp.where(sub < rows - 1, pltpu.roll(later, rows - 1, 0), total)
    shift = 1
    while shift < rows:
        moved = pltpu.roll(later, rows - shift, 0)
        later = jnp.minimum(later, jnp.where(sub < rows - shift, moved, total))
        shift *= 2
    return jnp.minimum(found, later)


def following(nxt, pos, total):
    after = jnp.minimum(pos + 1, total - 1)
    return jnp.where(pos + 1 < total, nxt[after >> 7, after & 127], total)


def pick_kernel(
    index, centers, mine, other, nxt, index_s, index_v, nxt_v, all_centers, wide, rows, sems, *, sides
):
    total = rows.shape[0]
    half = total // 2
    shard = half // (sides[0] * sides[1])
    count = centers.shape[0]
    position = lax.axis_index("centers")
    offset = position * count
    core = position & 1
    first, second = (position >> 1) // sides[1], (position >> 1) & (sides[1] - 1)
    to_vector = pltpu.make_async_copy(index, index_v, sems.at[2])
    to_vector.start()
    to_scalar = pltpu.make_async_copy(index, index_s, sems.at[3])
    to_scalar.start()
    load = pltpu.make_async_copy(centers, all_centers, sems.at[0])
    load.start()
    rows[...] = jnp.zeros_like(rows)
    to_vector.wait()
    nxt_v[...] = next_hits(index_v[...], offset, count)
    copy = pltpu.make_async_copy(nxt_v, nxt, sems.at[1])
    copy.start()
    to_scalar.wait()
    copy.wait()
    load.wait()

    shard_bits = shard.bit_length() - 1
    second_bits = sides[1].bit_length() - 1
    half_bits = half.bit_length() - 1

    def take(pos):
        after = following(nxt, pos, total)
        local = index_s[pos >> 7, pos & 127] - offset
        tile = pl.ds(pl.multiple_of((local >> 4) << 4, 16), 16)
        chip = (pos >> shard_bits) & (sides[0] * sides[1] - 1)
        along = ((chip >> second_bits) - first) & (sides[0] - 1)
        across = ((chip & (sides[1] - 1)) - second) & (sides[1] - 1)
        place = (((along << second_bits) | across) << shard_bits) | (pos & (shard - 1))
        spot = (((pos >> half_bits) ^ core) << half_bits) | place
        wide[...] = all_centers[tile, :].astype(f32)
        rows[pl.ds(spot, 1), :] = wide[pl.ds(local & 15, 1), :]
        return after

    lax.while_loop(lambda pos: pos < total, take, nxt[0, 0])
    mine[...] = rows[0:half, :].astype(bf16)
    other[...] = rows[half:total, :].astype(bf16)


def pick(index, centers, sides):
    total = index.shape[0]
    width = centers.shape[1]
    vmem = pl.BlockSpec(memory_space=pltpu.VMEM)
    smem = pl.BlockSpec(memory_space=pltpu.SMEM)
    hbm = pl.BlockSpec(memory_space=pltpu.HBM)
    return pl.pallas_call(
        functools.partial(pick_kernel, sides=sides),
        name="pick",
        in_specs=[hbm, hbm],
        out_specs=[vmem, vmem, smem],
        out_shape=[
            jax.ShapeDtypeStruct((total // 2, width), bf16),
            jax.ShapeDtypeStruct((total // 2, width), bf16),
            jax.ShapeDtypeStruct((total // 128, 128), i32),
        ],
        scratch_shapes=[
            pltpu.SMEM((total // 128, 128), i32),
            pltpu.VMEM((total // 128, 128), i32),
            pltpu.VMEM((total // 128, 128), i32),
            pltpu.VMEM(centers.shape, bf16),
            pltpu.VMEM((16, width), f32),
            pltpu.VMEM((total, width), f32),
            pltpu.SemaphoreType.DMA((4,)),
        ],
        compiler_params=pltpu.CompilerParams(vmem_limit_bytes=50 * 2**20),
        cost_estimate=pl.CostEstimate(flops=0, bytes_accessed=14 * 2**20, transcendentals=0),
    )(index.reshape(total // 128, 128), centers)


def prepare_kernel(subset, eigvec, high, low, wide):
    step = pl.program_id(0)
    vectors, count = eigvec.shape
    block = high.shape[0]

    @pl.when(step == 0)
    def _():
        offset = lax.axis_index("centers") * wide.shape[0]
        wide[...] = jnp.zeros_like(wide)

        def put(group, _):
            start = pl.multiple_of(group * 128, 128)
            turned = eigvec[:, pl.ds(start, 128)].T
            for eight in range(0, 128, 8):
                spots = [subset[start + eight + one] - offset for one in range(8)]
                for one in range(8):
                    wide[pl.ds(spots[one], 1), 0:vectors] = turned[eight + one : eight + one + 1, :]
            return 0

        lax.fori_loop(0, count // 128, put, 0)

    span = pl.ds(pl.multiple_of(step * block, block), block)
    high[...], low[...] = split_two(wide[span, 0:vectors])


def prepare(subset, eigvec, centers):
    vectors, count = eigvec.shape
    block = 2048
    lanes = -(-vectors // 128) * 128
    part = pl.BlockSpec((block, vectors), lambda i: (i, 0))
    return pl.pallas_call(
        prepare_kernel,
        name="prepare",
        grid=(centers // block,),
        in_specs=[
            pl.BlockSpec(memory_space=pltpu.SMEM),
            pl.BlockSpec((vectors, count), lambda i: (0, 0)),
        ],
        out_specs=[part, part],
        out_shape=[jax.ShapeDtypeStruct((centers, vectors), bf16)] * 2,
        scratch_shapes=[pltpu.VMEM((centers, lanes), f32)],
        compiler_params=pltpu.CompilerParams(vmem_limit_bytes=20 * 2**20),
        cost_estimate=pl.CostEstimate(flops=0, bytes_accessed=24 * 2**20, transcendentals=0),
    )(subset, eigvec)


def note_kernel(index_s, nxt, targets, hits, labels, all_targets, wide, sem):
    total = index_s.shape[0]
    count = targets.shape[0]
    position = lax.axis_index("centers")
    offset = position * count
    turn = (position & 1) * (total // 2)
    load = pltpu.make_async_copy(targets, all_targets, sem)
    load.start()
    labels[...] = jnp.zeros_like(labels)
    load.wait()

    def note(state):
        number, pos = state
        after = following(nxt, pos, total)
        local = index_s[pos] - offset
        hits[number] = pos * count + local
        tile = pl.ds(pl.multiple_of((local >> 4) << 4, 16), 16)
        wide[...] = all_targets[tile, :].astype(f32)
        labels[pl.ds(pos ^ turn, 1), :] = wide[pl.ds(local & 15, 1), :]
        return number + 1, after

    number, _ = lax.while_loop(lambda s: s[1] < total, note, (jnp.int32(1), nxt[0, 0]))
    hits[0] = number - 1


def note(index, nxt, targets):
    total, channels = index.shape[0], targets.shape[1]
    smem = pl.BlockSpec(memory_space=pltpu.SMEM)
    return pl.pallas_call(
        note_kernel,
        name="note",
        in_specs=[smem, smem, pl.BlockSpec(memory_space=pl.ANY)],
        out_specs=[smem, pl.BlockSpec(memory_space=pltpu.VMEM)],
        out_shape=[
            jax.ShapeDtypeStruct((total + 128,), i32),
            jax.ShapeDtypeStruct((total, channels), f32),
        ],
        scratch_shapes=[
            pltpu.VMEM(targets.shape, bf16),
            pltpu.VMEM((16, channels), f32),
            pltpu.SemaphoreType.DMA,
        ],
        compiler_params=pltpu.CompilerParams(vmem_limit_bytes=8 * 2**20),
        cost_estimate=pl.CostEstimate(flops=0, bytes_accessed=6 * 2**20, transcendentals=0),
    )(index, nxt, targets)


def main_kernel(
    all_centers, coeffs, vectors_t, rows_mine, rows_other, labels, mine, other,
    turned, norms, total, blocks, sems, *, part,
):
    step = pl.program_id(0)
    block = blocks.shape[1]
    slot = step & 1

    def load(step, slot):
        span = pl.ds(pl.multiple_of(step * block, block), block)
        return pltpu.make_async_copy(all_centers.at[span, :], blocks.at[slot], sems.at[slot])

    @pl.when(step == 0)
    def _():
        load(step, slot).start()

    @pl.when(step + 1 < pl.num_programs(0))
    def _():
        load(step + 1, 1 - slot).start()

    half = rows_mine.shape[0]
    channels = labels.shape[1]
    vectors = vectors_t.shape[1]

    @pl.when(step == 0)
    def _():
        ones = jnp.ones((8, rows_mine.shape[1]), bf16)
        for start, rows in ((0, rows_mine), (half, rows_other)):
            span = slice(start, start + half)
            values = rows[...]
            high, low = split_two(jnp.square(values.astype(f32)))
            norms[:, span] = (
                lax.dot_general(ones, high, NT, preferred_element_type=f32)
                + lax.dot_general(ones, low, NT, preferred_element_type=f32)
                + 0.001
            )
            turned[:, span] = (values * jnp.asarray(-2.0, bf16)).T
        total[...] = jnp.zeros_like(total)

    load(step, slot).wait()
    centers = blocks.at[slot]
    spots = list(range(0, block, part))

    def products(start):
        block = centers[start : start + part, :]
        own = jnp.sum(jnp.square(block.astype(f32)), axis=1, keepdims=True)
        return own, jnp.dot(block, turned[...], preferred_element_type=f32)

    def add(start, kernel):
        span = slice(start, start + part)
        columns = jnp.concatenate([coeffs[span, :].astype(bf16), vectors_t[span, :]], axis=1)
        total[...] += lax.dot_general(columns, kernel, TN, preferred_element_type=f32)

    ahead = products(spots[0])
    for number, start in enumerate(spots):
        own, prods = ahead
        if number + 1 < len(spots):
            ahead = products(spots[number + 1])
        distance = jnp.maximum(prods + (own + norms[0:1, :]), 0.001)
        kernel = jnp.exp2(distance * lax.rsqrt(distance) * (-LOG2_E / spread)).astype(bf16)
        if number > 0:
            add(*late)
        late = (start, kernel)
    add(*late)

    @pl.when(step == pl.num_programs(0) - 1)
    def _():
        for start, out in ((0, mine), (half, other)):
            span = slice(start, start + half)
            partial = total[0:channels, span].T - labels[span, :]
            high, low = split_two(partial)
            out[:, 0:channels] = high
            out[:, channels : 2 * channels] = low
            out[:, 2 * channels :] = jnp.zeros((half, out.shape[1] - 2 * channels), bf16)
            out[:, 2 * channels : 2 * channels + vectors] = total[channels:, span].T.astype(bf16)


def main(centers, coeffs, vectors_t, rows_mine, rows_other, labels):
    count, width = centers.shape
    half, channels = rows_mine.shape[0], labels.shape[1]
    columns = channels + vectors_t.shape[1]
    block, part = 2048, 512
    whole = lambda shape: pl.BlockSpec(shape, lambda i: (0, 0))
    return pl.pallas_call(
        functools.partial(main_kernel, part=part),
        name="kernel_sums",
        grid=(count // block,),
        in_specs=[
            pl.BlockSpec(memory_space=pltpu.HBM),
            pl.BlockSpec((block, channels), lambda i: (i, 0)),
            pl.BlockSpec((block, vectors_t.shape[1]), lambda i: (i, 0)),
            whole((half, width)),
            whole((half, width)),
            whole((2 * half, channels)),
        ],
        out_specs=[whole((half, 512)), whole((half, 512))],
        out_shape=[jax.ShapeDtypeStruct((half, 512), bf16)] * 2,
        scratch_shapes=[
            pltpu.VMEM((width, 2 * half), bf16),
            pltpu.VMEM((8, 2 * half), f32),
            pltpu.VMEM((columns, 2 * half), f32),
            pltpu.VMEM((2, block, width), bf16),
            pltpu.SemaphoreType.DMA((2,)),
        ],
        compiler_params=pltpu.CompilerParams(vmem_limit_bytes=38 * 2**20),
        cost_estimate=pl.CostEstimate(
            flops=2 * count * 2 * half * (width + columns),
            bytes_accessed=20 * 2**20,
            transcendentals=2 * count * 2 * half,
        ),
    )(centers, coeffs, vectors_t, rows_mine, rows_other, labels)


def finish_kernel(scale, high, low, coeffs, *refs, members):
    mine, other, refs = refs[:members], refs[members : 2 * members], refs[2 * members :]
    updated, residual, all_rows, weights, codes_v, codes, sem = refs
    step = pl.program_id(0)
    channels = coeffs.shape[1]
    half = residual.shape[0] // 2
    vectors = scale.shape[1]
    block = coeffs.shape[0]
    count = updated.shape[0]
    listed = half + vectors
    lines = codes.shape[0] // members
    copy = pltpu.make_async_copy(codes_v, codes, sem)

    @pl.when(step == 0)
    def _():
        core = lax.axis_index("centers") & 1
        first = (
            lax.broadcasted_iota(i32, (lines, 128), 0) + lax.broadcasted_iota(i32, (lines, 128), 1) == 0
        )
        for member in range(members):
            digits = [
                mine[member][listed + k * lines : listed + (k + 1) * lines, :].astype(f32)
                for k in range(3)
            ]
            code = (digits[0] + 256.0 * digits[1] + 65536.0 * digits[2]).astype(i32)
            local = code & (count - 1)
            pos = code >> (count.bit_length() - 1)
            side = (pos >> (half.bit_length() - 1)) ^ core
            source = (side * members + member) * half + (pos & (half - 1))
            codes_v[member * lines : (member + 1) * lines, :] = jnp.where(
                first, code, (source << 16) + local
            )
        copy.start()
        projected = jnp.zeros((vectors, channels), f32)
        for side, part in enumerate((mine, other)):
            for member in range(members):
                start = (side * members + member) * half
                all_rows[start : start + half, :] = part[member][0:half, :].astype(f32) * -step_size
                projected += part[member][half : half + vectors, :].astype(f32)
        scales = jnp.broadcast_to(scale[...], (channels, vectors)).T
        top, rest = split_two(projected * scales * step_size)
        weights[:, 0:channels] = top
        weights[:, channels:] = rest
        for side, part in enumerate((mine, other)):
            start = pl.multiple_of((core ^ side) * half, half)
            residual[pl.ds(start, half), :] = part[0][0:half, :].astype(f32)

    correction = jnp.dot(high[...], weights[...], preferred_element_type=f32)
    correction_low = jnp.dot(low[...], weights[:, 0:channels], preferred_element_type=f32)
    span = pl.ds(pl.multiple_of(step * block, block), block)
    updated[span, :] = coeffs[...] + (
        correction[:, 0:channels] + (correction[:, channels:] + correction_low)
    )

    @pl.when(step == pl.num_programs(0) - 1)
    def _():
        copy.wait()
        for member in range(members):
            base = member * lines

            def add(numbers):
                found = [codes[base + (k >> 7), k & 127] for k in numbers]
                changes = [all_rows[pl.ds(code >> 16, 1), :] for code in found]
                for code, change in zip(found, changes):
                    local = pl.ds(code & 65535, 1)
                    updated[local, :] = updated[local, :] + change

            def eight(group, _):
                add([group * 8 + one for one in range(1, 9)])
                return 0

            def single(k, _):
                add([k])
                return 0

            number = codes[base, 0]
            eights = number >> 3
            lax.fori_loop(0, eights, eight, 0)
            lax.fori_loop(eights * 8 + 1, number + 1, single, 0)


def finish(scale, high, low, coeffs, mine, other):
    count, channels = coeffs.shape
    vectors = scale.shape[0]
    members = len(mine)
    lines = LINES
    half = mine[0].shape[0] - vectors - 3 * lines
    block = 4096
    whole = lambda shape: pl.BlockSpec(shape, lambda i: (0,) * len(shape))
    return pl.pallas_call(
        functools.partial(finish_kernel, members=members),
        name="finish",
        grid=(count // block,),
        in_specs=[
            whole((1, vectors)),
            pl.BlockSpec((block, vectors), lambda i: (i, 0)),
            pl.BlockSpec((block, vectors), lambda i: (i, 0)),
            pl.BlockSpec((block, channels), lambda i: (i, 0)),
        ]
        + [whole(one.shape) for one in (*mine, *other)],
        out_specs=[whole((count, channels)), whole((2 * half, channels))],
        out_shape=[
            jax.ShapeDtypeStruct((count, channels), f32),
            jax.ShapeDtypeStruct((2 * half, channels), f32),
        ],
        scratch_shapes=[
            pltpu.VMEM((2 * members * half, channels), f32),
            pltpu.VMEM((vectors, 2 * channels), bf16),
            pltpu.VMEM((members * lines, 128), i32),
            pltpu.SMEM((members * lines, 128), i32),
            pltpu.SemaphoreType.DMA,
        ],
        compiler_params=pltpu.CompilerParams(vmem_limit_bytes=32 * 2**20),
        cost_estimate=pl.CostEstimate(flops=10**9, bytes_accessed=14 * 2**20, transcendentals=0),
    )(scale.reshape(1, vectors), high, low, coeffs, *mine, *other)


def body(centers, coeffs, targets, batch_index, subset_index, eigvec, eigen_scale, *, groups):
    count = centers.shape[0]
    channels = coeffs.shape[1]
    vectors = eigvec.shape[0]
    members = lax.axis_size("batch")
    half = batch_index.shape[0] // 2
    chips = len(groups[0])
    sides = (chips // 4, 4)
    swap = [(i, i ^ 1) for i in range(2 * chips)]

    def across(values):
        return lax.all_to_all(
            values, "centers", 0, 0, tiled=True, axis_index_groups=groups
        )

    def turned(blocks, axis):
        total = blocks[0]
        for k in sorted(range(1, len(blocks)), key=lambda k: -min(k, len(blocks) - k)):
            pairs = []
            for chip in range(chips):
                place = [chip // sides[1], chip % sides[1]]
                place[axis] = (place[axis] + k) % sides[axis]
                target = place[0] * sides[1] + place[1]
                pairs += [(2 * chip + core, 2 * target + core) for core in range(2)]
            total = total + lax.ppermute(blocks[k], "centers", pairs)
        return total

    def cut(values, parts):
        size = values.shape[0] // parts
        return [values[k * size : (k + 1) * size] for k in range(parts)]

    mine, other, nxt = pick(batch_index, centers, sides)
    summed = mine + lax.ppermute(other, "centers", swap)
    summed, eigvec = lax.optimization_barrier((summed, eigvec))
    vectors_t, vectors_low = prepare(subset_index, eigvec, count)
    row_sums = turned(cut(summed, sides[0]), 0)
    row_sums, vectors_t, vectors_low = lax.optimization_barrier((row_sums, vectors_t, vectors_low))
    shard = turned(cut(row_sums, sides[1]), 1)
    rows_mine = across(jnp.tile(shard, (chips, 1)))
    rows_other = lax.ppermute(rows_mine, "centers", swap)

    hits, labels = note(batch_index, nxt, targets)
    sums_mine, sums_other = main(centers, coeffs, vectors_t, rows_mine, rows_other, labels)

    def widened(values):
        values = values.astype(f32)
        return values[..., 0:channels] + values[..., channels : 2 * channels], values[..., 2 * channels :]

    def packed(residual, rest):
        high, low = split_rounded(residual)
        return jnp.concatenate([high, low, rest.astype(bf16)], axis=-1)

    first = widened(sums_mine)
    second = widened(lax.ppermute(sums_other, "centers", swap))
    chip_sums = packed(first[0] + second[0], first[1] + second[1])
    parts = widened(across(chip_sums).reshape(chips, half // chips, -1))
    shard = jnp.concatenate(
        [total_of(parts[0]).astype(bf16), total_of(parts[1]).astype(bf16)], axis=1
    )
    gathered = across(jnp.tile(shard, (chips, 1)))
    high = gathered[:, 0:channels]
    projected = lax.dot_general(
        gathered[:, channels : channels + vectors], high, TN, preferred_element_type=f32
    )
    lines = jnp.zeros((LINES * 128,), i32).at[0 : hits.shape[0]].set(hits).reshape(LINES, 128)
    digits = [((lines >> (8 * k)) & 255).astype(bf16) for k in range(3)]
    message = jnp.concatenate([high, projected.astype(bf16), *digits], axis=0)
    steps = sorted(range(1, members), key=lambda k: min(k, members - k))
    from_batch = [message] + [
        lax.ppermute(message, "batch", [(i, (i + k) % members) for i in range(members)])
        for k in steps
    ]
    from_other = [lax.ppermute(one, "centers", swap) for one in from_batch]
    return finish(eigen_scale, vectors_t, vectors_low, coeffs, from_batch, from_other)


def solution(mesh):
    chips = mesh.shape["centers"] // 2
    groups = [[2 * chip + core for chip in range(chips)] for core in range(2)]
    return jax.shard_map(
        functools.partial(body, groups=groups),
        mesh=mesh,
        in_specs=(
            P("centers", None),
            P("centers", None),
            P("centers", None),
            P("batch"),
            P("centers"),
            P(None, "centers"),
            P(),
        ),
        out_specs=(P("centers", None), P("batch", None)),
        check_vma=False,
    )
```

```python
import functools

import jax
import jax.numpy as jnp
from jax import lax
from jax.experimental import pallas as pl
from jax.experimental.pallas import tpu as pltpu
from jax.sharding import PartitionSpec as P

spread = 1.0
step_size = 0.5
NT = (((1,), (1,)), ((), ()))
TN = (((0,), (0,)), ((), ()))
bf16 = jnp.bfloat16
f32 = jnp.float32
i32 = jnp.int32
LINES = 9
LISTED = 32
LOG2_E = 1.4426950408889634


def split_two(values):
    high = values.astype(bf16)
    return high, (values - high.astype(f32)).astype(bf16)


def split_rounded(values):
    high = lax.reduce_precision(values, 8, 7)
    return high.astype(bf16), (values - high).astype(bf16)


def total_of(parts):
    return functools.reduce(jnp.add, [parts[k] for k in range(parts.shape[0])])


def next_hits(index, offset, count):
    rows = index.shape[0]
    total = rows * 128
    lane = lax.broadcasted_iota(i32, (rows, 128), 1)
    sub = lax.broadcasted_iota(i32, (rows, 128), 0)
    local = index - offset
    found = jnp.where((local >= 0) & (local < count), sub * 128 + lane, total)
    shift = 1
    while shift < 128:
        moved = pltpu.roll(found, 128 - shift, 1)
        found = jnp.minimum(found, jnp.where(lane < 128 - shift, moved, total))
        shift *= 2
    later = jnp.broadcast_to(found[:, 0:1], (rows, 128))
    later = jnp.where(sub < rows - 1, pltpu.roll(later, rows - 1, 0), total)
    shift = 1
    while shift < rows:
        moved = pltpu.roll(later, rows - shift, 0)
        later = jnp.minimum(later, jnp.where(sub < rows - shift, moved, total))
        shift *= 2
    return jnp.minimum(found, later)


def following(nxt, pos, total):
    after = jnp.minimum(pos + 1, total - 1)
    return jnp.where(pos + 1 < total, nxt[after >> 7, after & 127], total)


def pick_kernel(
    index, centers, mine, other, nxt, index_s, index_v, nxt_v, all_centers, wide, rows, sems, *, sides
):
    total = rows.shape[0]
    half = total // 2
    shard = half // (sides[0] * sides[1])
    count = centers.shape[0]
    position = lax.axis_index("centers")
    offset = position * count
    core = position & 1
    first, second = (position >> 1) // sides[1], (position >> 1) & (sides[1] - 1)
    to_vector = pltpu.make_async_copy(index, index_v, sems.at[2])
    to_vector.start()
    to_scalar = pltpu.make_async_copy(index, index_s, sems.at[3])
    to_scalar.start()
    load = pltpu.make_async_copy(centers, all_centers, sems.at[0])
    load.start()
    rows[...] = jnp.zeros_like(rows)
    to_vector.wait()
    nxt_v[...] = next_hits(index_v[...], offset, count)
    copy = pltpu.make_async_copy(nxt_v, nxt, sems.at[1])
    copy.start()
    to_scalar.wait()
    copy.wait()
    load.wait()

    shard_bits = shard.bit_length() - 1
    second_bits = sides[1].bit_length() - 1
    half_bits = half.bit_length() - 1

    def take(pos):
        after = following(nxt, pos, total)
        local = index_s[pos >> 7, pos & 127] - offset
        tile = pl.ds(pl.multiple_of((local >> 4) << 4, 16), 16)
        chip = (pos >> shard_bits) & (sides[0] * sides[1] - 1)
        along = ((chip >> second_bits) - first) & (sides[0] - 1)
        across = ((chip & (sides[1] - 1)) - second) & (sides[1] - 1)
        place = (((along << second_bits) | across) << shard_bits) | (pos & (shard - 1))
        spot = (((pos >> half_bits) ^ core) << half_bits) | place
        wide[...] = all_centers[tile, :].astype(f32)
        rows[pl.ds(spot, 1), :] = wide[pl.ds(local & 15, 1), :]
        return after

    lax.while_loop(lambda pos: pos < total, take, nxt[0, 0])
    mine[...] = rows[0:half, :].astype(bf16)
    other[...] = rows[half:total, :].astype(bf16)


def pick(index, centers, sides):
    total = index.shape[0]
    width = centers.shape[1]
    vmem = pl.BlockSpec(memory_space=pltpu.VMEM)
    smem = pl.BlockSpec(memory_space=pltpu.SMEM)
    hbm = pl.BlockSpec(memory_space=pltpu.HBM)
    return pl.pallas_call(
        functools.partial(pick_kernel, sides=sides),
        name="pick",
        in_specs=[hbm, hbm],
        out_specs=[vmem, vmem, smem],
        out_shape=[
            jax.ShapeDtypeStruct((total // 2, width), bf16),
            jax.ShapeDtypeStruct((total // 2, width), bf16),
            jax.ShapeDtypeStruct((total // 128, 128), i32),
        ],
        scratch_shapes=[
            pltpu.SMEM((total // 128, 128), i32),
            pltpu.VMEM((total // 128, 128), i32),
            pltpu.VMEM((total // 128, 128), i32),
            pltpu.VMEM(centers.shape, bf16),
            pltpu.VMEM((16, width), f32),
            pltpu.VMEM((total, width), f32),
            pltpu.SemaphoreType.DMA((4,)),
        ],
        compiler_params=pltpu.CompilerParams(vmem_limit_bytes=50 * 2**20),
        cost_estimate=pl.CostEstimate(flops=0, bytes_accessed=14 * 2**20, transcendentals=0),
    )(index.reshape(total // 128, 128), centers)


def prepare_kernel(subset, eigvec, high, low, wide):
    step = pl.program_id(0)
    vectors, count = eigvec.shape
    block = high.shape[0]

    @pl.when(step == 0)
    def _():
        offset = lax.axis_index("centers") * wide.shape[0]
        wide[...] = jnp.zeros_like(wide)

        def put(group, _):
            start = pl.multiple_of(group * 128, 128)
            turned = eigvec[:, pl.ds(start, 128)].T
            for eight in range(0, 128, 8):
                spots = [subset[start + eight + one] - offset for one in range(8)]
                for one in range(8):
                    wide[pl.ds(spots[one], 1), 0:vectors] = turned[eight + one : eight + one + 1, :]
            return 0

        lax.fori_loop(0, count // 128, put, 0)

    span = pl.ds(pl.multiple_of(step * block, block), block)
    high[...], low[...] = split_two(wide[span, 0:vectors])


def prepare(subset, eigvec, centers):
    vectors, count = eigvec.shape
    block = 2048
    lanes = -(-vectors // 128) * 128
    part = pl.BlockSpec((block, vectors), lambda i: (i, 0))
    return pl.pallas_call(
        prepare_kernel,
        name="prepare",
        grid=(centers // block,),
        in_specs=[
            pl.BlockSpec(memory_space=pltpu.SMEM),
            pl.BlockSpec((vectors, count), lambda i: (0, 0)),
        ],
        out_specs=[part, part],
        out_shape=[jax.ShapeDtypeStruct((centers, vectors), bf16)] * 2,
        scratch_shapes=[pltpu.VMEM((centers, lanes), f32)],
        compiler_params=pltpu.CompilerParams(vmem_limit_bytes=20 * 2**20),
        cost_estimate=pl.CostEstimate(flops=0, bytes_accessed=24 * 2**20, transcendentals=0),
    )(subset, eigvec)


def note_kernel(index_s, nxt, targets, hits, labels, all_targets, wide, sem):
    total = index_s.shape[0]
    count = targets.shape[0]
    position = lax.axis_index("centers")
    offset = position * count
    turn = (position & 1) * (total // 2)
    load = pltpu.make_async_copy(targets, all_targets, sem)
    load.start()
    labels[...] = jnp.zeros_like(labels)
    load.wait()

    def note(state):
        number, pos = state
        after = following(nxt, pos, total)
        local = index_s[pos] - offset
        hits[number] = pos * count + local
        tile = pl.ds(pl.multiple_of((local >> 4) << 4, 16), 16)
        wide[...] = all_targets[tile, :].astype(f32)
        labels[pl.ds(pos ^ turn, 1), :] = wide[pl.ds(local & 15, 1), :]
        return number + 1, after

    number, _ = lax.while_loop(lambda s: s[1] < total, note, (jnp.int32(1), nxt[0, 0]))
    hits[0] = number - 1


def note(index, nxt, targets):
    total, channels = index.shape[0], targets.shape[1]
    smem = pl.BlockSpec(memory_space=pltpu.SMEM)
    return pl.pallas_call(
        note_kernel,
        name="note",
        in_specs=[smem, smem, pl.BlockSpec(memory_space=pl.ANY)],
        out_specs=[smem, pl.BlockSpec(memory_space=pltpu.VMEM)],
        out_shape=[
            jax.ShapeDtypeStruct((total + 128,), i32),
            jax.ShapeDtypeStruct((total, channels), f32),
        ],
        scratch_shapes=[
            pltpu.VMEM(targets.shape, bf16),
            pltpu.VMEM((16, channels), f32),
            pltpu.SemaphoreType.DMA,
        ],
        compiler_params=pltpu.CompilerParams(vmem_limit_bytes=8 * 2**20),
        cost_estimate=pl.CostEstimate(flops=0, bytes_accessed=6 * 2**20, transcendentals=0),
    )(index, nxt, targets)


def main_kernel(
    all_centers, coeffs, vectors_t, rows_mine, rows_other, labels, mine, other,
    turned, norms, total, blocks, sems, *, part,
):
    step = pl.program_id(0)
    block = blocks.shape[1]
    slot = step & 1

    def load(step, slot):
        span = pl.ds(pl.multiple_of(step * block, block), block)
        return pltpu.make_async_copy(all_centers.at[span, :], blocks.at[slot], sems.at[slot])

    @pl.when(step == 0)
    def _():
        load(step, slot).start()

    @pl.when(step + 1 < pl.num_programs(0))
    def _():
        load(step + 1, 1 - slot).start()

    half = rows_mine.shape[0]
    channels = labels.shape[1]
    vectors = vectors_t.shape[1]

    @pl.when(step == 0)
    def _():
        ones = jnp.ones((8, rows_mine.shape[1]), bf16)
        for start, rows in ((0, rows_mine), (half, rows_other)):
            span = slice(start, start + half)
            values = rows[...]
            high, low = split_two(jnp.square(values.astype(f32)))
            norms[:, span] = (
                lax.dot_general(ones, high, NT, preferred_element_type=f32)
                + lax.dot_general(ones, low, NT, preferred_element_type=f32)
                + 0.001
            )
            turned[:, span] = (values * jnp.asarray(-2.0, bf16)).T
        total[...] = jnp.zeros_like(total)

    load(step, slot).wait()
    centers = blocks.at[slot]
    spots = list(range(0, block, part))

    def products(start):
        block = centers[start : start + part, :]
        own = jnp.sum(jnp.square(block.astype(f32)), axis=1, keepdims=True)
        return own, jnp.dot(block, turned[...], preferred_element_type=f32)

    def add(start, kernel):
        span = slice(start, start + part)
        columns = jnp.concatenate([coeffs[span, :].astype(bf16), vectors_t[span, :]], axis=1)
        total[...] += lax.dot_general(columns, kernel, TN, preferred_element_type=f32)

    ahead = products(spots[0])
    for number, start in enumerate(spots):
        own, prods = ahead
        if number + 1 < len(spots):
            ahead = products(spots[number + 1])
        distance = jnp.maximum(prods + (own + norms[0:1, :]), 0.001)
        kernel = jnp.exp2(distance * lax.rsqrt(distance) * (-LOG2_E / spread)).astype(bf16)
        if number > 0:
            add(*late)
        late = (start, kernel)
    add(*late)

    @pl.when(step == pl.num_programs(0) - 1)
    def _():
        for start, out in ((0, mine), (half, other)):
            span = slice(start, start + half)
            partial = total[0:channels, span].T - labels[span, :]
            high, low = split_two(partial)
            out[:, 0:channels] = high
            out[:, channels : 2 * channels] = low
            out[:, 2 * channels :] = jnp.zeros((half, out.shape[1] - 2 * channels), bf16)
            out[:, 2 * channels : 2 * channels + vectors] = total[channels:, span].T.astype(bf16)


def main(centers, coeffs, vectors_t, rows_mine, rows_other, labels):
    count, width = centers.shape
    half, channels = rows_mine.shape[0], labels.shape[1]
    columns = channels + vectors_t.shape[1]
    block, part = 2048, 512
    whole = lambda shape: pl.BlockSpec(shape, lambda i: (0, 0))
    return pl.pallas_call(
        functools.partial(main_kernel, part=part),
        name="kernel_sums",
        grid=(count // block,),
        in_specs=[
            pl.BlockSpec(memory_space=pltpu.HBM),
            pl.BlockSpec((block, channels), lambda i: (i, 0)),
            pl.BlockSpec((block, vectors_t.shape[1]), lambda i: (i, 0)),
            whole((half, width)),
            whole((half, width)),
            whole((2 * half, channels)),
        ],
        out_specs=[whole((half, 512)), whole((half, 512))],
        out_shape=[jax.ShapeDtypeStruct((half, 512), bf16)] * 2,
        scratch_shapes=[
            pltpu.VMEM((width, 2 * half), bf16),
            pltpu.VMEM((8, 2 * half), f32),
            pltpu.VMEM((columns, 2 * half), f32),
            pltpu.VMEM((2, block, width), bf16),
            pltpu.SemaphoreType.DMA((2,)),
        ],
        compiler_params=pltpu.CompilerParams(vmem_limit_bytes=38 * 2**20),
        cost_estimate=pl.CostEstimate(
            flops=2 * count * 2 * half * (width + columns),
            bytes_accessed=20 * 2**20,
            transcendentals=2 * count * 2 * half,
        ),
    )(centers, coeffs, vectors_t, rows_mine, rows_other, labels)


def finish_kernel(scale, high, low, coeffs, *refs, members):
    mine, other, refs = refs[:members], refs[members : 2 * members], refs[2 * members :]
    updated, residual, all_rows, weights, codes_v, codes, sem = refs
    step = pl.program_id(0)
    channels = coeffs.shape[1]
    half = residual.shape[0] // 2
    vectors = scale.shape[1]
    block = coeffs.shape[0]
    count = updated.shape[0]
    listed = half + vectors
    lines = LINES
    copy = pltpu.make_async_copy(codes_v, codes, sem)

    @pl.when(step == 0)
    def _():
        core = lax.axis_index("centers") & 1
        first = (
            lax.broadcasted_iota(i32, (lines, 128), 0) + lax.broadcasted_iota(i32, (lines, 128), 1) == 0
        )
        for member in range(members):
            listing = mine[member][listed : listed + LISTED, :].astype(f32)
            digits = [listing[k * lines : (k + 1) * lines, :] for k in range(3)]
            code = (digits[0] + 256.0 * digits[1] + 65536.0 * digits[2]).astype(i32)
            local = code & (count - 1)
            pos = code >> (count.bit_length() - 1)
            side = (pos >> (half.bit_length() - 1)) ^ core
            source = (side * members + member) * half + (pos & (half - 1))
            codes_v[member * 16 : member * 16 + lines, :] = jnp.where(
                first, code, (source << 16) + local
            )
        copy.start()
        projected = jnp.zeros((vectors, channels), f32)
        for side, part in enumerate((mine, other)):
            for member in range(members):
                start = (side * members + member) * half
                all_rows[start : start + half, :] = part[member][0:half, :].astype(f32) * -step_size
                projected += part[member][half : half + vectors, :].astype(f32)
        scales = jnp.broadcast_to(scale[...], (channels, vectors)).T
        top, rest = split_two(projected * scales * step_size)
        weights[:, 0:channels] = top
        weights[:, channels:] = rest
        for side, part in enumerate((mine, other)):
            start = pl.multiple_of((core ^ side) * half, half)
            residual[pl.ds(start, half), :] = part[0][0:half, :].astype(f32)

    correction = jnp.dot(high[...], weights[...], preferred_element_type=f32)
    correction_low = jnp.dot(low[...], weights[:, 0:channels], preferred_element_type=f32)
    span = pl.ds(pl.multiple_of(step * block, block), block)
    updated[span, :] = coeffs[...] + (
        correction[:, 0:channels] + (correction[:, channels:] + correction_low)
    )

    @pl.when(step == pl.num_programs(0) - 1)
    def _():
        copy.wait()
        for member in range(members):
            base = member * 16

            def add(numbers):
                found = [codes[base + (k >> 7), k & 127] for k in numbers]
                changes = [all_rows[pl.ds(code >> 16, 1), :] for code in found]
                for code, change in zip(found, changes):
                    local = pl.ds(code & 65535, 1)
                    updated[local, :] = updated[local, :] + change

            def eight(group, _):
                add([group * 8 + one for one in range(1, 9)])
                return 0

            def single(k, _):
                add([k])
                return 0

            number = codes[base, 0]
            eights = number >> 3
            lax.fori_loop(0, eights, eight, 0)
            lax.fori_loop(eights * 8 + 1, number + 1, single, 0)


def finish(scale, high, low, coeffs, mine, other):
    count, channels = coeffs.shape
    vectors = scale.shape[0]
    members = len(mine)
    half = mine[0].shape[0] - vectors - LISTED
    block = 4096
    whole = lambda shape: pl.BlockSpec(shape, lambda i: (0,) * len(shape))
    return pl.pallas_call(
        functools.partial(finish_kernel, members=members),
        name="finish",
        grid=(count // block,),
        in_specs=[
            whole((1, vectors)),
            pl.BlockSpec((block, vectors), lambda i: (i, 0)),
            pl.BlockSpec((block, vectors), lambda i: (i, 0)),
            pl.BlockSpec((block, channels), lambda i: (i, 0)),
        ]
        + [whole(one.shape) for one in (*mine, *other)],
        out_specs=[whole((count, channels)), whole((2 * half, channels))],
        out_shape=[
            jax.ShapeDtypeStruct((count, channels), f32),
            jax.ShapeDtypeStruct((2 * half, channels), f32),
        ],
        scratch_shapes=[
            pltpu.VMEM((2 * members * half, channels), f32),
            pltpu.VMEM((vectors, 2 * channels), bf16),
            pltpu.VMEM((members * 16, 128), i32),
            pltpu.SMEM((members * 16, 128), i32),
            pltpu.SemaphoreType.DMA,
        ],
        compiler_params=pltpu.CompilerParams(vmem_limit_bytes=32 * 2**20),
        cost_estimate=pl.CostEstimate(flops=10**9, bytes_accessed=14 * 2**20, transcendentals=0),
    )(scale.reshape(1, vectors), high, low, coeffs, *mine, *other)


def body(centers, coeffs, targets, batch_index, subset_index, eigvec, eigen_scale, *, groups):
    count = centers.shape[0]
    channels = coeffs.shape[1]
    vectors = eigvec.shape[0]
    members = lax.axis_size("batch")
    half = batch_index.shape[0] // 2
    chips = len(groups[0])
    sides = (chips // 4, 4)
    swap = [(i, i ^ 1) for i in range(2 * chips)]

    def across(values):
        return lax.all_to_all(
            values, "centers", 0, 0, tiled=True, axis_index_groups=groups
        )

    def turned(blocks, axis):
        total = blocks[0]
        for k in range(1, len(blocks)):
            pairs = []
            for chip in range(chips):
                place = [chip // sides[1], chip % sides[1]]
                place[axis] = (place[axis] + k) % sides[axis]
                target = place[0] * sides[1] + place[1]
                pairs += [(2 * chip + core, 2 * target + core) for core in range(2)]
            total = total + lax.ppermute(blocks[k], "centers", pairs)
        return total

    def cut(values, parts):
        size = values.shape[0] // parts
        return [values[k * size : (k + 1) * size] for k in range(parts)]

    mine, other, nxt = pick(batch_index, centers, sides)
    summed = mine + lax.ppermute(other, "centers", swap)
    summed, eigvec = lax.optimization_barrier((summed, eigvec))
    vectors_t, vectors_low = prepare(subset_index, eigvec, count)
    row_sums = turned(cut(summed, sides[0]), 0)
    row_sums, vectors_t, vectors_low = lax.optimization_barrier((row_sums, vectors_t, vectors_low))
    shard = turned(cut(row_sums, sides[1]), 1)
    rows_mine = across(jnp.tile(shard, (chips, 1)))
    rows_other = lax.ppermute(rows_mine, "centers", swap)

    hits, labels = note(batch_index, nxt, targets)
    sums_mine, sums_other = main(centers, coeffs, vectors_t, rows_mine, rows_other, labels)

    def widened(values):
        values = values.astype(f32)
        return values[..., 0:channels] + values[..., channels : 2 * channels], values[..., 2 * channels :]

    def packed(residual, rest):
        high, low = split_rounded(residual)
        return jnp.concatenate([high, low, rest.astype(bf16)], axis=-1)

    first = widened(sums_mine)
    second = widened(lax.ppermute(sums_other, "centers", swap))
    chip_sums = packed(first[0] + second[0], first[1] + second[1])
    parts = widened(across(chip_sums).reshape(chips, half // chips, -1))
    shard = jnp.concatenate(
        [total_of(parts[0]).astype(bf16), total_of(parts[1]).astype(bf16)], axis=1
    )
    gathered = across(jnp.tile(shard, (chips, 1)))
    high = gathered[:, 0:channels]
    projected = lax.dot_general(
        gathered[:, channels : channels + vectors], high, TN, preferred_element_type=f32
    )
    lines = hits.reshape(LINES, 128)
    digits = [((lines >> (8 * k)) & 255).astype(bf16) for k in range(3)]
    digits.append(jnp.zeros((LISTED - 3 * LINES, 128), bf16))
    message = jnp.concatenate([high, projected.astype(bf16), *digits], axis=0)
    steps = sorted(range(1, members), key=lambda k: min(k, members - k))
    from_batch = [message] + [
        lax.ppermute(message, "batch", [(i, (i + k) % members) for i in range(members)])
        for k in steps
    ]
    from_other = [lax.ppermute(one, "centers", swap) for one in from_batch]
    return finish(eigen_scale, vectors_t, vectors_low, coeffs, from_batch, from_other)


def solution(mesh):
    chips = mesh.shape["centers"] // 2
    groups = [[2 * chip + core for chip in range(chips)] for core in range(2)]
    return jax.shard_map(
        functools.partial(body, groups=groups),
        mesh=mesh,
        in_specs=(
            P("centers", None),
            P("centers", None),
            P("centers", None),
            P("batch"),
            P("centers"),
            P(None, "centers"),
            P(),
        ),
        out_specs=(P("centers", None), P("batch", None)),
        check_vma=False,
    )
```
